32 devices in a mesh: grp: 4 (over y, x), dp: 8 (over z, core).
Axes of the slice: x: 2, y: 2, z: 4, core: 2. Of those that a mesh axis runs over, the one named last changes fastest.
Arguments:
- images: float32 [4, 24, 3, 1024], P('grp', 'dp'), may hold values from -6 to 6
- probes: float32 [4, 24, 3, 1024], P('grp', 'dp'), may hold values from -6 to 6
- out_cotangent: float32 [4, 24, 3, 1024], P('grp', 'dp'), may hold values from -3.2 to 4.8
- counts: int32 [4, 8], P('grp', 'dp'), may hold values from 1 to 3, 16 in all within a row
- terms: int32 [4, 24], P('grp', 'dp'), may hold values from 1 to 4, as said below
- power_left: float32 [4, 2, 512], P('grp'), may hold values from -6 to 6
- power_out: float32 [4, 3], P('grp'), may hold values from -6 to 6
- mid_weight: float32 [4, 512, 512], P('grp', None, 'dp')
- mid_first: float32 [4, 512, 512], P('grp', None, 'dp'), may hold values from -1.25 to 1.25
- mid_second: float32 [4, 512, 512], P('grp', None, 'dp'), may hold values from 0.0005138022 to 0.002055209
- side_weight: float32 [4, 58, 512], P('grp', None, 'dp')
- side_first: float32 [4, 58, 512], P('grp', None, 'dp')
- side_second: float32 [4, 58, 512], P('grp', None, 'dp')
- tiny_weight: float32 [4, 4, 3], P('grp')
- tiny_first: float32 [4, 4, 3], P('grp')
- tiny_second: float32 [4, 4, 3], P('grp')
- mid_outer: float32 [512, 512], P(None, 'dp')
- mid_momentum: float32 [512, 512], P(None, 'dp'), may hold values from -0.3125 to 0.3125
- side_outer: float32 [58, 512], P(None, 'dp')
- side_momentum: float32 [58, 512], P(None, 'dp'), may hold values from -0.3125 to 0.3125
- tiny_outer: float32 [4, 3], replicated
- tiny_momentum: float32 [4, 3], replicated, may hold values from -0.75 to 0.75
Outputs:
- flow_out: float32 [4, 24, 3, 1024], P('grp', 'dp')
- input_gradient: float32 [4, 24, 3, 1024], P('grp', 'dp')
- log_det: float32 [4, 24], P('grp', 'dp')
- log_det_mean: float32 [4], P('grp')
- mid_first_new: float32 [4, 512, 512], P('grp', None, 'dp')
- mid_second_new: float32 [4, 512, 512], P('grp', None, 'dp')
- mid_new: float32 [4, 512, 512], P('grp', None, 'dp')
- side_first_new: float32 [4, 58, 512], P('grp', None, 'dp')
- side_second_new: float32 [4, 58, 512], P('grp', None, 'dp')
- side_new: float32 [4, 58, 512], P('grp', None, 'dp')
- tiny_first_new: float32 [4, 4, 3], P('grp')
- tiny_second_new: float32 [4, 3, 3], P('grp')
- slope_second_new: float32 [4, 3], P('grp')
- tiny_new: float32 [4, 4, 3], P('grp')
- mid_delta: float32 [512, 512], P(None, 'dp')
- mid_momentum_new: float32 [512, 512], P(None, 'dp')
- mid_outer_new: float32 [512, 512], P(None, 'dp')
- side_delta: float32 [58, 512], P(None, 'dp')
- side_momentum_new: float32 [58, 512], P(None, 'dp')
- side_outer_new: float32 [58, 512], P(None, 'dp')
- tiny_delta: float32 [4, 3], replicated
- tiny_momentum_new: float32 [4, 3], replicated
- tiny_outer_new: float32 [4, 3], replicated
The draws below stay inside these ranges and needn't reach their ends.
Inputs may be any that keep to these rules, and one draw needn't show every extreme that they name: In each group the devices' counts sum to 16, and some device holds 3. `terms`: in each group some valid image has 4.
All inputs are finite; a program needn't handle non-finite values.
Results may differ from the reference program's by a relative error of at most 0.0003.
Values sent between devices are 32-bit elements; how exact they have to be, the bound alone decides.
A program may use at most 128 MiB of HBM per device.

```python
import math
import jax
import jax.numpy as jnp
import numpy as np
from jax import lax

HIDDEN_SIZE = 512
COLORS = 3
HEIGHT = 32
WIDTH = 32
TERMS = 4
SLOTS = 3
PIXELS = 1024
GROUPS = 4
IMAGE_SLOTS = 24
GROUP_IMAGES = 16
SIDE_ROWS = 58
N_DP = 8


def side_kinds():
    rows = jnp.arange(SIDE_ROWS)[:, None]
    pix = 1.0 * PIXELS
    slopes = (rows == 28) | (rows == 30)
    return jnp.where(rows < 27, 0.004 * pix, jnp.where(rows >= 31, 0.027 * pix, jnp.where(slopes, 0.004 * pix, 0.013 * pix)))


def tiny_kinds():
    rows = jnp.arange(4)[:, None]
    pix = 1.0 * PIXELS
    return jnp.where(rows == 0, 0.8 * pix, jnp.where(rows == 1, 1.6 * pix, jnp.where(rows == 2, pix, 0.1 * pix)))


def normal_clip(key, shape):
    return jnp.clip(jax.random.normal(key, shape, jnp.float32), -6.0, 6.0)


def first_block(key, lead):
    taps = 9 * COLORS
    shape = lead + (taps, HIDDEN_SIZE)
    rows = jnp.arange(taps)[:, None]
    chans = jnp.arange(HIDDEN_SIZE)[None, :]
    strong = jnp.exp(0.5 * jax.random.uniform(key, shape, jnp.float32, -1.0, 1.0))
    noise = normal_clip(jax.random.fold_in(key, 1), shape)
    return jnp.where(chans % taps == rows, strong, 0.0) + 0.1 * noise


def side_values(key, lead):
    taps = 9 * COLORS
    first = first_block(key, lead)
    small_shape = lead + (1, HIDDEN_SIZE)
    bias_one = 0.1 * normal_clip(jax.random.fold_in(key, 2), small_shape)
    slope_one = jax.random.uniform(jax.random.fold_in(key, 3), small_shape, jnp.float32, 2.0, 5.0)
    bias_two = 0.1 * normal_clip(jax.random.fold_in(key, 4), small_shape)
    slope_two = jax.random.uniform(jax.random.fold_in(key, 5), small_shape, jnp.float32, -1.0, 1.0)
    index = jnp.arange(taps)
    partner = index // 9 * 9 + 8 - index % 9
    flipped = jnp.take(first, partner, axis=-2)
    noise = normal_clip(jax.random.fold_in(key, 6), lead + (taps, HIDDEN_SIZE))
    last = 0.5 * (taps / (1.0 * HIDDEN_SIZE)) ** 0.5 * flipped + 1.05 * noise / (9.0 * HIDDEN_SIZE) ** 0.5
    return jnp.concatenate([first, bias_one, slope_one, bias_two, slope_two, last], axis=-2)


def mid_values(key, lead):
    noise = normal_clip(key, lead + (HIDDEN_SIZE, HIDDEN_SIZE))
    ident = (jnp.arange(HIDDEN_SIZE)[:, None] == jnp.arange(HIDDEN_SIZE)[None, :]).astype(jnp.float32)
    return 2.5 * ident + noise / (1.0 * HIDDEN_SIZE) ** 0.5


def tiny_values(key, shape):
    rows = jnp.arange(4)[:, None]
    noise = normal_clip(key, shape)
    flat = jax.random.uniform(jax.random.fold_in(key, 13), shape, jnp.float32, -1.0, 1.0)
    return jnp.where(rows < 2, 0.3 * noise, jnp.where(rows == 2, 0.55 + 0.35 * flat, flat))


def draw_out_cotangent(key, part):
    shape = (GROUPS, IMAGE_SLOTS, COLORS, PIXELS)
    spread = jnp.clip(jax.random.normal(key, shape, jnp.float32), -4.0, 4.0)
    return 0.8 + spread


def draw_terms(key, part):
    base = jax.random.randint(key, (GROUPS, IMAGE_SLOTS), 1, TERMS + 1)
    device = jax.random.randint(jax.random.fold_in(key, 3), (GROUPS, 1), 0, IMAGE_SLOTS // SLOTS)
    spot = device * SLOTS
    return jnp.where(jnp.arange(IMAGE_SLOTS)[None, :] == spot, TERMS, base).astype(jnp.int32)


def draw_mid_weight(key, part):
    return mid_values(key, (GROUPS,))


def draw_mid_outer(key, part):
    return mid_values(jax.random.fold_in(key, 5), ())


def draw_side_weight(key, part):
    return side_values(key, (GROUPS,))


def draw_side_outer(key, part):
    return side_values(jax.random.fold_in(key, 7), ())


def draw_side_first(key, part):
    noise = normal_clip(key, (GROUPS, SIDE_ROWS, HIDDEN_SIZE))
    return 0.111 * side_kinds() * noise


def draw_side_second(key, part):
    spread = jax.random.uniform(key, (GROUPS, SIDE_ROWS, HIDDEN_SIZE), jnp.float32, 0.0, jnp.log(4.0))
    return 0.001 * side_kinds() ** 2 * jnp.exp(spread)


def draw_tiny_weight(key, part):
    return tiny_values(key, (GROUPS, 4, COLORS))


def draw_tiny_outer(key, part):
    return tiny_values(jax.random.fold_in(key, 9), (4, COLORS))


def draw_tiny_first(key, part):
    noise = normal_clip(key, (GROUPS, 4, COLORS))
    return 0.111 * tiny_kinds() * noise


def draw_tiny_second(key, part):
    spread = jax.random.uniform(key, (GROUPS, 4, COLORS), jnp.float32, 0.0, jnp.log(4.0))
    return 0.001 * tiny_kinds() ** 2 * jnp.exp(spread)


def block_scale(key, extent, pieces, smallest, high):
    level, own = 1.0, jax.random.fold_in(key, 6)
    for axis_at, blocks in pieces:
        draws = jnp.exp(jax.random.uniform(jax.random.fold_in(own, axis_at), (blocks,), jnp.float32, smallest / len(pieces), high / len(pieces)))
        level = level * jnp.repeat(draws, extent[axis_at] // blocks).reshape([-1 if axis == axis_at else 1 for axis in range(len(extent))])
    return level


def profile(number_of, total, most, skew):
    portions = [(1 << 20) // math.isqrt(standing ** skew) + 1 for standing in range(2, number_of + 1)]
    surplus, holding = total - most - (number_of - 1), [1] * (number_of - 1)
    while surplus > 0:
        candidates = [i for i in range(number_of - 1) if holding[i] < most]
        mass, budget = sum([portions[i] for i in candidates]), surplus
        for i in candidates:
            more = min(most - holding[i], max(1, budget * portions[i] // mass), surplus)
            holding[i] = holding[i] + more
            surplus = surplus - more
    return np.array([most] + holding)


def uneven_parts(stream_key, count, total, most, lean):
    if count == 2:
        one = jax.random.randint(stream_key, (), max(1, total - most), min(most, total - 1) + 1)
        return jnp.stack([one, total - one])
    lengths = jnp.asarray(profile(count, total, most, lean), jnp.int32)
    twos = (count - 1) // 2
    donor, receiver = lengths[1:1 + 2 * twos:2], lengths[2:2 + 2 * twos:2]
    slack = jnp.minimum(donor - 1, most - receiver)
    shifted = jax.random.randint(jax.random.fold_in(stream_key, 1), (twos,), 0, 1 << 20) % (slack + 1)
    lengths = lengths.at[1:1 + 2 * twos:2].set(donor - shifted).at[2:2 + 2 * twos:2].set(receiver + shifted)
    return lengths[jax.random.permutation(jax.random.fold_in(stream_key, 2), count)]


def normal_values(own_key, dims, width, limit, cuts=(), kind=jnp.bfloat16):
    values = jax.random.normal(own_key, dims, jnp.float32) * width
    if len(cuts) > 0:
        values = block_scale(own_key, dims, cuts, -0.22, 0.18) * values
    return jnp.clip(values, min=-limit, max=limit).astype(kind)


def setup_inputs(seed: int = 0) -> dict:
    streams_of = jax.random.split(jax.random.key(seed), 23)
    images = normal_values(streams_of[0], (GROUPS, IMAGE_SLOTS, COLORS, PIXELS), 1.0, 6.0, ((0, 4), (1, 8)), jnp.float32)
    probes = normal_values(streams_of[1], (GROUPS, IMAGE_SLOTS, COLORS, PIXELS), 1.0, 6.0, ((0, 4), (1, 8)), jnp.float32)
    out_cotangent = draw_out_cotangent(jax.random.fold_in(streams_of[22], 71), 0)
    counts = jax.vmap(lambda own: uneven_parts(own, N_DP, GROUP_IMAGES, SLOTS, 2))(jax.random.split(streams_of[3], GROUPS)).reshape((GROUPS, N_DP)).astype(jnp.int32)
    terms = draw_terms(jax.random.fold_in(streams_of[22], 71), 0)
    power_left = normal_values(streams_of[5], (GROUPS, 2, HIDDEN_SIZE), 1.0, 6.0, ((0, 4),), jnp.float32)
    power_out = normal_values(streams_of[6], (GROUPS, COLORS), 1.0, 6.0, ((0, 4),), jnp.float32)
    mid_weight = draw_mid_weight(jax.random.fold_in(streams_of[22], 71), 0)
    mid_first = normal_values(streams_of[8], (GROUPS, HIDDEN_SIZE, HIDDEN_SIZE), (0.0000777 * PIXELS), 1.25, ((0, 4), (2, 8)), jnp.float32)
    mid_second = jnp.clip(jnp.exp(math.log(0.002055209) - 1.3862944 * jax.random.uniform(streams_of[9], (GROUPS, HIDDEN_SIZE, HIDDEN_SIZE), jnp.float32) ** block_scale(streams_of[9], (GROUPS, HIDDEN_SIZE, HIDDEN_SIZE), ((0, 4), (2, 8)), -0.2, 0.2)), 0.0005138022, 0.002055209)
    side_weight = draw_side_weight(jax.random.fold_in(streams_of[22], 71), 0)
    side_first = draw_side_first(jax.random.fold_in(streams_of[22], 71), 0)
    side_second = draw_side_second(jax.random.fold_in(streams_of[22], 71), 0)
    tiny_weight = draw_tiny_weight(jax.random.fold_in(streams_of[22], 71), 0)
    tiny_first = draw_tiny_first(jax.random.fold_in(streams_of[22], 71), 0)
    tiny_second = draw_tiny_second(jax.random.fold_in(streams_of[22], 71), 0)
    mid_outer = draw_mid_outer(jax.random.fold_in(streams_of[22], 71), 0)
    mid_momentum = normal_values(streams_of[17], (HIDDEN_SIZE, HIDDEN_SIZE), 0.02, 0.3125, ((1, 8),), jnp.float32)
    side_outer = draw_side_outer(jax.random.fold_in(streams_of[22], 71), 0)
    side_momentum = normal_values(streams_of[19], (SIDE_ROWS, HIDDEN_SIZE), 0.02, 0.3125, ((1, 8),), jnp.float32)
    tiny_outer = draw_tiny_outer(jax.random.fold_in(streams_of[22], 71), 0)
    tiny_momentum = normal_values(streams_of[21], (4, COLORS), 0.05, 0.75, (), jnp.float32)
    return dict(images=images, probes=probes, out_cotangent=out_cotangent, counts=counts, terms=terms, power_left=power_left, power_out=power_out, mid_weight=mid_weight, mid_first=mid_first, mid_second=mid_second, side_weight=side_weight, side_first=side_first, side_second=side_second, tiny_weight=tiny_weight, tiny_first=tiny_first, tiny_second=tiny_second, mid_outer=mid_outer, mid_momentum=mid_momentum, side_outer=side_outer, side_momentum=side_momentum, tiny_outer=tiny_outer, tiny_momentum=tiny_momentum)


highest = lax.Precision.HIGHEST
clip_level = 0.98
adam_first = 0.9
adam_second = 0.999
adam_eps = 1e-08
decay_rate = 0.01
step_count = 5.0
outer_rate = 0.7
outer_beta = 0.9

def tap_shift(field, tap):
    channels = field.shape[0]
    grid = field.reshape(channels, HEIGHT, WIDTH)
    padded = jnp.pad(grid, ((0, 0), (1, 1), (1, 1)))
    row_shift = tap // 3
    col_shift = tap % 3
    return padded[:, row_shift:row_shift + HEIGHT, col_shift:col_shift + WIDTH].reshape(channels, HEIGHT * WIDTH)

def lipswish(value, slope_raw):
    slope = jax.nn.softplus(slope_raw)[:, None]
    return value * jax.nn.sigmoid(slope * value) / 1.1

def unit(vector):
    return vector / jnp.sqrt(jnp.sum(vector * vector) + 1e-12)

def matrices(params):
    middle, side, tiny = params
    first = side[0:27].T
    last = side[31:58].reshape(COLORS, 9 * HIDDEN_SIZE)
    return (first, middle, last)

def power_pairs(params, lefts):
    pairs = []
    for matrix, left in zip(matrices(params), lefts):
        right = unit(jnp.dot(matrix.T, left, precision=highest))
        pairs.append((unit(jnp.dot(matrix, right, precision=highest)), right))
    return pairs

def normalized(matrix, pair):
    left, right = pair
    sigma = jnp.dot(left, jnp.dot(matrix, right, precision=highest), precision=highest)
    return matrix / jnp.maximum(1.0, sigma / clip_level)

def branch(params, pairs, field):
    middle, side, tiny = params
    mats = matrices(params)
    first = normalized(mats[0], pairs[0])
    second = normalized(mats[1], pairs[1])
    last = normalized(mats[2], pairs[2])
    act_zero = lipswish(field, tiny[3])
    stacked = jnp.stack([tap_shift(act_zero, tap) for tap in range(9)], 1).reshape(COLORS * 9, -1)
    hidden_one = jnp.dot(first, stacked, precision=highest) + side[27][:, None]
    act_one = lipswish(hidden_one, side[28])
    hidden_two = jnp.dot(second, act_one, precision=highest) + side[29][:, None]
    act_two = lipswish(hidden_two, side[30])
    per_tap = jnp.dot(last.reshape(COLORS * 9, HIDDEN_SIZE), act_two, precision=highest).reshape(COLORS, 9, -1)
    result = tap_shift(per_tap[:, 0], 0)
    for tap in range(1, 9):
        result = result + tap_shift(per_tap[:, tap], tap)
    return result + tiny[0][:, None]

def actnorm(tiny, image):
    return (image + tiny[1][:, None]) * jnp.exp(tiny[2])[:, None]

def image_pass(params, pairs, image, probe, cotangent, count):
    tiny = params[2]
    field = actnorm(tiny, image)
    output, pull = jax.vjp(lambda inner: branch(params, pairs, inner), field)
    vector = probe
    series = jnp.zeros((), jnp.float32)
    neumann = jnp.zeros_like(probe)
    for power in range(TERMS):
        live = (count > power).astype(jnp.float32)
        neumann = neumann + live * (-1.0) ** power * vector
        vector = pull(vector)[0]
        series = series + live * ((-1.0) ** power / (power + 1)) * jnp.sum(vector * probe)
    log_total = HEIGHT * WIDTH * jnp.sum(tiny[2]) + series

    def objective(weights, start):
        inner = actnorm(weights[2], start)
        result, back = jax.vjp(lambda value: branch(weights, pairs, value), inner)
        return jnp.sum(cotangent * (inner + result)) - HEIGHT * WIDTH * jnp.sum(weights[2][2]) - jnp.sum(probe * back(neumann)[0])
    gradients, image_gradient = jax.grad(objective, argnums=(0, 1))(params, image)
    return (field + output, image_gradient, log_total / (COLORS * HEIGHT * WIDTH), gradients)

def run_images(params, pairs, batch, series, keep):
    empty = jax.tree.map(jnp.zeros_like, params)

    def visit(carry, item):
        image, probe, cotangent, count, weight = item
        output, image_gradient, log_part, gradients = image_pass(params, pairs, image, probe, cotangent, count)
        carry = jax.tree.map(lambda running, gradient: running + weight * gradient, carry, gradients)
        return (carry, (weight * output, weight * image_gradient, weight * log_part))
    return lax.scan(visit, empty, (batch[0], batch[1], batch[2], series, keep))

def adam_update(weight, gradient, first, second, rate):
    first = adam_first * first + (1.0 - adam_first) * gradient
    second = adam_second * second + (1.0 - adam_second) * gradient * gradient
    first_hat = first / (1.0 - adam_first ** step_count)
    second_hat = second / (1.0 - adam_second ** step_count)
    return (weight - rate * (first_hat / (jnp.sqrt(second_hat) + adam_eps) + decay_rate * weight), first, second)

def update_all(params, gradients, firsts, seconds):
    rows = jnp.arange(params[1].shape[0])[:, None]
    rates = (0.01, jnp.where(rows >= 31, 0.004, 0.05), 0.05)
    updated = []
    for kind in range(3):
        updated.append(adam_update(params[kind], gradients[kind], firsts[kind], seconds[kind], rates[kind]))
    return updated

def reference(images, probes, out_cotangent, counts, terms, power_left, power_out, mid_weight, mid_first, mid_second, side_weight, side_first, side_second, tiny_weight, tiny_first, tiny_second, mid_outer, mid_momentum, side_outer, side_momentum, tiny_outer, tiny_momentum):
    slot = jnp.arange(IMAGE_SLOTS)
    flows, backs, logs, means, updates = ([], [], [], [], [])
    for group in range(GROUPS):
        params = (mid_weight[group], side_weight[group], tiny_weight[group])
        pairs = power_pairs(params, (power_left[group, 0], power_left[group, 1], power_out[group]))
        keep = (slot % SLOTS < jnp.take(counts[group], slot // SLOTS)).astype(jnp.float32)
        totals, (flow, back, log_part) = run_images(params, pairs, (images[group], probes[group], out_cotangent[group]), terms[group], keep)
        gradients = [running / GROUP_IMAGES for running in totals]
        updates.append(update_all(params, gradients, (mid_first[group], side_first[group], tiny_first[group]), (mid_second[group], side_second[group], tiny_second[group])))
        flows.append(flow)
        backs.append(back)
        logs.append(log_part)
        means.append(jnp.sum(log_part) / GROUP_IMAGES)
    outers = (mid_outer, side_outer, tiny_outer)
    momenta = (mid_momentum, side_momentum, tiny_momentum)
    globals_new = []
    for kind in range(3):
        delta = outers[kind] - updates[0][kind][0]
        for group in range(1, GROUPS):
            delta = delta + (outers[kind] - updates[group][kind][0])
        delta = delta / GROUPS
        momentum_new = outer_beta * momenta[kind] + delta
        globals_new.append((delta, momentum_new, outers[kind] - outer_rate * (delta + outer_beta * momentum_new)))
    stacked = []
    for kind in range(3):
        stacked.append(tuple((jnp.stack([updates[group][kind][member] for group in range(GROUPS)], 0) for member in range(3))))
    return (jnp.stack(flows, 0), jnp.stack(backs, 0), jnp.stack(logs, 0), jnp.stack(means, 0), stacked[0][1], stacked[0][2], stacked[0][0], stacked[1][1], stacked[1][2], stacked[1][0], stacked[2][1], stacked[2][2][:, 0:3], stacked[2][2][:, 3], stacked[2][0], globals_new[0][0], globals_new[0][1], globals_new[0][2], globals_new[1][0], globals_new[1][1], globals_new[1][2], globals_new[2][0], globals_new[2][1], globals_new[2][2])
```

```python
import functools

import jax, jax.numpy as jnp
from jax import lax
from jax.experimental import pallas as pl
from jax.experimental.pallas import tpu as pltpu
from jax.sharding import PartitionSpec as P

bf16, f32 = jnp.bfloat16, jnp.float32
HIGH = lax.Precision.HIGHEST
C, PX, TILE = 512, 1024, 512
CLIP = 0.98
LIP = 2.2


def dot_nn(a, b):
    return jnp.dot(a, b, preferred_element_type=f32)


def dot_tn(a, b):
    return lax.dot_general(a, b, (((0,), (0,)), ((), ())), preferred_element_type=f32)


def dot_nt(a, b):
    return lax.dot_general(a, b, (((1,), (1,)), ((), ())), preferred_element_type=f32)


def tap_masks():
    lane = lax.broadcasted_iota(jnp.int32, (8, PX), 1)
    row, col = lane // 32, lane % 32
    masks = []
    for tap in range(9):
        down, right = tap // 3 - 1, tap % 3 - 1
        ok = (row + down >= 0) & (row + down < 32) & (col + right >= 0) & (col + right < 32)
        masks.append(ok)
    return masks


def shift(field, tap, masks):
    if tap == 4:
        return field
    offset = (tap // 3 - 1) * 32 + tap % 3 - 1
    return jnp.where(masks[tap], pltpu.roll(field, (-offset) % PX, 1), 0.0)


def expand(field, flip, one, masks):
    high = field.astype(bf16).astype(f32)
    low = field - high
    row = lax.broadcasted_iota(jnp.int32, (8, PX), 0)
    base = jnp.where(row < 3, high, jnp.where(row < 6, pltpu.roll(low, 3, 0), one))
    parts = [shift(base, 8 - tap if flip else tap, masks) for tap in range(9)]
    return jnp.concatenate(parts + [jnp.zeros((8, PX), f32)], 0).astype(bf16)


def collapse(prod, flip, masks):
    total = prod[32:40]
    for tap in (0, 1, 2, 3, 5, 6, 7, 8):
        total = total + shift(prod[8 * tap : 8 * tap + 8], 8 - tap if flip else tap, masks)
    return total + pltpu.roll(total, 5, 0)


def pieces(h, slope_half):
    x = slope_half * h
    t = jnp.tanh(x)
    e = 1.0 - t * t
    return x, t, e


def softplus(raw):
    return jnp.maximum(raw, 0.0) + jnp.log1p(jnp.exp(-jnp.abs(raw)))


def sigmoid(raw):
    return 1.0 / (1.0 + jnp.exp(-raw))


def wide(ref, width):
    block = ref[...]
    return jnp.concatenate([block] * (width // 128), 1)


def to_column(row):
    return jnp.transpose(jnp.broadcast_to(row, (128, C)))


def prepare_side(side, lefts, out_left, stage, wa1, wp1, wa3, wp3, cols):
    rows = lax.broadcasted_iota(jnp.int32, (80, C), 0)
    stage[...] = jnp.zeros_like(stage)
    for color in range(3):
        for tap in range(9):
            stage[0, 8 * tap + color : 8 * tap + color + 1, :] = side[9 * color + tap : 9 * color + tap + 1, :]
            at = 31 + 9 * color + tap
            stage[1, 8 * tap + color : 8 * tap + color + 1, :] = side[at : at + 1, :]
    first = stage[0]
    u = lefts[0:1, :]
    right1 = jnp.sum(first * u, axis=1, keepdims=True)
    right1 = right1 / jnp.sqrt(jnp.sum(right1 * right1) + 1e-12)
    y1 = jnp.sum(first * right1, axis=0, keepdims=True)
    left1 = y1 / jnp.sqrt(jnp.sum(y1 * y1) + 1e-12)
    sigma1 = jnp.sum(left1 * y1)
    last = stage[1]
    inner = rows % 8
    weight = jnp.where(inner == 0, out_left[0], jnp.where(inner == 1, out_left[1], out_left[2]))
    mixed = jnp.where(inner < 3, last * weight, 0.0)
    right3 = mixed + pltpu.roll(mixed, 79, 0) + pltpu.roll(mixed, 78, 0)
    right3 = jnp.where(inner == 0, right3, 0.0)
    right3 = right3 / jnp.sqrt(jnp.sum(right3 * right3) + 1e-12)
    right3 = right3 + pltpu.roll(right3, 1, 0) + pltpu.roll(right3, 2, 0)
    prod = last * right3
    y3 = [jnp.sum(jnp.where(inner == k, prod, 0.0)) for k in range(3)]
    norm3 = jnp.sqrt(y3[0] * y3[0] + y3[1] * y3[1] + y3[2] * y3[2] + 1e-12)
    left3 = [value / norm3 for value in y3]
    sigma3 = left3[0] * y3[0] + left3[1] * y3[1] + left3[2] * y3[2]
    outer3 = jnp.where(inner == 0, left3[0], jnp.where(inner == 1, left3[1], left3[2])) * right3
    outer1 = right1 * left1
    q1, q3 = jnp.maximum(1.0, sigma1 / CLIP), jnp.maximum(1.0, sigma3 / CLIP)
    for at, q, wa, wp in ((0, q1, wa1, wp1), (1, q3, wa3, wp3)):
        scaled = stage[at] / (LIP * q)
        high = scaled.astype(bf16).astype(f32)
        low = scaled - high
        top = high + pltpu.roll(high, 3, 0)
        if at == 0:
            bias = side[27:28, :]
            bias_high = bias.astype(bf16).astype(f32)
            top = jnp.where(rows == 38, bias_high, jnp.where(rows == 39, bias - bias_high, top))
        wa[0:80, :] = top.astype(bf16)
        wa[80:160, :] = (low + pltpu.roll(low, 3, 0)).astype(bf16)
        wp[...] = (high + pltpu.roll(low, 3, 0)).astype(bf16)
    cols[0] = to_column(0.5 * softplus(side[28:29, :]))
    cols[1] = to_column(side[29:30, :])
    cols[2] = to_column(0.5 * softplus(side[30:31, :]))
    cols[3] = to_column(lefts[1:2, :])
    return (q1, sigma1, outer1), (q3, sigma3, outer3)


def prepare_mid(mid, cols, m_high, m_low):
    full = mid[...]
    right = jnp.sum(full * wide(cols.at[3], C), axis=0, keepdims=True)
    right = right / jnp.sqrt(jnp.sum(right * right) + 1e-12)
    y = jnp.sum(full * right, axis=1, keepdims=True)
    left = y / jnp.sqrt(jnp.sum(y * y) + 1e-12)
    sigma = jnp.sum(left * y)
    q = jnp.maximum(1.0, sigma / CLIP)
    scaled = full / (LIP * q)
    high = scaled.astype(bf16)
    m_high[...] = high
    m_low[...] = (scaled - high.astype(f32)).astype(bf16)
    return q, sigma, left, right


def correction(raw_grad, weight, q, sigma):
    ratio = sigma / CLIP
    active = jnp.where(ratio > 1.0, 1.0, jnp.where(ratio == 1.0, 0.5, 0.0))
    return 1.0 / (LIP * q), -active * jnp.sum(raw_grad * weight) / (LIP * q * q * CLIP)


def color_column(values):
    row = lax.broadcasted_iota(jnp.int32, (8, 1), 0)
    return jnp.where(row == 0, values[0], jnp.where(row == 1, values[1], values[2]))


PARTS = PX // TILE


def tile_at(image, part):
    if isinstance(image, int):
        return slice(image * PX + part * TILE, image * PX + (part + 1) * TILE)
    return pl.ds(pl.multiple_of(image * PX + part * TILE, TILE), TILE)


def each_image(body):
    lax.fori_loop(0, 2, lambda b, c: (body(b), c)[1], 0)


def compute(side, mid, lefts, out_left, tiny, live, images, probes, cotangents, s, o):
    side1, side3 = prepare_side(side, lefts, out_left, s["stage"], s["wa1"], s["wp1"], s["wa3"], s["wp3"], s["cols"])
    bias_col = color_column([tiny[0, k] for k in range(3)])
    shift_col = color_column([tiny[1, k] for k in range(3)])
    scale_col = jnp.exp(color_column([tiny[2, k] for k in range(3)]))
    slope_raw = color_column([tiny[3, k] for k in range(3)])
    slope0 = 0.5 * softplus(slope_raw)
    wa1, wp1, wa3, wp3 = s["wa1"], s["wp1"], s["wa3"], s["wp3"]
    slope1 = lambda: wide(s["cols"].at[0], TILE)
    bias2 = lambda: wide(s["cols"].at[1], TILE)
    slope2 = lambda: wide(s["cols"].at[2], TILE)
    valid = lambda: lax.broadcasted_iota(jnp.int32, (8, PX), 0) < 3
    s["small"][...] = jnp.zeros_like(s["small"])
    SZ, SP, SC, SD, SV, SN, SS, ST, SA, SB = range(10)

    def alive(b, step):
        row = live[pl.ds(b * 4 + step, 1), :]
        return jnp.concatenate([row] * (PX // 128), 1)

    def doubled(index, part):
        block = s["field"][index, :, part * TILE : (part + 1) * TILE]
        return jnp.concatenate([block, block], 0)

    def layer_one(b):
        masks = tap_masks()
        s["small"][SZ, b, 0:3] = images[b]
        s["small"][SP, b, 0:3] = probes[b]
        s["small"][SC, b, 0:3] = cotangents[b]
        field = (s["small"][SZ, b] + shift_col) * scale_col
        p = s["small"][SP, b]
        s["small"][SZ, b] = field
        x, t, e = pieces(field, slope0)
        d0 = 1.0 + t + x * e
        s["small"][SD, b] = d0
        s["field"][b] = expand(field + field * t, False, 1.0, masks)
        s["field"][2 + b] = expand(d0 * p, False, 0.0, masks)
        s["field"][4 + b] = expand(s["small"][SC, b], True, 0.0, masks)
        s["small"][SV, b] = p
        s["small"][SN, b] = -alive(b, 0) * p
        s["small"][SS, b] = alive(b, 0) * p
        for part in range(PARTS):
            at = tile_at(b, part)
            h = dot_tn(wa1[...], doubled(b, part))
            x, t, e = pieces(h, slope1())
            d = 1.0 + t + x * e
            dh = dot_tn(wa1[...], doubled(2 + b, part))
            s["h1"][:, at] = h
            s["g1"][:, at] = dh
            s["d1"][:, at] = d.astype(bf16)
            s["a1"][:, at] = (h + h * t).astype(bf16)
            s["b1"][:, at] = (d * dh).astype(bf16)

    each_image(layer_one)
    q2, sigma2, left2, right2 = prepare_mid(mid, s["cols"], s["mh"], s["ml"])

    def layer_two(b):
        masks = tap_masks()
        prods, dprods = [], []
        for part in range(PARTS):
            at = tile_at(b, part)
            a1 = s["a1"][:, at]
            h = dot_nn(s["mh"][...], a1) + dot_nn(s["ml"][...], a1) + bias2()
            x, t, e = pieces(h, slope2())
            d = 1.0 + t + x * e
            dh = dot_nn(s["mh"][...], s["b1"][:, at])
            s["h2"][:, at] = h
            s["g2"][:, at] = dh
            s["d2"][:, at] = d.astype(bf16)
            a2 = (h + h * t).astype(bf16)
            b2 = (d * dh).astype(bf16)
            s["a2"][:, at] = a2
            s["b2"][:, at] = b2
            prods.append(dot_nn(wp3[...], a2))
            dprods.append(dot_nn(wp3[...], b2))
        g = collapse(jnp.concatenate(prods, 1), False, masks)
        o["flow"][b] = (s["small"][SZ, b] + g + bias_col)[0:3]
        s["small"][ST, b] = jnp.where(valid(), collapse(jnp.concatenate(dprods, 1), False, masks), 0.0)

    each_image(layer_two)

    def pull(step, sign):
        masks = tap_masks()
        for b in range(2):
            spread = expand(s["small"][SV, b], True, 0.0, masks)
            prods = []
            for part in range(PARTS):
                at = tile_at(b, part)
                block = spread[:, part * TILE : (part + 1) * TILE]
                u2 = dot_tn(wa3[...], jnp.concatenate([block, block], 0)).astype(bf16) * s["d2"][:, at]
                u1 = dot_tn(s["mh"][...], u2).astype(bf16) * s["d1"][:, at]
                prods.append(dot_nn(wp1[...], u1))
            v = jnp.where(valid(), s["small"][SD, b] * collapse(jnp.concatenate(prods, 1), True, masks), 0.0)
            on = sign * alive(b, step + 1)
            s["small"][SV, b] = v
            s["small"][SN, b] = s["small"][SN, b] - on * v
            s["small"][SS, b] = s["small"][SS, b] + (on / (step + 2).astype(f32)) * v
        return -sign

    lax.fori_loop(0, 3, pull, jnp.float32(-1.0))
    s["sums"][...] = jnp.zeros_like(s["sums"])

    def back_two(b):
        masks = tap_masks()
        s["field"][6 + b] = expand(s["small"][SN, b], True, 0.0, masks)
        slope_sum, bias_sum = s["sums"][1], s["sums"][0]
        for part in range(PARTS):
            at = tile_at(b, part)
            h = s["h2"][:, at]
            sl = slope2()
            x, t, e = pieces(h, sl)
            d = 1.0 + t + x * e
            c_a = dot_tn(wa3[...], doubled(4 + b, part))
            t_a = dot_tn(wa3[...], doubled(6 + b, part))
            q = (2.0 * e * (1.0 - x * t)) * s["g2"][:, at] * t_a
            c_h = d * c_a + sl * q
            grad = h * (c_a * h * e + q)
            for k in range(TILE // 128):
                slope_sum = slope_sum + grad[:, k * 128 : (k + 1) * 128]
                bias_sum = bias_sum + c_h[:, k * 128 : (k + 1) * 128]
            s["c2"][:, at] = c_h.astype(bf16)
            s["t2"][:, at] = (d * t_a).astype(bf16)
        s["sums"][1] = slope_sum
        s["sums"][0] = bias_sum

    each_image(back_two)
    raw = dot_nt(s["c2"][...], s["a1"][...]) + dot_nt(s["t2"][...], s["b1"][...])
    straight, across = correction(raw, mid[...], q2, sigma2)
    o["mid"][...] = straight * raw + (across * left2) * right2
    g3 = dot_nt(s["field"][4], s["a2"][:, 0:PX]) + dot_nt(s["field"][6], s["b2"][:, 0:PX])
    s["stage2"][1] = g3 + dot_nt(s["field"][5], s["a2"][:, PX:]) + dot_nt(s["field"][7], s["b2"][:, PX:])

    def back_one(b):
        masks = tap_masks()
        slope_sum = s["sums"][2]
        prods, dprods = [], []
        for part in range(PARTS):
            at = tile_at(b, part)
            h = s["h1"][:, at]
            sl = slope1()
            x, t, e = pieces(h, sl)
            d = 1.0 + t + x * e
            c2 = s["c2"][:, at]
            c_a = dot_tn(s["mh"][...], c2) + dot_tn(s["ml"][...], c2)
            t_a = dot_tn(s["mh"][...], s["t2"][:, at])
            q = (2.0 * e * (1.0 - x * t)) * s["g1"][:, at] * t_a
            c_h = (d * c_a + sl * q).astype(bf16)
            t_h = (d * t_a).astype(bf16)
            grad = h * (c_a * h * e + q)
            for k in range(TILE // 128):
                slope_sum = slope_sum + grad[:, k * 128 : (k + 1) * 128]
            prods.append(dot_nn(wp1[...], c_h))
            dprods.append(dot_nn(wp1[...], t_h))
            s["a2"][:, at] = c_h
            s["b2"][:, at] = t_h
        s["sums"][2] = slope_sum
        s["small"][SA, b] = collapse(jnp.concatenate(prods, 1), True, masks)
        s["small"][SB, b] = collapse(jnp.concatenate(dprods, 1), True, masks)

    each_image(back_one)
    g1 = dot_nt(s["field"][0], s["a2"][:, 0:PX]) + dot_nt(s["field"][2], s["b2"][:, 0:PX])
    g1 = g1 + dot_nt(s["field"][1], s["a2"][:, PX:]) + dot_nt(s["field"][3], s["b2"][:, PX:])
    g3 = s["stage2"][1]
    lane = lax.broadcasted_iota(jnp.int32, (8, 128), 1)
    sub = lax.broadcasted_iota(jnp.int32, (8, 128), 0)
    total_scale = tiny[2, 0] + tiny[2, 1] + tiny[2, 2]
    tile = jnp.zeros((8, 128), f32)
    for b in range(2):
        field, p, cot = s["small"][SZ, b], s["small"][SP, b], s["small"][SC, b]
        c_a, t_a = s["small"][SA, b], s["small"][SB, b]
        x, t, e = pieces(field, slope0)
        q = 2.0 * e * (1.0 - x * t) * p * t_a
        c_z = jnp.where(valid(), cot + (1.0 + t + x * e) * c_a + slope0 * q, 0.0)
        slope_grad = jnp.where(valid(), field * (c_a * field * e + q), 0.0)
        o["back"][b] = (c_z * scale_col)[0:3]
        sums = [
            jnp.sum(cot, axis=1, keepdims=True),
            jnp.sum(c_z, axis=1, keepdims=True) * scale_col,
            jnp.sum(c_z * field, axis=1, keepdims=True) - 1024.0,
            jnp.sum(slope_grad, axis=1, keepdims=True) * (0.5 * sigmoid(slope_raw)),
        ]
        for r in range(4):
            tile = tile + jnp.where((lane == r) & (sub < 3), sums[r], 0.0)
        log_part = (1024.0 * total_scale + jnp.sum(s["small"][SS, b] * s["small"][ST, b])) / 3072.0
        tile = tile + jnp.where((lane == 4) & (sub == b), log_part, 0.0)
    eye = (sub == lane).astype(f32)
    flipped = lax.dot_general(tile, eye, (((0,), (0,)), ((), ())), precision=HIGH, preferred_element_type=f32)
    o["tiny"][...] = flipped[0:8]
    ones = jnp.ones((8, 128), f32)
    lanes_to_row = lambda acc: lax.dot_general(ones, acc, (((1,), (1,)), ((), ())), precision=HIGH, preferred_element_type=f32)[0:1]
    o["side"][27:28, :] = g1[38:39]
    o["side"][28:29, :] = lanes_to_row(s["sums"][2]) * (0.5 * sigmoid(side[28:29, :]))
    o["side"][29:30, :] = lanes_to_row(s["sums"][0])
    o["side"][30:31, :] = lanes_to_row(s["sums"][1]) * (0.5 * sigmoid(side[30:31, :]))
    o["side"][58:64, :] = jnp.zeros((6, C), f32)
    inner = lax.broadcasted_iota(jnp.int32, (80, C), 0) % 8
    for at, (q, sigma, outer), raw, start in ((0, side1, g1, 0), (1, side3, g3, 31)):
        joined = jnp.where(inner < 3, raw + pltpu.roll(raw, 77, 0), 0.0)
        joined = jnp.where(lax.broadcasted_iota(jnp.int32, (80, C), 0) < 72, joined, 0.0)
        straight, across = correction(joined, s["stage"][at], q, sigma)
        s["stage2"][at] = straight * joined + across * outer
        for color in range(3):
            for tap in range(9):
                to = start + 9 * color + tap
                o["side"][to : to + 1, :] = s["stage2"][at, 8 * tap + color : 8 * tap + color + 1, :]


def big(dtype):
    return pltpu.VMEM((C, 2 * PX), dtype)


SCRATCH = dict(
    stage=pltpu.VMEM((2, 80, C), f32),
    stage2=pltpu.VMEM((2, 80, C), f32),
    wa1=pltpu.VMEM((160, C), bf16),
    wp1=pltpu.VMEM((80, C), bf16),
    wa3=pltpu.VMEM((160, C), bf16),
    wp3=pltpu.VMEM((80, C), bf16),
    cols=pltpu.VMEM((4, C, 128), f32),
    small=pltpu.VMEM((10, 2, 8, PX), f32),
    sums=pltpu.VMEM((3, C, 128), f32),
    field=pltpu.VMEM((8, 80, PX), bf16),
    mh=pltpu.VMEM((C, C), bf16),
    ml=pltpu.VMEM((C, C), bf16),
    h1=big(f32), g1=big(f32), h2=big(f32), g2=big(f32),
    d1=big(bf16), a1=big(bf16), b1=big(bf16),
    d2=big(bf16), a2=big(bf16), b2=big(bf16),
    c2=big(bf16), t2=big(bf16),
)
NAMES = list(SCRATCH)


def kernel(side, mid, lefts, out_left, tiny, live, images, probes, cotangents, flow, back, mid_grad, side_grad, tiny_out, *scratch):
    s = dict(zip(NAMES, scratch))
    o = dict(flow=flow, back=back, mid=mid_grad, side=side_grad, tiny=tiny_out)
    ol = [out_left[0, k] for k in range(3)]
    compute(side, mid, lefts, ol, tiny, live, images, probes, cotangents, s, o)


def core(side, mid, lefts, out_left, tiny, live, images, probes, cotangents):
    vm = pl.BlockSpec(memory_space=pltpu.VMEM)
    sm = pl.BlockSpec(memory_space=pltpu.SMEM)
    sd = jax.ShapeDtypeStruct
    return pl.pallas_call(
        kernel,
        in_specs=[vm, vm, vm, sm, sm, vm, vm, vm, vm],
        out_specs=[vm] * 5,
        out_shape=[sd((2, 3, PX), f32), sd((2, 3, PX), f32), sd((C, C), f32), sd((64, C), f32), sd((8, 128), f32)],
        scratch_shapes=list(SCRATCH.values()),
        compiler_params=pltpu.CompilerParams(vmem_limit_bytes=60 << 20),
    )(side, mid, lefts, out_left, tiny, live, images, probes, cotangents)


MESH = pl.DeviceIdType.MESH


def scale_sizes(n):
    w = C // n
    fold = 128 // w
    return w, fold, C // fold, 64 // fold


def pack(block, fold):
    rows = block.shape[0] // fold
    return jnp.concatenate([block[i * rows : (i + 1) * rows] for i in range(fold)], 1)


def unpack(block, fold):
    w = 128 // fold
    return jnp.concatenate([block[:, i * w : (i + 1) * w] for i in range(fold)], 0)


def spread_rows(blocks, fold):
    w = 128 // fold
    return [jnp.concatenate([block[:, i * w : (i + 1) * w] for block in blocks], 1) for i in range(fold)]


class Gather:
    def __init__(self, n, buf, sems):
        self.n, self.m, self.buf, self.sems = n, n // 2, buf, sems
        self.me = lax.axis_index("dp")
        self.chip, self.core = self.me // 2, self.me % 2
        self.pair = self.me + 1 - 2 * self.core

    def copy(self, slot, sem, target):
        return pltpu.make_async_remote_copy(
            src_ref=self.buf.at[slot],
            dst_ref=self.buf.at[slot],
            send_sem=self.sems.at[0, sem],
            recv_sem=self.sems.at[1, sem],
            device_id={"dp": target},
            device_id_type=MESH,
        )

    def peer(self, j):
        return lax.rem(self.chip + j, self.m) * 2 + self.core

    def start(self):
        for j in range(1, self.m):
            self.copy(self.me, j, self.peer(j)).start()
        self.copy(self.me, self.m, self.pair).start()

    def forward(self):
        for j in range(1, self.m):
            source = self.peer(j)
            self.copy(source, self.m - j, source).wait_recv()
            self.copy(source, self.m + j, self.pair).start()

    def finish(self):
        for j in range(self.m):
            self.copy(self.me, self.m + j, self.pair).wait_recv()
        for j in range(1, 2 * self.m):
            self.copy(self.me, j, self.pair).wait_send()


def barrier(n, groups):
    me, grp = lax.axis_index("dp"), lax.axis_index("grp")
    sem = pltpu.get_barrier_semaphore()
    m = n // 2
    chip, core = me // 2, me % 2
    for j in range(1, m):
        pl.semaphore_signal(sem, inc=1, device_id={"dp": lax.rem(chip + j, m) * 2 + core}, device_id_type=MESH)
    pl.semaphore_signal(sem, inc=1, device_id={"dp": me + 1 - 2 * core}, device_id_type=MESH)
    for j in range(1, groups):
        pl.semaphore_signal(sem, inc=1, device_id={"grp": lax.rem(grp + j, groups)}, device_id_type=MESH)
    pl.semaphore_wait(sem, m + groups - 1)


def put_chunks(ref, lead, base, field):
    rows = field.shape[0]
    for k in range(8):
        ref[lead, base + k * rows : base + (k + 1) * rows, :] = field[:, k * 128 : (k + 1) * 128]


def get_chunks(block, base, rows):
    return jnp.concatenate([block[base + k * rows : base + (k + 1) * rows] for k in range(8)], 1)


def match(counts, me, wanted_mine, wanted_theirs):
    n = len(counts)
    zero = jnp.zeros((1, 128), f32)
    mine, my_rank = zero, zero
    for d in range(n):
        hit = jnp.where(counts[d] == wanted_mine, 1.0, 0.0)
        my_rank = my_rank + jnp.where(d < me, hit, zero)
        mine = mine + jnp.where(d == me, hit, zero)
    rank, masks = zero, []
    for d in range(n):
        hit = jnp.where(counts[d] == wanted_theirs, 1.0, 0.0)
        masks.append(jnp.where(rank == my_rank, hit * mine, zero))
        rank = rank + hit
    return masks


def gather_kernel(n, groups, mid_w, side_w, images, probes, cotangents, counts, terms,
                  mid, side, im, pr, co, live, early, late, early_sem, late_sem):
    w, fold, mid_rows, side_rows = scale_sizes(n)
    me = lax.axis_index("dp")
    first, second = Gather(n, early, early_sem), Gather(n, late, late_sem)
    early[me, 0:side_rows, :] = pack(jnp.concatenate([side_w[...], jnp.zeros((6, w), f32)], 0), fold)
    third = jnp.concatenate([images[2], probes[2], cotangents[2]], 0)
    put_chunks(early, me, side_rows, third)
    lane = lax.broadcasted_iota(jnp.int32, (8, 128), 1)
    meta = jnp.where(lane == 0, counts[0, 0].astype(f32), terms[0, 2].astype(f32))
    early[me, side_rows + 72 : side_rows + 80, :] = meta
    late[me] = pack(mid_w[...], fold)
    barrier(n, groups)
    first.start()
    second.start()
    first.forward()
    first.finish()
    blocks = [early[d] for d in range(n)]
    rows = spread_rows([block[0:side_rows] for block in blocks], fold)
    for i in range(fold):
        side[i * side_rows : (i + 1) * side_rows, :] = rows[i]
    metas = [block[side_rows + 72 : side_rows + 73] for block in blocks]
    count_rows = [jnp.broadcast_to(meta[:, 0:1], (1, 128)) for meta in metas]
    term_rows = [jnp.broadcast_to(meta[:, 1:2], (1, 128)) for meta in metas]
    masks = match(count_rows, me, 1.0, 3.0)
    picked, term = jnp.zeros((72, 128), f32), jnp.zeros((1, 128), f32)
    helper = jnp.zeros((1, 128), f32)
    for d in range(n):
        picked = jnp.where(masks[d] > 0.0, blocks[d][side_rows : side_rows + 72], picked)
        term = jnp.where(masks[d] > 0.0, term_rows[d], term)
        helper = helper + masks[d]
    other = get_chunks(picked, 0, 9)
    wide_helper = jnp.concatenate([helper] * 8, 1)
    for at, (out, own) in enumerate(((im, images), (pr, probes), (co, cotangents))):
        out[0] = own[0]
        out[1] = jnp.where(wide_helper > 0.0, other[3 * at : 3 * at + 3], own[1])
    sub = lax.broadcasted_iota(jnp.int32, (8, 128), 0)
    second_term = jnp.where(helper > 0.0, term, terms[0, 1].astype(f32))
    limit = jnp.where(sub < 4, terms[0, 0].astype(f32), second_term)
    live[...] = jnp.where(limit > (sub % 4).astype(f32), 1.0, 0.0)
    second.forward()
    second.finish()
    rows = spread_rows([late[d] for d in range(n)], fold)
    for i in range(fold):
        mid[i * mid_rows : (i + 1) * mid_rows, :] = rows[i]


def adam(weight, gradient, first, second, rate):
    first = 0.9 * first + (1.0 - 0.9) * gradient
    second = 0.999 * second + (1.0 - 0.999) * gradient * gradient
    first_hat = first / (1.0 - 0.9**5.0)
    second_hat = second / (1.0 - 0.999**5.0)
    return weight - rate * (first_hat / (jnp.sqrt(second_hat) + 1e-8) + 0.01 * weight), first, second


def update_kernel(n, groups, mid_grad, side_grad, tiny_grad, flow_in, back_in, counts,
                  mid_w, mid_f, mid_s, side_w, side_f, side_s, tiny_w, tiny_f, tiny_s,
                  mid_o, mid_m, side_o, side_m, tiny_o, tiny_m,
                  flow, back, log_det, log_mean, mid_f_new, mid_s_new, mid_new, side_f_new, side_s_new, side_new,
                  tiny_f_new, tiny_s_new, slope_s_new, tiny_new, mid_d, mid_m_new, mid_o_new,
                  side_d, side_m_new, side_o_new, tiny_d, tiny_m_new, tiny_o_new,
                  to_pair, from_pair, chipsum, from_chips, results, quarters, whole, summed, tinies,
                  pair_sem, chip_sem, result_sem, quarter_sem, whole_sem, tiny_sem):
    w, fold, mid_rows, side_rows = scale_sizes(n)
    rows = mid_rows + side_rows
    m = n // 2
    me, grp = lax.axis_index("dp"), lax.axis_index("grp")
    chip, core = me // 2, me % 2
    pair = me + 1 - 2 * core
    share = Gather(n, results, result_sem)
    for k in range(m):
        packs = []
        for c in range(2):
            at = (2 * k + c) * w
            packs.append(jnp.concatenate([pack(mid_grad[:, at : at + w], fold), pack(side_grad[:, at : at + w], fold)], 0))
        to_pair[k] = jnp.where(core == 0, packs[1], packs[0])
        chipsum[k] = jnp.where(core == 0, packs[0], packs[1])
    put_chunks(results, me, 0, jnp.concatenate([flow_in[1], back_in[1]], 0))
    tile = tiny_grad[...]
    sub = lax.broadcasted_iota(jnp.int32, (8, 128), 0)
    results[me, 48:56, :] = jnp.where(sub == 5, counts[0, 0].astype(f32), tile)
    barrier(n, groups)
    swap = pltpu.make_async_remote_copy(
        src_ref=to_pair, dst_ref=from_pair, send_sem=pair_sem.at[0], recv_sem=pair_sem.at[1],
        device_id={"dp": pair}, device_id_type=MESH)
    swap.start()
    share.start()
    swap.wait_recv()
    for k in range(m):
        chipsum[k] = chipsum[k] + from_pair[k]

    def chip_copy(source, slot, j, target):
        return pltpu.make_async_remote_copy(
            src_ref=chipsum.at[source], dst_ref=from_chips.at[slot], send_sem=chip_sem.at[0, j], recv_sem=chip_sem.at[1, j],
            device_id={"dp": target}, device_id_type=MESH)

    for j in range(1, m):
        to = lax.rem(chip + j, m)
        chip_copy(to, j, j, to * 2 + core).start()
    share.forward()
    total = chipsum[chip]
    for j in range(1, m):
        chip_copy(chip, j, j, pair).wait_recv()
        total = total + from_chips[j]
    grad = total / (2.0 * n)
    mid_g, side_g = unpack(grad[0:mid_rows], fold), unpack(grad[mid_rows:rows], fold)[0:58]
    new, first, second = adam(mid_w[...], mid_g, mid_f[...], mid_s[...], 0.01)
    mid_f_new[...], mid_s_new[...], mid_new[...] = first, second, new
    mid_diff = mid_o[...] - new
    at = lax.broadcasted_iota(jnp.int32, (58, w), 0)
    new, first, second = adam(side_w[...], side_g, side_f[...], side_s[...], jnp.where(at >= 31, 0.004, 0.05))
    side_f_new[...], side_s_new[...], side_new[...] = first, second, new
    side_diff = jnp.concatenate([side_o[...] - new, jnp.zeros((6, w), f32)], 0)
    whole[0:mid_rows, :] = pack(mid_diff, fold)
    whole[mid_rows:rows, :] = pack(side_diff, fold)
    if whole.shape[0] > rows:
        whole[rows:, :] = jnp.zeros((whole.shape[0] - rows, 128), f32)
    piece = whole.shape[0] // groups

    def part(index):
        return pl.ds(pl.multiple_of(index * piece, 8), piece)

    def quarter_copy(index, j, target):
        return pltpu.make_async_remote_copy(
            src_ref=whole.at[part(index)], dst_ref=quarters.at[grp], send_sem=quarter_sem.at[0, j], recv_sem=quarter_sem.at[1, j],
            device_id={"grp": target}, device_id_type=MESH)

    for j in range(1, groups):
        to = lax.rem(grp + j, groups)
        quarter_copy(to, j, to).start()
    quarters[grp] = whole[part(grp), :]
    share.finish()
    blocks = [results[d] for d in range(n)]
    tiny_sum = blocks[0][48:56]
    for d in range(1, n):
        tiny_sum = tiny_sum + blocks[d][48:56]
    tiny_new_v, tiny_first, tiny_second = adam(tiny_w[...], tiny_sum[0:4, 0:3] / (2.0 * n), tiny_f[...], tiny_s[...], 0.05)
    tiny_f_new[...], tiny_new[...] = tiny_first, tiny_new_v
    tiny_s_new[...] = tiny_second[0:3]
    slope_s_new[...] = tiny_second[3:4]
    log_mean[...] = (tiny_sum[4:5, 0:1] + tiny_sum[4:5, 1:2]) / (2.0 * n)
    tinies[grp] = jnp.zeros((8, 128), f32)
    tinies[grp, 0:4, 0:3] = tiny_o[...] - tiny_new_v

    def tiny_copy(j, target):
        return pltpu.make_async_remote_copy(
            src_ref=tinies.at[grp], dst_ref=tinies.at[grp], send_sem=tiny_sem.at[0, j], recv_sem=tiny_sem.at[1, j],
            device_id={"grp": target}, device_id_type=MESH)

    for j in range(1, groups):
        tiny_copy(j, lax.rem(grp + j, groups)).start()
    for j in range(1, groups):
        quarter_copy(grp, j, grp).wait_recv()
    acc = quarters[0]
    for k in range(1, groups):
        acc = acc + quarters[k]
    summed[part(grp), :] = acc

    def whole_copy(j, target):
        return pltpu.make_async_remote_copy(
            src_ref=summed.at[part(grp)], dst_ref=summed.at[part(grp)], send_sem=whole_sem.at[0, j], recv_sem=whole_sem.at[1, j],
            device_id={"grp": target}, device_id_type=MESH)

    for j in range(1, groups):
        whole_copy(j, lax.rem(grp + j, groups)).start()
    count_rows = [jnp.broadcast_to(block[53:54, 0:1], (1, 128)) for block in blocks]
    masks = match(count_rows, me, 3.0, 1.0)
    picked, log_third = jnp.zeros((48, 128), f32), jnp.zeros((1, 128), f32)
    own_count = jnp.zeros((1, 128), f32) + counts[0, 0].astype(f32)
    for d in range(n):
        picked = jnp.where(masks[d] > 0.0, blocks[d][0:48], picked)
        log_third = jnp.where(masks[d] > 0.0, jnp.broadcast_to(blocks[d][52:53, 1:2], (1, 128)), log_third)
    other = get_chunks(picked, 0, 6)
    has_two = jnp.concatenate([own_count] * 8, 1) > 1.5
    for out, own, base in ((flow, flow_in, 0), (back, back_in, 3)):
        out[0] = own[0]
        out[1] = jnp.where(has_two, own[1], 0.0)
        out[2] = other[base : base + 3]
    lane = lax.broadcasted_iota(jnp.int32, (1, 128), 1)
    own_logs = tile[4:5]
    logs = jnp.where(lane == 0, own_logs, jnp.where(lane == 1, jnp.where(own_count > 1.5, own_logs, 0.0), log_third))
    log_det[...] = logs[:, 0:3]
    for j in range(1, groups):
        tiny_copy(j, grp).wait_recv()
    tiny_total = tinies[0]
    for k in range(1, groups):
        tiny_total = tiny_total + tinies[k]

    def outer(diff, o, mom, d_out, m_out, o_out):
        delta = diff / groups
        mom_new = 0.9 * mom[...] + delta
        d_out[...], m_out[...] = delta, mom_new
        o_out[...] = o[...] - 0.7 * (delta + 0.9 * mom_new)

    outer(tiny_total[0:4, 0:3], tiny_o, tiny_m, tiny_d, tiny_m_new, tiny_o_new)
    for j in range(1, groups):
        whole_copy(j, grp).wait_recv()
    outer(unpack(summed[0:mid_rows, :], fold), mid_o, mid_m, mid_d, mid_m_new, mid_o_new)
    outer(unpack(summed[mid_rows:rows, :], fold)[0:58], side_o, side_m, side_d, side_m_new, side_o_new)
    swap.wait_send()
    for j in range(1, m):
        chip_copy(chip, j, j, pair).wait_send()
    for j in range(1, groups):
        quarter_copy(grp, j, grp).wait_send()
        whole_copy(j, grp).wait_send()
        tiny_copy(j, grp).wait_send()


def on_device(images, probes, out_cotangent, counts, terms, power_left, power_out, mid_weight, mid_first, mid_second,
              side_weight, side_first, side_second, tiny_weight, tiny_first, tiny_second,
              mid_outer, mid_momentum, side_outer, side_momentum, tiny_outer, tiny_momentum):
    n, groups = lax.axis_size("dp"), lax.axis_size("grp")
    w, fold, mid_rows, side_rows = scale_sizes(n)
    rows = mid_rows + side_rows
    padded = -(-rows // (8 * groups)) * 8 * groups
    vm = pl.BlockSpec(memory_space=pltpu.VMEM)
    sm = pl.BlockSpec(memory_space=pltpu.SMEM)
    sd = lambda *shape: jax.ShapeDtypeStruct(shape, f32)
    dma = lambda *shape: pltpu.SemaphoreType.DMA(shape)
    mid, side, im, pr, co, live = pl.pallas_call(
        functools.partial(gather_kernel, n, groups),
        in_specs=[vm] * 5 + [sm] * 2,
        out_specs=[vm] * 6,
        out_shape=[sd(C, C), sd(64, C), sd(2, 3, PX), sd(2, 3, PX), sd(2, 3, PX), sd(8, 128)],
        scratch_shapes=[
            pltpu.VMEM((n, side_rows + 80, 128), f32),
            pltpu.VMEM((n, mid_rows, 128), f32),
            dma(2, n), dma(2, n),
        ],
        compiler_params=pltpu.CompilerParams(vmem_limit_bytes=60 << 20, collective_id=0, has_side_effects=True),
    )(mid_weight[0], side_weight[0], images[0], probes[0], out_cotangent[0], counts, terms)
    flow, back, mid_grad, side_grad, tiny_grad = core(side, mid, power_left[0], power_out, tiny_weight[0], live, im, pr, co)
    small = [sd(3, 3, PX), sd(3, 3, PX), sd(1, 3), sd(1, 1)]
    shard = [sd(C, w)] * 3 + [sd(58, w)] * 3
    outs = pl.pallas_call(
        functools.partial(update_kernel, n, groups),
        in_specs=[vm] * 5 + [sm] + [vm] * 15,
        out_specs=[vm] * 23,
        out_shape=small + shard + [sd(4, 3), sd(3, 3), sd(1, 3), sd(4, 3)] + shard + [sd(4, 3)] * 3,
        scratch_shapes=[
            pltpu.VMEM((n // 2, rows, 128), f32),
            pltpu.VMEM((n // 2, rows, 128), f32),
            pltpu.VMEM((n // 2, rows, 128), f32),
            pltpu.VMEM((n // 2, rows, 128), f32),
            pltpu.VMEM((n, 56, 128), f32),
            pltpu.VMEM((groups, padded // groups, 128), f32),
            pltpu.VMEM((padded, 128), f32),
            pltpu.VMEM((padded, 128), f32),
            pltpu.VMEM((groups, 8, 128), f32),
            dma(2), dma(2, n // 2), dma(2, n), dma(2, groups), dma(2, groups), dma(2, groups),
        ],
        compiler_params=pltpu.CompilerParams(vmem_limit_bytes=60 << 20, collective_id=1, has_side_effects=True),
    )(mid_grad, side_grad, tiny_grad, flow, back, counts,
      mid_weight[0], mid_first[0], mid_second[0], side_weight[0], side_first[0], side_second[0],
      tiny_weight[0], tiny_first[0], tiny_second[0],
      mid_outer, mid_momentum, side_outer, side_momentum, tiny_outer, tiny_momentum)
    outs = list(outs)
    outs[3] = outs[3].reshape(1)
    for k in (0, 1) + tuple(range(4, 12)) + (13,):
        outs[k] = outs[k][None]
    return tuple(outs)


def solution(mesh):
    split = P("grp", None, "dp")
    group = P("grp", None, None)
    image = P("grp", "dp", None, None)
    return jax.shard_map(
        on_device,
        mesh=mesh,
        in_specs=(image, image, image, P("grp", "dp"), P("grp", "dp"), group, P("grp", None),
                  split, split, split, split, split, split, group, group, group,
                  P(None, "dp"), P(None, "dp"), P(None, "dp"), P(None, "dp"), P(), P()),
        out_specs=(image, image, P("grp", "dp"), P("grp"), split, split, split, split, split, split,
                   group, group, P("grp", None), group) + (P(None, "dp"),) * 6 + (P(), P(), P()),
        check_vma=False,
    )
```

```python
import functools
import types

import jax, jax.numpy as jnp
from jax import lax
from jax.experimental import pallas as pl
from jax.experimental.pallas import tpu as pltpu
from jax.sharding import PartitionSpec as P

bf16, f32 = jnp.bfloat16, jnp.float32
HIGH = lax.Precision.HIGHEST
C, PX, TILE = 512, 1024, 512
CLIP = 0.98
LIP = 2.2


def dot_nn(a, b):
    return jnp.dot(a, b, preferred_element_type=f32)


def dot_tn(a, b):
    return lax.dot_general(a, b, (((0,), (0,)), ((), ())), preferred_element_type=f32)


def dot_nt(a, b):
    return lax.dot_general(a, b, (((1,), (1,)), ((), ())), preferred_element_type=f32)


def tap_masks():
    lane = lax.broadcasted_iota(jnp.int32, (8, PX), 1)
    row, col = lane // 32, lane % 32
    masks = []
    for tap in range(9):
        down, right = tap // 3 - 1, tap % 3 - 1
        ok = (row + down >= 0) & (row + down < 32) & (col + right >= 0) & (col + right < 32)
        masks.append(ok)
    return masks


def shift(field, tap, masks):
    if tap == 4:
        return field
    offset = (tap // 3 - 1) * 32 + tap % 3 - 1
    return jnp.where(masks[tap], pltpu.roll(field, (-offset) % PX, 1), 0.0)


def expand(field, flip, one, masks):
    high = field.astype(bf16).astype(f32)
    low = field - high
    row = lax.broadcasted_iota(jnp.int32, (8, PX), 0)
    base = jnp.where(row < 3, high, jnp.where(row < 6, pltpu.roll(low, 3, 0), one))
    parts = [shift(base, 8 - tap if flip else tap, masks) for tap in range(9)]
    return jnp.concatenate(parts + [jnp.zeros((8, PX), f32)], 0).astype(bf16)


def collapse(prod, flip, masks):
    total = prod[32:40]
    for tap in (0, 1, 2, 3, 5, 6, 7, 8):
        total = total + shift(prod[8 * tap : 8 * tap + 8], 8 - tap if flip else tap, masks)
    return total + pltpu.roll(total, 5, 0)


def pieces(h, slope_half):
    x = slope_half * h
    t = jnp.tanh(x)
    e = 1.0 - t * t
    return x, t, e


def softplus(raw):
    return jnp.maximum(raw, 0.0) + jnp.log1p(jnp.exp(-jnp.abs(raw)))


def sigmoid(raw):
    return 1.0 / (1.0 + jnp.exp(-raw))


def wide(ref, width):
    block = ref[...]
    return jnp.concatenate([block] * (width // 128), 1)


def to_column(row):
    return jnp.transpose(jnp.broadcast_to(row, (128, C)))


def prepare_side(side, lefts, out_left, stage, wa1, wp1, wa3, wp3, cols):
    rows = lax.broadcasted_iota(jnp.int32, (80, C), 0)
    stage[...] = jnp.zeros_like(stage)
    for color in range(3):
        for tap in range(9):
            stage[0, 8 * tap + color : 8 * tap + color + 1, :] = side[9 * color + tap : 9 * color + tap + 1, :]
            at = 31 + 9 * color + tap
            stage[1, 8 * tap + color : 8 * tap + color + 1, :] = side[at : at + 1, :]
    first = stage[0]
    u = lefts[0:1, :]
    right1 = jnp.sum(first * u, axis=1, keepdims=True)
    right1 = right1 / jnp.sqrt(jnp.sum(right1 * right1) + 1e-12)
    y1 = jnp.sum(first * right1, axis=0, keepdims=True)
    left1 = y1 / jnp.sqrt(jnp.sum(y1 * y1) + 1e-12)
    sigma1 = jnp.sum(left1 * y1)
    last = stage[1]
    inner = rows % 8
    weight = jnp.where(inner == 0, out_left[0], jnp.where(inner == 1, out_left[1], out_left[2]))
    mixed = jnp.where(inner < 3, last * weight, 0.0)
    right3 = mixed + pltpu.roll(mixed, 79, 0) + pltpu.roll(mixed, 78, 0)
    right3 = jnp.where(inner == 0, right3, 0.0)
    right3 = right3 / jnp.sqrt(jnp.sum(right3 * right3) + 1e-12)
    right3 = right3 + pltpu.roll(right3, 1, 0) + pltpu.roll(right3, 2, 0)
    prod = last * right3
    y3 = [jnp.sum(jnp.where(inner == k, prod, 0.0)) for k in range(3)]
    norm3 = jnp.sqrt(y3[0] * y3[0] + y3[1] * y3[1] + y3[2] * y3[2] + 1e-12)
    left3 = [value / norm3 for value in y3]
    sigma3 = left3[0] * y3[0] + left3[1] * y3[1] + left3[2] * y3[2]
    outer3 = jnp.where(inner == 0, left3[0], jnp.where(inner == 1, left3[1], left3[2])) * right3
    outer1 = right1 * left1
    q1, q3 = jnp.maximum(1.0, sigma1 / CLIP), jnp.maximum(1.0, sigma3 / CLIP)
    for at, q, wa, wp in ((0, q1, wa1, wp1), (1, q3, wa3, wp3)):
        scaled = stage[at] / (LIP * q)
        high = scaled.astype(bf16).astype(f32)
        low = scaled - high
        top = high + pltpu.roll(high, 3, 0)
        if at == 0:
            bias = side[27:28, :]
            bias_high = bias.astype(bf16).astype(f32)
            top = jnp.where(rows == 38, bias_high, jnp.where(rows == 39, bias - bias_high, top))
        wa[0:80, :] = top.astype(bf16)
        wa[80:160, :] = (low + pltpu.roll(low, 3, 0)).astype(bf16)
        wp[...] = (high + pltpu.roll(low, 3, 0)).astype(bf16)
    cols[0] = to_column(0.5 * softplus(side[28:29, :]))
    cols[1] = to_column(side[29:30, :])
    cols[2] = to_column(0.5 * softplus(side[30:31, :]))
    return (q1, sigma1, outer1), (q3, sigma3, outer3)


def prepare_mid(mid, lefts, m_high, m_low, outer):
    right = jnp.sum(mid * lefts[1:2, :], axis=1, keepdims=True)
    right = right / jnp.sqrt(jnp.sum(right * right) + 1e-12)
    y = jnp.sum(mid * right, axis=0, keepdims=True)
    left = y / jnp.sqrt(jnp.sum(y * y) + 1e-12)
    sigma = jnp.sum(left * y)
    q = jnp.maximum(1.0, sigma / CLIP)
    scaled = mid / (LIP * q)
    high = scaled.astype(bf16)
    m_high[...] = high
    m_low[...] = (scaled - high.astype(f32)).astype(bf16)
    outer[0:8, :] = jnp.broadcast_to(left, (8, C))
    return q, sigma, right


def correction(raw_grad, weight, q, sigma):
    ratio = sigma / CLIP
    active = jnp.where(ratio > 1.0, 1.0, jnp.where(ratio == 1.0, 0.5, 0.0))
    return 1.0 / (LIP * q), -active * jnp.sum(raw_grad * weight) / (LIP * q * q * CLIP)


def color_column(values):
    row = lax.broadcasted_iota(jnp.int32, (8, 1), 0)
    return jnp.where(row == 0, values[0], jnp.where(row == 1, values[1], values[2]))


PARTS = PX // TILE


def tile_at(image, part):
    if isinstance(image, int):
        return slice(image * PX + part * TILE, image * PX + (part + 1) * TILE)
    return pl.ds(pl.multiple_of(image * PX + part * TILE, TILE), TILE)


def each_image(body):
    lax.fori_loop(0, 2, lambda b, c: (body(b), c)[1], 0)


MESH = pl.DeviceIdType.MESH
SZ, SP, SC, SD, SV, SN, SS, ST, SA, SB = range(10)


def scale_sizes(n):
    w = C // n
    fold = 128 // w
    return w, fold, 64 // fold


def pack(block, fold):
    rows = block.shape[0] // fold
    return jnp.concatenate([block[i * rows : (i + 1) * rows] for i in range(fold)], 1)


def unpack(block, fold):
    w = 128 // fold
    return jnp.concatenate([block[:, i * w : (i + 1) * w] for i in range(fold)], 0)


class Gather:
    def __init__(self, n, buf, sems):
        self.n, self.m, self.buf, self.sems = n, n // 2, buf, sems
        self.me = lax.axis_index("dp")
        self.chip, self.core = self.me // 2, self.me % 2
        self.pair = self.me + 1 - 2 * self.core

    def copy(self, slot, sem, target):
        return pltpu.make_async_remote_copy(
            src_ref=self.buf.at[slot],
            dst_ref=self.buf.at[slot],
            send_sem=self.sems.at[0, sem],
            recv_sem=self.sems.at[1, sem],
            device_id={"dp": target},
            device_id_type=MESH,
        )

    def peer(self, j):
        return lax.rem(self.chip + j, self.m) * 2 + self.core

    def start(self):
        for j in range(1, self.m):
            self.copy(self.me, j, self.peer(j)).start()
        self.copy(self.me, self.m, self.pair).start()

    def forward(self):
        for j in range(1, self.m):
            source = self.peer(j)
            self.copy(source, self.m - j, source).wait_recv()
            self.copy(source, self.m + j, self.pair).start()

    def finish(self):
        for j in range(self.m):
            self.copy(self.me, self.m + j, self.pair).wait_recv()
        for j in range(1, 2 * self.m):
            self.copy(self.me, j, self.pair).wait_send()


class Reduce:
    def __init__(self, n, source, from_pair, chipsum, from_chips, sems):
        self.n, self.m = n, n // 2
        self.source, self.from_pair, self.chipsum, self.from_chips, self.sems = source, from_pair, chipsum, from_chips, sems
        self.me = lax.axis_index("dp")
        self.chip, self.core = self.me // 2, self.me % 2
        self.pair = self.me + 1 - 2 * self.core

    def swap_copy(self, k):
        return pltpu.make_async_remote_copy(
            src_ref=self.source.at[2 * k + 1 - self.core], dst_ref=self.from_pair.at[k],
            send_sem=self.sems.at[0, k], recv_sem=self.sems.at[1, k],
            device_id={"dp": self.pair}, device_id_type=MESH)

    def chip_copy(self, slot, j, target):
        return pltpu.make_async_remote_copy(
            src_ref=self.chipsum.at[slot], dst_ref=self.from_chips.at[j],
            send_sem=self.sems.at[0, self.m + j], recv_sem=self.sems.at[1, self.m + j],
            device_id={"dp": target}, device_id_type=MESH)

    def start(self):
        for k in range(self.m):
            self.swap_copy(k).start()

    def forward(self):
        for k in range(self.m):
            self.swap_copy(k).wait_recv()
            self.chipsum[k] = self.source[2 * k + self.core] + self.from_pair[k]
        for j in range(1, self.m):
            to = lax.rem(self.chip + j, self.m)
            self.chip_copy(to, j, to * 2 + self.core).start()

    def finish(self):
        total = self.chipsum[self.chip]
        for j in range(1, self.m):
            self.chip_copy(self.chip, j, self.pair).wait_recv()
            total = total + self.from_chips[j]
        return total

    def drain(self):
        for k in range(self.m):
            self.swap_copy(k).wait_send()
        for j in range(1, self.m):
            self.chip_copy(self.chip, j, self.pair).wait_send()


class Across:
    def __init__(self, groups, sems):
        self.groups, self.sems, self.grp = groups, sems, lax.axis_index("grp")

    def copy(self, src, dst, j, target):
        return pltpu.make_async_remote_copy(
            src_ref=src, dst_ref=dst, send_sem=self.sems.at[0, j], recv_sem=self.sems.at[1, j],
            device_id={"grp": target}, device_id_type=MESH)

    def others(self):
        return [(j, lax.rem(self.grp + j, self.groups)) for j in range(1, self.groups)]


def barrier(n, groups):
    me, grp = lax.axis_index("dp"), lax.axis_index("grp")
    sem = pltpu.get_barrier_semaphore()
    m = n // 2
    chip, core = me // 2, me % 2
    for j in range(1, m):
        pl.semaphore_signal(sem, inc=1, device_id={"dp": lax.rem(chip + j, m) * 2 + core}, device_id_type=MESH)
    pl.semaphore_signal(sem, inc=1, device_id={"dp": me + 1 - 2 * core}, device_id_type=MESH)
    for j in range(1, groups):
        pl.semaphore_signal(sem, inc=1, device_id={"grp": lax.rem(grp + j, groups)}, device_id_type=MESH)
    pl.semaphore_wait(sem, m + groups - 1)


def match(counts, me, wanted_mine, wanted_theirs):
    zero = jnp.zeros((1, 128), f32)
    mine, my_rank = zero, zero
    for d in range(len(counts)):
        hit = jnp.where(counts[d] == wanted_mine, 1.0, 0.0)
        my_rank = my_rank + jnp.where(d < me, hit, zero)
        mine = mine + jnp.where(d == me, hit, zero)
    rank, masks = zero, []
    for d in range(len(counts)):
        hit = jnp.where(counts[d] == wanted_theirs, 1.0, 0.0)
        masks.append(jnp.where(rank == my_rank, hit * mine, zero))
        rank = rank + hit
    return masks


def adam(weight, gradient, first, second, rate):
    first = 0.9 * first + (1.0 - 0.9) * gradient
    second = 0.999 * second + (1.0 - 0.999) * gradient * gradient
    first_hat = first / (1.0 - 0.9**5.0)
    second_hat = second / (1.0 - 0.999**5.0)
    return weight - rate * (first_hat / (jnp.sqrt(second_hat) + 1e-8) + 0.01 * weight), first, second


def side_rate(w):
    return jnp.where(lax.broadcasted_iota(jnp.int32, (58, w), 0) >= 31, 0.004, 0.05)


def flip(tile):
    eye = lax.broadcasted_iota(jnp.int32, (8, 128), 0) == lax.broadcasted_iota(jnp.int32, (8, 128), 1)
    return lax.dot_general(tile, eye.astype(f32), (((0,), (0,)), ((), ())), precision=HIGH, preferred_element_type=f32)[0:8]


def spread_field(ref, base, small, at, b):
    for c in range(3):
        for k in range(8):
            small[at, b, c : c + 1, k * 128 : (k + 1) * 128] = ref[base + c, k : k + 1, :]


def fold_field(value, ref, base):
    for c in range(3):
        for k in range(8):
            ref[base + c, k : k + 1, :] = value[c : c + 1, k * 128 : (k + 1) * 128]


def main_kernel(n, groups, names, *refs):
    r = types.SimpleNamespace(**dict(zip(names, refs)))
    w, fold, side_rows = scale_sizes(n)
    m = n // 2
    me, grp = lax.axis_index("dp"), lax.axis_index("grp")
    counts, terms, tiny = r.counts, r.terms, r.tiny
    get_side = Gather(n, r.sides, r.sides_sem)
    get_third = Gather(n, r.thirds, r.thirds_sem)
    get_mid = Gather(n, r.mids, r.mids_sem)
    share = Gather(n, r.results, r.results_sem)
    r.sides[me] = pack(jnp.concatenate([r.side_w[:, 0, :], jnp.zeros((6, w), f32)], 0), fold)
    for at, ref in enumerate((r.images, r.probes, r.cots)):
        r.thirds[me, 3 * at : 3 * at + 3] = ref[6:9]
    lane = lax.broadcasted_iota(jnp.int32, (8, 128), 1)
    sub = lax.broadcasted_iota(jnp.int32, (8, 128), 0)
    own_count = jnp.broadcast_to(counts[0, 0].astype(f32), (1, 128))
    r.thirds[me, 9] = jnp.where(lane == 0, counts[0, 0].astype(f32), terms[0, 2].astype(f32))
    r.mids[me] = r.mid_w[...]
    barrier(n, groups)
    get_side.start()
    get_third.start()
    get_mid.start()
    small, side = r.small, r.side
    small[...] = jnp.zeros_like(small)
    for at, ref in ((SZ, r.images), (SP, r.probes), (SC, r.cots)):
        spread_field(ref, 0, small, at, 0)
    r.live[...] = jnp.where(terms[0, 0].astype(f32) > (sub % 4).astype(f32), 1.0, 0.0)
    get_side.forward()
    get_side.finish()
    for i in range(fold):
        side[i * side_rows : (i + 1) * side_rows, :] = jnp.concatenate(
            [r.sides[d][:, i * w : (i + 1) * w] for d in range(n)], 1)
    lefts = r.lefts
    side1, side3 = prepare_side(side, lefts, [r.out_left[0, k] for k in range(3)], r.stage,
                                r.wa1, r.wp1, r.wa3, r.wp3, r.cols)
    bias_col = color_column([tiny[k, 0, 0] for k in range(3)])
    shift_col = color_column([tiny[k, 0, 1] for k in range(3)])
    scale_col = jnp.exp(color_column([tiny[k, 0, 2] for k in range(3)]))
    slope_raw = color_column([tiny[k, 0, 3] for k in range(3)])
    slope0 = 0.5 * softplus(slope_raw)
    wa1, wp1, wa3, wp3 = r.wa1, r.wp1, r.wa3, r.wp3
    mh, ml = r.mh, r.ml
    slope1 = lambda: wide(r.cols.at[0], TILE)
    bias2 = lambda: wide(r.cols.at[1], TILE)
    slope2 = lambda: wide(r.cols.at[2], TILE)
    valid = lambda: lax.broadcasted_iota(jnp.int32, (8, PX), 0) < 3

    def alive(b, step):
        row = r.live[pl.ds(b * 4 + step, 1), :]
        return jnp.concatenate([row] * (PX // 128), 1)

    def doubled(index, part):
        block = r.field[index, :, part * TILE : (part + 1) * TILE]
        return jnp.concatenate([block, block], 0)

    def third_image():
        get_third.forward()
        get_third.finish()
        metas = [r.thirds[d, 9, 0:1, :] for d in range(n)]
        count_rows = [jnp.broadcast_to(meta[:, 0:1], (1, 128)) for meta in metas]
        masks = match(count_rows, me, 1.0, 3.0)
        helper, term = jnp.zeros((1, 128), f32), jnp.zeros((1, 128), f32) + terms[0, 1].astype(f32)
        for d in range(n):
            helper = helper + masks[d]
            term = jnp.where(masks[d] > 0.0, jnp.broadcast_to(metas[d][:, 1:2], (1, 128)), term)
        for at, ref in enumerate((r.images, r.probes, r.cots)):
            for c in range(3):
                picked = ref[3 + c]
                for d in range(n):
                    picked = jnp.where(masks[d] > 0.0, r.thirds[d, 3 * at + c], picked)
                r.picked[3 * at + c] = picked
        for at, place in ((0, SZ), (1, SP), (2, SC)):
            spread_field(r.picked, 3 * at, small, place, 1)
        r.live[...] = jnp.where(sub < 4, r.live[...], jnp.where(term > (sub % 4).astype(f32), 1.0, 0.0))

    def layer_one(b):
        pl.when(b == 1)(third_image)
        masks = tap_masks()
        field = (small[SZ, b] + shift_col) * scale_col
        p = small[SP, b]
        small[SZ, b] = field
        x, t, e = pieces(field, slope0)
        d0 = 1.0 + t + x * e
        small[SD, b] = d0
        r.field[b] = expand(field + field * t, False, 1.0, masks)
        r.field[2 + b] = expand(d0 * p, False, 0.0, masks)
        r.field[4 + b] = expand(small[SC, b], True, 0.0, masks)
        small[SV, b] = p
        small[SN, b] = -alive(b, 0) * p
        small[SS, b] = alive(b, 0) * p
        for part in range(PARTS):
            at = tile_at(b, part)
            h = dot_tn(wa1[...], doubled(b, part))
            x, t, e = pieces(h, slope1())
            d = 1.0 + t + x * e
            dh = dot_tn(wa1[...], doubled(2 + b, part))
            r.h1[:, at] = h
            r.g1[:, at] = dh
            r.d1[:, at] = d.astype(bf16)
            r.a1[:, at] = (h + h * t).astype(bf16)
            r.b1[:, at] = (d * dh).astype(bf16)

    each_image(layer_one)
    get_mid.forward()
    get_mid.finish()
    q2, sigma2, right2 = prepare_mid(r.mids[...].reshape(C, C), lefts, mh, ml, r.left2)

    def layer_two(b):
        masks = tap_masks()
        prods, dprods = [], []
        for part in range(PARTS):
            at = tile_at(b, part)
            a1 = r.a1[:, at]
            h = dot_tn(mh[...], a1) + dot_tn(ml[...], a1) + bias2()
            x, t, e = pieces(h, slope2())
            d = 1.0 + t + x * e
            dh = dot_tn(mh[...], r.b1[:, at])
            r.h2[:, at] = h
            r.g2[:, at] = dh
            r.d2[:, at] = d.astype(bf16)
            a2 = (h + h * t).astype(bf16)
            b2 = (d * dh).astype(bf16)
            r.a2[:, at] = a2
            r.b2[:, at] = b2
            prods.append(dot_nn(wp3[...], a2))
            dprods.append(dot_nn(wp3[...], b2))
        small[SA, b] = small[SZ, b] + collapse(jnp.concatenate(prods, 1), False, masks) + bias_col
        small[ST, b] = jnp.where(valid(), collapse(jnp.concatenate(dprods, 1), False, masks), 0.0)

    each_image(layer_two)
    fold_field(small[SA, 0], r.firsts, 0)
    fold_field(small[SA, 1], r.results.at[me], 0)

    def pull(step, sign):
        masks = tap_masks()
        for b in range(2):
            spread = expand(small[SV, b], True, 0.0, masks)
            prods = []
            for part in range(PARTS):
                at = tile_at(b, part)
                block = spread[:, part * TILE : (part + 1) * TILE]
                u2 = dot_tn(wa3[...], jnp.concatenate([block, block], 0)).astype(bf16) * r.d2[:, at]
                u1 = dot_nn(mh[...], u2).astype(bf16) * r.d1[:, at]
                prods.append(dot_nn(wp1[...], u1))
            v = jnp.where(valid(), small[SD, b] * collapse(jnp.concatenate(prods, 1), True, masks), 0.0)
            on = sign * alive(b, step + 1)
            small[SV, b] = v
            small[SN, b] = small[SN, b] - on * v
            small[SS, b] = small[SS, b] + (on / (step + 2).astype(f32)) * v
        return -sign

    lax.fori_loop(0, 3, pull, jnp.float32(-1.0))
    r.sums[...] = jnp.zeros_like(r.sums)

    def back_two(b):
        masks = tap_masks()
        r.field[6 + b] = expand(small[SN, b], True, 0.0, masks)
        slope_sum, bias_sum = r.sums[1], r.sums[0]
        for part in range(PARTS):
            at = tile_at(b, part)
            h = r.h2[:, at]
            sl = slope2()
            x, t, e = pieces(h, sl)
            d = 1.0 + t + x * e
            c_a = dot_tn(wa3[...], doubled(4 + b, part))
            t_a = dot_tn(wa3[...], doubled(6 + b, part))
            q = (2.0 * e * (1.0 - x * t)) * r.g2[:, at] * t_a
            c_h = d * c_a + sl * q
            grad = h * (c_a * h * e + q)
            for k in range(TILE // 128):
                slope_sum = slope_sum + grad[:, k * 128 : (k + 1) * 128]
                bias_sum = bias_sum + c_h[:, k * 128 : (k + 1) * 128]
            r.c2[:, at] = c_h.astype(bf16)
            r.t2[:, at] = (d * t_a).astype(bf16)
        r.sums[1] = slope_sum
        r.sums[0] = bias_sum

    each_image(back_two)
    raw = dot_nt(r.a1[...], r.c2[...]) + dot_nt(r.b1[...], r.t2[...])
    straight, across = correction(raw, r.mids[...].reshape(C, C), q2, sigma2)
    r.dmid[...] = (straight * raw + (across * right2) * r.left2[0:1, :]).reshape(n, w, C)
    sum_mid = Reduce(n, r.dmid, r.mid_pair, r.mid_chip, r.mid_chips, r.mid_sem)
    sum_mid.start()
    g3 = dot_nt(r.field[4], r.a2[:, 0:PX]) + dot_nt(r.field[6], r.b2[:, 0:PX])
    r.stage2[1] = g3 + dot_nt(r.field[5], r.a2[:, PX:]) + dot_nt(r.field[7], r.b2[:, PX:])

    def back_one(b):
        masks = tap_masks()
        slope_sum = r.sums[2]
        prods, dprods = [], []
        for part in range(PARTS):
            if part == 1:
                pl.when(b == 0)(sum_mid.forward)
            at = tile_at(b, part)
            h = r.h1[:, at]
            sl = slope1()
            x, t, e = pieces(h, sl)
            d = 1.0 + t + x * e
            c2 = r.c2[:, at]
            c_a = dot_nn(mh[...], c2) + dot_nn(ml[...], c2)
            t_a = dot_nn(mh[...], r.t2[:, at])
            q = (2.0 * e * (1.0 - x * t)) * r.g1[:, at] * t_a
            c_h = (d * c_a + sl * q).astype(bf16)
            t_h = (d * t_a).astype(bf16)
            grad = h * (c_a * h * e + q)
            for k in range(TILE // 128):
                slope_sum = slope_sum + grad[:, k * 128 : (k + 1) * 128]
            r.prod[0, :, part * TILE : (part + 1) * TILE] = dot_nn(wp1[...], c_h)
            r.prod[1, :, part * TILE : (part + 1) * TILE] = dot_nn(wp1[...], t_h)
            r.a2[:, at] = c_h
            r.b2[:, at] = t_h
            r.sums[2] = slope_sum
        small[SA, b] = collapse(r.prod[0], True, masks)
        small[SB, b] = collapse(r.prod[1], True, masks)

    each_image(back_one)
    g1 = dot_nt(r.field[0], r.a2[:, 0:PX]) + dot_nt(r.field[2], r.b2[:, 0:PX])
    g1 = g1 + dot_nt(r.field[1], r.a2[:, PX:]) + dot_nt(r.field[3], r.b2[:, PX:])
    ones = jnp.ones((8, 128), f32)
    row_of = lambda acc: lax.dot_general(
        ones, acc, (((1,), (1,)), ((), ())), precision=HIGH, preferred_element_type=f32)[0:1]
    dside = r.dside
    dside[27:28, :] = g1[38:39]
    dside[28:29, :] = row_of(r.sums[2]) * (0.5 * sigmoid(side[28:29, :]))
    dside[29:30, :] = row_of(r.sums[0])
    dside[30:31, :] = row_of(r.sums[1]) * (0.5 * sigmoid(side[30:31, :]))
    dside[58:64, :] = jnp.zeros((6, C), f32)
    row80 = lax.broadcasted_iota(jnp.int32, (80, C), 0)
    for at, (q, sigma, outer), grad, start in ((0, side1, g1, 0), (1, side3, r.stage2[1], 31)):
        joined = jnp.where((row80 % 8 < 3) & (row80 < 72), grad + pltpu.roll(grad, 77, 0), 0.0)
        straight, across = correction(joined, r.stage[at], q, sigma)
        r.stage2[at] = straight * joined + across * outer
        for color in range(3):
            for tap in range(9):
                to = start + 9 * color + tap
                dside[to : to + 1, :] = r.stage2[at, 8 * tap + color : 8 * tap + color + 1, :]
    for d in range(n):
        r.side_blocks[d] = pack(dside[:, d * w : (d + 1) * w], fold)
    sum_side = Reduce(n, r.side_blocks, r.side_pair, r.side_chip, r.side_chips, r.side_sem)
    sum_side.start()
    total_scale = tiny[0, 0, 2] + tiny[1, 0, 2] + tiny[2, 0, 2]
    tile = jnp.where(lane == 5, counts[0, 0].astype(f32), 0.0)
    for b in range(2):
        field, p, cot = small[SZ, b], small[SP, b], small[SC, b]
        c_a, t_a = small[SA, b], small[SB, b]
        x, t, e = pieces(field, slope0)
        q = 2.0 * e * (1.0 - x * t) * p * t_a
        c_z = jnp.where(valid(), cot + (1.0 + t + x * e) * c_a + slope0 * q, 0.0)
        slope_grad = jnp.where(valid(), field * (c_a * field * e + q), 0.0)
        fold_field(c_z * scale_col, r.firsts if b == 0 else r.results.at[me], 3)
        sums = [
            jnp.sum(cot, axis=1, keepdims=True),
            jnp.sum(c_z, axis=1, keepdims=True) * scale_col,
            jnp.sum(c_z * field, axis=1, keepdims=True) - 1024.0,
            jnp.sum(slope_grad, axis=1, keepdims=True) * (0.5 * sigmoid(slope_raw)),
        ]
        for k in range(4):
            tile = tile + jnp.where((lane == k) & (sub < 3), sums[k], 0.0)
        log_part = (1024.0 * total_scale + jnp.sum(small[SS, b] * small[ST, b])) / 3072.0
        tile = tile + jnp.where((lane == 4) & (sub == b), log_part, 0.0)
    r.results[me, 6] = tile
    share.start()
    mid_grad = sum_mid.finish() / (2.0 * n)
    r.mid_g[...] = mid_grad
    diff = r.mid_o[...] - adam(r.mid_w[...], mid_grad, r.mid_f[...], r.mid_s[...], 0.01)[0]
    chunk = C // groups
    for k in range(groups):
        r.mid_diff[k] = diff[:, k * chunk : (k + 1) * chunk]
    ring1, ring2 = Across(groups, r.ring1_sem), Across(groups, r.ring2_sem)
    ring3, ring4 = Across(groups, r.ring3_sem), Across(groups, r.ring4_sem)
    for j, to in ring1.others():
        ring1.copy(r.mid_diff.at[to], r.mid_parts.at[j], j, to).start()
    sum_side.forward()
    share.forward()
    total = r.mid_diff[grp]
    for j, to in ring1.others():
        ring1.copy(r.mid_diff.at[to], r.mid_parts.at[j], j, to).wait_recv()
        total = total + r.mid_parts[j]
    r.mid_sum[grp] = total
    for j, to in ring2.others():
        ring2.copy(r.mid_sum.at[grp], r.mid_sum.at[grp], j, to).start()
    side_grad = unpack(sum_side.finish(), fold)[0:58] / (2.0 * n)
    r.side_g[...] = side_grad
    new = adam(r.side_w[:, 0, :], side_grad, r.side_f[:, 0, :], r.side_s[:, 0, :], side_rate(w))[0]
    r.side_diff[grp] = pack(jnp.concatenate([r.side_o[...] - new, jnp.zeros((6, w), f32)], 0), fold)
    for j, to in ring3.others():
        ring3.copy(r.side_diff.at[grp], r.side_diff.at[grp], j, to).start()
    share.finish()
    tiny_sum = r.results[0, 6]
    for d in range(1, n):
        tiny_sum = tiny_sum + r.results[d, 6]
    r.out_small[0] = tiny_sum
    r.tiles[...] = jnp.zeros_like(r.tiles)
    for c in range(3):
        for k, ref in enumerate((r.tiny_w, r.tiny_f, r.tiny_s)):
            r.tiles[k, c : c + 1, 0:4] = ref[c, 0:1, :]
    r.tiles[3, 0:4, 0:3] = r.tiny_o[...]
    new = adam(r.tiles[0], tiny_sum / (2.0 * n), r.tiles[1], r.tiles[2], 0.05)[0]
    r.tiny_diff[grp] = r.tiles[3] - flip(jnp.where(lane < 4, new, 0.0))
    for j, to in ring4.others():
        ring4.copy(r.tiny_diff.at[grp], r.tiny_diff.at[grp], j, to).start()
    tiles = [r.results[d, 6] for d in range(n)]
    masks = match([jnp.broadcast_to(t[0:1, 5:6], (1, 128)) for t in tiles], me, 3.0, 1.0)
    log_third = jnp.zeros((1, 128), f32)
    for d in range(n):
        log_third = jnp.where(masks[d] > 0.0, jnp.broadcast_to(tiles[d][1:2, 4:5], (1, 128)), log_third)
    for k in range(6):
        out, c = (r.out_flow, k) if k < 3 else (r.out_back, k - 3)
        picked = jnp.zeros((8, 128), f32)
        for d in range(n):
            picked = jnp.where(masks[d] > 0.0, r.results[d, k], picked)
        out[c] = r.firsts[k]
        out[3 + c] = jnp.where(own_count > 1.5, r.results[me, k], 0.0)
        out[6 + c] = picked
    logs = [jnp.broadcast_to(tile[b : b + 1, 4:5], (1, 128)) for b in range(2)]
    logs[1] = jnp.where(own_count > 1.5, logs[1], 0.0)
    row_lane = lax.broadcasted_iota(jnp.int32, (1, 128), 1)
    r.out_small[1] = jnp.broadcast_to(
        jnp.where(row_lane == 0, logs[0], jnp.where(row_lane == 1, logs[1], log_third)), (8, 128))
    for j, to in ring3.others():
        ring3.copy(r.side_diff.at[grp], r.side_diff.at[grp], j, to).wait_recv()
    total = r.side_diff[0]
    for k in range(1, groups):
        total = total + r.side_diff[k]
    r.side_t[...] = unpack(total, fold)[0:58]
    for j, to in ring4.others():
        ring4.copy(r.tiny_diff.at[grp], r.tiny_diff.at[grp], j, to).wait_recv()
    total = r.tiny_diff[0]
    for k in range(1, groups):
        total = total + r.tiny_diff[k]
    r.out_small[2] = total
    for j, to in ring2.others():
        ring2.copy(r.mid_sum.at[grp], r.mid_sum.at[grp], j, to).wait_recv()
    for k in range(groups):
        r.mid_t[:, k * chunk : (k + 1) * chunk] = r.mid_sum[k]
    sum_mid.drain()
    sum_side.drain()
    for ring in (ring1, ring2):
        for j, to in ring.others():
            ring.copy(r.mid_sum.at[grp], r.mid_sum.at[grp], j, to).wait_send()
    for j, to in ring3.others():
        ring3.copy(r.side_diff.at[grp], r.side_diff.at[grp], j, to).wait_send()
    for j, to in ring4.others():
        ring4.copy(r.tiny_diff.at[grp], r.tiny_diff.at[grp], j, to).wait_send()


def last_kernel(n, groups, names, *refs):
    r = types.SimpleNamespace(**dict(zip(names, refs)))
    w = C // n
    lane = lax.broadcasted_iota(jnp.int32, (8, 128), 1)
    r.flow_o[...] = r.flow[...]
    r.back_o[...] = r.back[...]
    r.log_det[...] = r.small[1, 0:1, 0:3]
    tiny_sum = r.small[0]
    r.log_mean[...] = (tiny_sum[0:1, 4:5] + tiny_sum[1:2, 4:5]) / (2.0 * n)
    new, first, second = adam(r.mid_w[...], r.mid_g[...], r.mid_f[...], r.mid_s[...], 0.01)
    r.mid_f_new[...], r.mid_s_new[...], r.mid_new[...] = first, second, new
    new, first, second = adam(r.side_w[:, 0, :], r.side_g[...], r.side_f[:, 0, :], r.side_s[:, 0, :], side_rate(w))
    r.side_f_new[:, 0, :], r.side_s_new[:, 0, :], r.side_new[:, 0, :] = first, second, new
    r.tiles[...] = jnp.zeros_like(r.tiles)
    for c in range(3):
        for k, ref in enumerate((r.tiny_w, r.tiny_f, r.tiny_s)):
            r.tiles[k, c : c + 1, 0:4] = ref[c, 0:1, :]
    new, first, second = adam(r.tiles[0], tiny_sum / (2.0 * n), r.tiles[1], r.tiles[2], 0.05)
    for c in range(3):
        r.tiny_f_new[c, 0:1, :] = first[c : c + 1, 0:4]
        r.tiny_new[c, 0:1, :] = new[c : c + 1, 0:4]
    turned = flip(jnp.where(lane < 4, second, 0.0))
    for k in range(3):
        r.tiny_s_new[k, 0:1, :] = turned[k : k + 1, 0:3]
    r.slope_s_new[...] = turned[3:4, 0:3]

    def outer(diff, old, momentum, delta_out, momentum_out, out):
        delta = diff / groups
        mom = 0.9 * momentum[...] + delta
        delta_out[...], momentum_out[...] = delta, mom
        out[...] = old[...] - 0.7 * (delta + 0.9 * mom)

    outer(r.mid_t[...], r.mid_o, r.mid_m, r.mid_d, r.mid_m_new, r.mid_o_new)
    outer(r.side_t[...], r.side_o, r.side_m, r.side_d, r.side_m_new, r.side_o_new)
    outer(r.small[2, 0:4, 0:3], r.tiny_o, r.tiny_m, r.tiny_d, r.tiny_m_new, r.tiny_o_new)


def on_device(images, probes, out_cotangent, counts, terms, power_left, power_out, mid_weight, mid_first, mid_second,
              side_weight, side_first, side_second, tiny_weight, tiny_first, tiny_second,
              mid_outer, mid_momentum, side_outer, side_momentum, tiny_outer, tiny_momentum):
    n, groups = lax.axis_size("dp"), lax.axis_size("grp")
    w, fold, side_rows = scale_sizes(n)
    m = n // 2
    vm = pl.BlockSpec(memory_space=pltpu.VMEM)
    sm = pl.BlockSpec(memory_space=pltpu.SMEM)
    sd = lambda *shape: jax.ShapeDtypeStruct(shape, f32)
    dma = lambda *shape: pltpu.SemaphoreType.DMA(shape)
    vmem = lambda *shape: pltpu.VMEM(shape, f32)
    big = lambda dtype: pltpu.VMEM((C, 2 * PX), dtype)
    half = lambda *shape: pltpu.VMEM(shape, bf16)
    image = lambda x: x[0].reshape(9, 8, 128)
    turn = lambda x: jnp.swapaxes(x, -1, -2)
    row = lambda x: x[0][:, None, :]
    color = lambda x: jnp.transpose(x, (2, 0, 1))
    state = dict(
        mid_w=turn(mid_weight[0]), mid_f=turn(mid_first[0]), mid_s=turn(mid_second[0]), mid_o=turn(mid_outer),
        side_w=row(side_weight), side_f=row(side_first), side_s=row(side_second), side_o=side_outer,
        tiny_w=color(tiny_weight), tiny_f=color(tiny_first), tiny_s=color(tiny_second), tiny_o=tiny_outer,
    )
    vmem_in = dict(images=image(images), probes=image(probes), cots=image(out_cotangent), lefts=power_left[0], **state)
    smem_in = dict(counts=counts, terms=terms, out_left=power_out, tiny=color(tiny_weight))
    outs = dict(out_flow=sd(9, 8, 128), out_back=sd(9, 8, 128), out_small=sd(3, 8, 128), mid_g=sd(w, C), mid_t=sd(w, C),
                side_g=sd(58, w), side_t=sd(58, w))
    scratch = dict(
        stage=vmem(2, 80, C), stage2=vmem(2, 80, C), wa1=half(160, C), wp1=half(80, C), wa3=half(160, C), wp3=half(80, C),
        cols=vmem(3, C, 128), small=vmem(10, 2, 8, PX), sums=vmem(3, C, 128), field=half(8, 80, PX), prod=vmem(2, 80, PX),
        mh=half(C, C), ml=half(C, C), left2=vmem(8, C), live=vmem(8, 128), side=vmem(64, C),
        h1=big(f32), g1=big(f32), h2=big(f32), g2=big(f32),
        d1=big(bf16), a1=big(bf16), b1=big(bf16), d2=big(bf16), a2=big(bf16), b2=big(bf16), c2=big(bf16), t2=big(bf16),
        sides=vmem(n, side_rows, 128), thirds=vmem(n, 10, 8, 128), mids=vmem(n, w, C), results=vmem(n, 7, 8, 128),
        picked=vmem(9, 8, 128), firsts=vmem(6, 8, 128), dmid=vmem(n, w, C), dside=vmem(64, C),
        side_blocks=vmem(n, side_rows, 128),
        mid_pair=vmem(m, w, C), mid_chip=vmem(m, w, C), mid_chips=vmem(m, w, C),
        side_pair=vmem(m, side_rows, 128), side_chip=vmem(m, side_rows, 128), side_chips=vmem(m, side_rows, 128),
        mid_diff=vmem(groups, w, C // groups), mid_parts=vmem(groups, w, C // groups), mid_sum=vmem(groups, w, C // groups),
        side_diff=vmem(groups, side_rows, 128), tiny_diff=vmem(groups, 8, 128), tiles=vmem(4, 8, 128),
        sides_sem=dma(2, n), thirds_sem=dma(2, n), mids_sem=dma(2, n), results_sem=dma(2, n),
        mid_sem=dma(2, n), side_sem=dma(2, n),
        ring1_sem=dma(2, groups), ring2_sem=dma(2, groups), ring3_sem=dma(2, groups), ring4_sem=dma(2, groups),
    )
    ins = {**vmem_in, **smem_in}
    made = pl.pallas_call(
        functools.partial(main_kernel, n, groups, list(ins) + list(outs) + list(scratch)),
        in_specs=[vm] * len(vmem_in) + [sm] * len(smem_in),
        out_specs=[vm] * len(outs),
        out_shape=list(outs.values()),
        scratch_shapes=list(scratch.values()),
        compiler_params=pltpu.CompilerParams(vmem_limit_bytes=60 << 20, collective_id=0, has_side_effects=True),
    )(*ins.values())
    flow, back, small, mid_g, mid_t, side_g, side_t = made
    ins = dict(flow=flow, back=back, small=small, mid_g=mid_g, mid_t=mid_t, side_g=side_g, side_t=side_t, **state)
    ins.update(mid_m=turn(mid_momentum), side_m=side_momentum, tiny_m=tiny_momentum)
    scratch = dict(tiles=vmem(3, 8, 128))
    outs = dict(
        flow_o=sd(9, 8, 128), back_o=sd(9, 8, 128), log_det=sd(1, 3), log_mean=sd(1, 1),
        mid_f_new=sd(w, C), mid_s_new=sd(w, C), mid_new=sd(w, C),
        side_f_new=sd(58, 1, w), side_s_new=sd(58, 1, w), side_new=sd(58, 1, w),
        tiny_f_new=sd(3, 1, 4), tiny_s_new=sd(3, 1, 3), slope_s_new=sd(1, 3), tiny_new=sd(3, 1, 4),
        mid_d=sd(w, C), mid_m_new=sd(w, C), mid_o_new=sd(w, C),
        side_d=sd(58, w), side_m_new=sd(58, w), side_o_new=sd(58, w),
        tiny_d=sd(4, 3), tiny_m_new=sd(4, 3), tiny_o_new=sd(4, 3),
    )
    made = pl.pallas_call(
        functools.partial(last_kernel, n, groups, list(ins) + list(outs) + list(scratch)),
        in_specs=[vm] * len(ins),
        out_specs=[vm] * len(outs),
        out_shape=list(outs.values()),
        scratch_shapes=list(scratch.values()),
        compiler_params=pltpu.CompilerParams(vmem_limit_bytes=32 << 20),
    )(*ins.values())
    o = types.SimpleNamespace(**dict(zip(outs, made)))
    whole = lambda x: x.reshape(1, 3, 3, PX)
    back_turn = lambda x: turn(x)[None]
    return (
        whole(o.flow_o), whole(o.back_o), o.log_det, o.log_mean.reshape(1),
        back_turn(o.mid_f_new), back_turn(o.mid_s_new), back_turn(o.mid_new),
        o.side_f_new[:, 0][None], o.side_s_new[:, 0][None], o.side_new[:, 0][None],
        jnp.transpose(o.tiny_f_new, (1, 2, 0)), jnp.transpose(o.tiny_s_new, (1, 0, 2)), o.slope_s_new, jnp.transpose(o.tiny_new, (1, 2, 0)),
        turn(o.mid_d), turn(o.mid_m_new), turn(o.mid_o_new),
        o.side_d, o.side_m_new, o.side_o_new, o.tiny_d, o.tiny_m_new, o.tiny_o_new,
    )


def solution(mesh):
    split = P("grp", None, "dp")
    group = P("grp", None, None)
    image = P("grp", "dp", None, None)
    return jax.shard_map(
        on_device,
        mesh=mesh,
        in_specs=(image, image, image, P("grp", "dp"), P("grp", "dp"), group, P("grp", None),
                  split, split, split, split, split, split, group, group, group,
                  P(None, "dp"), P(None, "dp"), P(None, "dp"), P(None, "dp"), P(), P()),
        out_specs=(image, image, P("grp", "dp"), P("grp"), split, split, split, split, split, split,
                   group, group, P("grp", None), group) + (P(None, "dp"),) * 6 + (P(), P(), P()),
        check_vma=False,
    )
```

```python
import functools
import types

import jax, jax.numpy as jnp
from jax import lax
from jax.experimental import pallas as pl
from jax.experimental.pallas import tpu as pltpu
from jax.sharding import PartitionSpec as P

bf16, f32 = jnp.bfloat16, jnp.float32
HIGH = lax.Precision.HIGHEST
C, PX, TILE = 512, 1024, 512
CLIP = 0.98
LIP = 2.2


def dot_nn(a, b):
    return jnp.dot(a, b, preferred_element_type=f32)


def dot_tn(a, b):
    return lax.dot_general(a, b, (((0,), (0,)), ((), ())), preferred_element_type=f32)


def dot_nt(a, b):
    return lax.dot_general(a, b, (((1,), (1,)), ((), ())), preferred_element_type=f32)


def tap_masks():
    lane = lax.broadcasted_iota(jnp.int32, (8, PX), 1)
    row, col = lane // 32, lane % 32
    masks = []
    for tap in range(9):
        down, right = tap // 3 - 1, tap % 3 - 1
        ok = (row + down >= 0) & (row + down < 32) & (col + right >= 0) & (col + right < 32)
        masks.append(ok)
    return masks


def shift(field, tap, masks):
    if tap == 4:
        return field
    offset = (tap // 3 - 1) * 32 + tap % 3 - 1
    return jnp.where(masks[tap], pltpu.roll(field, (-offset) % PX, 1), 0.0)


def expand(field, flip, one, masks):
    high = field.astype(bf16).astype(f32)
    low = field - high
    row = lax.broadcasted_iota(jnp.int32, (8, PX), 0)
    base = jnp.where(row < 3, high, jnp.where(row < 6, pltpu.roll(low, 3, 0), one))
    parts = [shift(base, 8 - tap if flip else tap, masks) for tap in range(9)]
    return jnp.concatenate(parts + [jnp.zeros((8, PX), f32)], 0).astype(bf16)


def collapse(prod, flip, masks):
    total = prod[32:40]
    for tap in (0, 1, 2, 3, 5, 6, 7, 8):
        total = total + shift(prod[8 * tap : 8 * tap + 8], 8 - tap if flip else tap, masks)
    return total + pltpu.roll(total, 5, 0)


def pieces(h, slope_half):
    x = slope_half * h
    t = jnp.tanh(x)
    e = 1.0 - t * t
    return x, t, e


def softplus(raw):
    return jnp.maximum(raw, 0.0) + jnp.log1p(jnp.exp(-jnp.abs(raw)))


def sigmoid(raw):
    return 1.0 / (1.0 + jnp.exp(-raw))


def wide(ref, width):
    block = ref[...]
    return jnp.concatenate([block] * (width // 128), 1)


def to_column(row):
    return jnp.transpose(jnp.broadcast_to(row, (128, C)))


def prepare_side(side, lefts, out_left, stage, wa1, wp1, wa3, wp3, cols):
    rows = lax.broadcasted_iota(jnp.int32, (80, C), 0)
    stage[...] = jnp.zeros_like(stage)
    for color in range(3):
        for tap in range(9):
            stage[0, 8 * tap + color : 8 * tap + color + 1, :] = side[9 * color + tap : 9 * color + tap + 1, :]
            at = 31 + 9 * color + tap
            stage[1, 8 * tap + color : 8 * tap + color + 1, :] = side[at : at + 1, :]
    first = stage[0]
    u = lefts[0:1, :]
    right1 = jnp.sum(first * u, axis=1, keepdims=True)
    right1 = right1 / jnp.sqrt(jnp.sum(right1 * right1) + 1e-12)
    y1 = jnp.sum(first * right1, axis=0, keepdims=True)
    left1 = y1 / jnp.sqrt(jnp.sum(y1 * y1) + 1e-12)
    sigma1 = jnp.sum(left1 * y1)
    last = stage[1]
    inner = rows % 8
    weight = jnp.where(inner == 0, out_left[0], jnp.where(inner == 1, out_left[1], out_left[2]))
    mixed = jnp.where(inner < 3, last * weight, 0.0)
    right3 = mixed + pltpu.roll(mixed, 79, 0) + pltpu.roll(mixed, 78, 0)
    right3 = jnp.where(inner == 0, right3, 0.0)
    right3 = right3 / jnp.sqrt(jnp.sum(right3 * right3) + 1e-12)
    right3 = right3 + pltpu.roll(right3, 1, 0) + pltpu.roll(right3, 2, 0)
    prod = last * right3
    y3 = [jnp.sum(jnp.where(inner == k, prod, 0.0)) for k in range(3)]
    norm3 = jnp.sqrt(y3[0] * y3[0] + y3[1] * y3[1] + y3[2] * y3[2] + 1e-12)
    left3 = [value / norm3 for value in y3]
    sigma3 = left3[0] * y3[0] + left3[1] * y3[1] + left3[2] * y3[2]
    outer3 = jnp.where(inner == 0, left3[0], jnp.where(inner == 1, left3[1], left3[2])) * right3
    outer1 = right1 * left1
    q1, q3 = jnp.maximum(1.0, sigma1 / CLIP), jnp.maximum(1.0, sigma3 / CLIP)
    for at, q, wa, wp in ((0, q1, wa1, wp1), (1, q3, wa3, wp3)):
        scaled = stage[at] / (LIP * q)
        high = scaled.astype(bf16).astype(f32)
        low = scaled - high
        top = high + pltpu.roll(high, 3, 0)
        if at == 0:
            bias = side[27:28, :]
            bias_high = bias.astype(bf16).astype(f32)
            top = jnp.where(rows == 38, bias_high, jnp.where(rows == 39, bias - bias_high, top))
        wa[0:80, :] = top.astype(bf16)
        wa[80:160, :] = (low + pltpu.roll(low, 3, 0)).astype(bf16)
        wp[...] = (high + pltpu.roll(low, 3, 0)).astype(bf16)
    cols[0] = to_column(0.5 * softplus(side[28:29, :]))
    cols[1] = to_column(side[29:30, :])
    cols[2] = to_column(0.5 * softplus(side[30:31, :]))
    return (q1, sigma1, outer1), (q3, sigma3, outer3)


def prepare_mid(mid, lefts, m_high, m_low, outer):
    right = jnp.sum(mid * lefts[1:2, :], axis=1, keepdims=True)
    right = right / jnp.sqrt(jnp.sum(right * right) + 1e-12)
    y = jnp.sum(mid * right, axis=0, keepdims=True)
    left = y / jnp.sqrt(jnp.sum(y * y) + 1e-12)
    sigma = jnp.sum(left * y)
    q = jnp.maximum(1.0, sigma / CLIP)
    scaled = mid / (LIP * q)
    high = scaled.astype(bf16)
    m_high[...] = high
    m_low[...] = (scaled - high.astype(f32)).astype(bf16)
    outer[0:8, :] = jnp.broadcast_to(left, (8, C))
    return q, sigma, right


def correction(raw_grad, weight, q, sigma):
    ratio = sigma / CLIP
    active = jnp.where(ratio > 1.0, 1.0, jnp.where(ratio == 1.0, 0.5, 0.0))
    return 1.0 / (LIP * q), -active * jnp.sum(raw_grad * weight) / (LIP * q * q * CLIP)


def color_column(values):
    row = lax.broadcasted_iota(jnp.int32, (8, 1), 0)
    return jnp.where(row == 0, values[0], jnp.where(row == 1, values[1], values[2]))


PARTS = PX // TILE
RC = 32
AT = [slice(k * TILE, (k + 1) * TILE) for k in range(2 * PARTS)]
IM = (slice(0, PX), slice(PX, 2 * PX))
CHUNKS = [slice(k, k + RC) for k in range(0, C, RC)]


def pipeline(parts, dots, elem, after=None):
    held = dots(parts[0])
    for i, k in enumerate(parts):
        ahead = dots(parts[i + 1]) if i + 1 < len(parts) else None
        elem(k, *held)
        if after is not None and i >= 1:
            after(parts[i - 1])
        held = ahead
    if after is not None:
        after(parts[-1])


MESH = pl.DeviceIdType.MESH
SZ, SP, SC, SD, SV, SN, SS, ST, SA, SB = range(10)


def scale_sizes(n):
    w = C // n
    fold = 128 // w
    return w, fold, 64 // fold


def pack(block, fold):
    rows = block.shape[0] // fold
    return jnp.concatenate([block[i * rows : (i + 1) * rows] for i in range(fold)], 1)


def unpack(block, fold):
    w = 128 // fold
    return jnp.concatenate([block[:, i * w : (i + 1) * w] for i in range(fold)], 0)


class Gather:
    def __init__(self, n, buf, sems):
        self.n, self.m, self.buf, self.sems = n, n // 2, buf, sems
        self.me = lax.axis_index("dp")
        self.chip, self.core = self.me // 2, self.me % 2
        self.pair = self.me + 1 - 2 * self.core

    def copy(self, slot, sem, target):
        return pltpu.make_async_remote_copy(
            src_ref=self.buf.at[slot],
            dst_ref=self.buf.at[slot],
            send_sem=self.sems.at[0, sem],
            recv_sem=self.sems.at[1, sem],
            device_id={"dp": target},
            device_id_type=MESH,
        )

    def peer(self, j):
        return lax.rem(self.chip + j, self.m) * 2 + self.core

    def start(self):
        for j in range(1, self.m):
            self.copy(self.me, j, self.peer(j)).start()
        self.copy(self.me, self.m, self.pair).start()

    def forward(self):
        for j in range(1, self.m):
            source = self.peer(j)
            self.copy(source, self.m - j, source).wait_recv()
            self.copy(source, self.m + j, self.pair).start()

    def finish(self):
        for j in range(self.m):
            self.copy(self.me, self.m + j, self.pair).wait_recv()
        for j in range(1, 2 * self.m):
            self.copy(self.me, j, self.pair).wait_send()


class Reduce:
    def __init__(self, n, source, from_pair, chipsum, from_chips, sems):
        self.n, self.m = n, n // 2
        self.source, self.from_pair, self.chipsum, self.from_chips, self.sems = source, from_pair, chipsum, from_chips, sems
        self.me = lax.axis_index("dp")
        self.chip, self.core = self.me // 2, self.me % 2
        self.pair = self.me + 1 - 2 * self.core

    def swap_copy(self, k, sem):
        return pltpu.make_async_remote_copy(
            src_ref=self.source.at[2 * k + 1 - self.core], dst_ref=self.from_pair.at[k],
            send_sem=self.sems.at[0, sem], recv_sem=self.sems.at[1, sem],
            device_id={"dp": self.pair}, device_id_type=MESH)

    def chip_copy(self, slot, j, target):
        return pltpu.make_async_remote_copy(
            src_ref=self.chipsum.at[slot], dst_ref=self.from_chips.at[j],
            send_sem=self.sems.at[0, self.m + j], recv_sem=self.sems.at[1, self.m + j],
            device_id={"dp": target}, device_id_type=MESH)

    def start(self):
        for j in range(1, self.m + 1):
            self.swap_copy(lax.rem(self.chip + j, self.m), j % self.m).start()

    def forward(self):
        for j in range(1, self.m + 1):
            to = lax.rem(self.chip + j, self.m)
            self.swap_copy(to, j % self.m).wait_recv()
            self.chipsum[to] = self.source[2 * to + self.core] + self.from_pair[to]
            if j < self.m:
                self.chip_copy(to, j, to * 2 + self.core).start()

    def finish(self):
        total = self.chipsum[self.chip]
        for j in range(1, self.m):
            self.chip_copy(self.chip, j, self.pair).wait_recv()
            total = total + self.from_chips[j]
        return total

    def drain(self):
        for k in range(self.m):
            self.swap_copy(k, k).wait_send()
        for j in range(1, self.m):
            self.chip_copy(self.chip, j, self.pair).wait_send()


class Across:
    def __init__(self, groups, sems):
        self.groups, self.sems, self.grp = groups, sems, lax.axis_index("grp")

    def copy(self, src, dst, j, target):
        return pltpu.make_async_remote_copy(
            src_ref=src, dst_ref=dst, send_sem=self.sems.at[0, j], recv_sem=self.sems.at[1, j],
            device_id={"grp": target}, device_id_type=MESH)

    def others(self):
        return [(j, lax.rem(self.grp + j, self.groups)) for j in range(1, self.groups)]


def barrier(n, groups):
    me, grp = lax.axis_index("dp"), lax.axis_index("grp")
    sem = pltpu.get_barrier_semaphore()
    m = n // 2
    chip, core = me // 2, me % 2
    for j in range(1, m):
        pl.semaphore_signal(sem, inc=1, device_id={"dp": lax.rem(chip + j, m) * 2 + core}, device_id_type=MESH)
    pl.semaphore_signal(sem, inc=1, device_id={"dp": me + 1 - 2 * core}, device_id_type=MESH)
    for j in range(1, groups):
        pl.semaphore_signal(sem, inc=1, device_id={"grp": lax.rem(grp + j, groups)}, device_id_type=MESH)
    pl.semaphore_wait(sem, m + groups - 1)


def match(counts, me, wanted_mine, wanted_theirs):
    zero = jnp.zeros((1, 128), f32)
    mine, my_rank = zero, zero
    for d in range(len(counts)):
        hit = jnp.where(counts[d] == wanted_mine, 1.0, 0.0)
        my_rank = my_rank + jnp.where(d < me, hit, zero)
        mine = mine + jnp.where(d == me, hit, zero)
    rank, masks = zero, []
    for d in range(len(counts)):
        hit = jnp.where(counts[d] == wanted_theirs, 1.0, 0.0)
        masks.append(jnp.where(rank == my_rank, hit * mine, zero))
        rank = rank + hit
    return masks


def adam(weight, gradient, first, second, rate):
    first = 0.9 * first + (1.0 - 0.9) * gradient
    second = 0.999 * second + (1.0 - 0.999) * gradient * gradient
    first_hat = first / (1.0 - 0.9**5.0)
    second_hat = second / (1.0 - 0.999**5.0)
    return weight - rate * (first_hat / (jnp.sqrt(second_hat) + 1e-8) + 0.01 * weight), first, second


def side_rate(w):
    return jnp.where(lax.broadcasted_iota(jnp.int32, (58, w), 0) >= 31, 0.004, 0.05)


def flip(tile):
    eye = lax.broadcasted_iota(jnp.int32, (8, 128), 0) == lax.broadcasted_iota(jnp.int32, (8, 128), 1)
    return lax.dot_general(tile, eye.astype(f32), (((0,), (0,)), ((), ())), precision=HIGH, preferred_element_type=f32)[0:8]


def spread_field(ref, base, small, at, b):
    for c in range(3):
        for k in range(8):
            small[at, b, c : c + 1, k * 128 : (k + 1) * 128] = ref[base + c, k : k + 1, :]


def fold_field(value, ref, base):
    for c in range(3):
        for k in range(8):
            ref[base + c, k : k + 1, :] = value[c : c + 1, k * 128 : (k + 1) * 128]


def main_kernel(n, groups, names, *refs):
    r = types.SimpleNamespace(**dict(zip(names, refs)))
    w, fold, side_rows = scale_sizes(n)
    m = n // 2
    me, grp = lax.axis_index("dp"), lax.axis_index("grp")
    counts, terms, tiny = r.counts, r.terms, r.tiny
    get_side = Gather(n, r.sides, r.sides_sem)
    get_third = Gather(n, r.thirds, r.thirds_sem)
    get_mid = Gather(n, r.mids, r.mids_sem)
    share = Gather(n, r.results, r.results_sem)
    r.sides[me] = pack(jnp.concatenate([r.side_w[:, 0, :], jnp.zeros((6, w), f32)], 0), fold)
    for at, ref in enumerate((r.images, r.probes, r.cots)):
        r.thirds[me, 3 * at : 3 * at + 3] = ref[6:9]
    lane = lax.broadcasted_iota(jnp.int32, (8, 128), 1)
    sub = lax.broadcasted_iota(jnp.int32, (8, 128), 0)
    own_count = jnp.broadcast_to(counts[0, 0].astype(f32), (1, 128))
    r.thirds[me, 9] = jnp.where(lane == 0, counts[0, 0].astype(f32), terms[0, 2].astype(f32))
    r.mids[me] = r.mid_w[...]
    barrier(n, groups)
    get_side.start()
    get_third.start()
    get_mid.start()
    small, side = r.small, r.side
    small[...] = jnp.zeros_like(small)
    for at, ref in ((SZ, r.images), (SP, r.probes), (SC, r.cots)):
        spread_field(ref, 0, small, at, 0)
    r.live[...] = jnp.where(terms[0, 0].astype(f32) > (sub % 4).astype(f32), 1.0, 0.0)
    bias_col = color_column([tiny[k, 0, 0] for k in range(3)])
    shift_col = color_column([tiny[k, 0, 1] for k in range(3)])
    scale_col = jnp.exp(color_column([tiny[k, 0, 2] for k in range(3)]))
    slope_raw = color_column([tiny[k, 0, 3] for k in range(3)])
    slope0 = 0.5 * softplus(slope_raw)

    def alive(b, step):
        return jnp.concatenate([r.live[b * 4 + step : b * 4 + step + 1, :]] * (PX // 128), 1)

    def prepare_image(b):
        masks = tap_masks()
        field = (small[SZ, b] + shift_col) * scale_col
        p = small[SP, b]
        small[SZ, b] = field
        x, t, e = pieces(field, slope0)
        d0 = 1.0 + t + x * e
        small[SD, b] = d0
        r.field[b] = expand(field + field * t, False, 1.0, masks)
        r.field[2 + b] = expand(d0 * p, False, 0.0, masks)
        r.field[4 + b] = expand(small[SC, b], True, 0.0, masks)
        r.field[6 + b] = expand(p, True, 0.0, masks)
        small[SV, b] = p
        small[SN, b] = -alive(b, 0) * p
        small[SS, b] = alive(b, 0) * p

    prepare_image(0)
    get_side.forward()
    get_side.finish()
    for i in range(fold):
        side[i * side_rows : (i + 1) * side_rows, :] = jnp.concatenate(
            [r.sides[d][:, i * w : (i + 1) * w] for d in range(n)], 1)
    lefts = r.lefts
    side1, side3 = prepare_side(side, lefts, [r.out_left[0, k] for k in range(3)], r.stage,
                                r.wa1, r.wp1, r.wa3, r.wp3, r.cols)
    wa1, wp1, wa3, wp3 = r.wa1, r.wp1, r.wa3, r.wp3
    mh, ml = r.mh, r.ml
    valid = lambda: lax.broadcasted_iota(jnp.int32, (8, PX), 0) < 3

    stages = []

    def stage(body):
        stages.append(body)
        pl.when(me + len(stages) > 0)(body)

    def doubled(index, k):
        block = r.field[index + k // PARTS, :, (k % PARTS) * TILE : (k % PARTS + 1) * TILE]
        return jnp.concatenate([block, block], 0)

    def column(which, rs):
        return jnp.concatenate([r.cols[which, rs]] * (TILE // 128), 1)

    one = (r.h1, r.g1, r.d1)
    two = (r.h2, r.g2, r.d2)

    def forward(kept, slope, bias, act, dact, k, h_all, dh_all):
        at = AT[k]
        hs, ys, ds = kept
        for rs in CHUNKS:
            h, dh = h_all[rs], dh_all[rs]
            if bias is not None:
                h = h + column(bias, rs)
            x = column(slope, rs) * h
            t = jnp.tanh(x)
            e = 1.0 - t * t
            d = 1.0 + t + x * e
            hs[rs, at] = h
            ds[rs, at] = d
            ys[rs, at] = e * (1.0 - x * t) * dh
            act[rs, at] = (h + h * t).astype(bf16)
            dact[rs, at] = (d * dh).astype(bf16)

    def backward(kept, slope, slope_to, bias_to, c_to, t_to, k, ca_all, ta_all):
        at = AT[k]
        hs, ys, ds = kept
        for rs in CHUNKS:
            h, d, c_a, t_a = hs[rs, at], ds[rs, at], ca_all[rs], ta_all[rs]
            sl = column(slope, rs)
            t = jnp.tanh(sl * h)
            he = h * (0.5 - 0.5 * (t * t))
            q = ys[rs, at] * t_a
            c_h = d * c_a + (sl + sl) * q
            grad = h * (c_a * he + q)
            gs, cs = grad[:, 0:128], c_h[:, 0:128]
            for j in range(1, TILE // 128):
                gs = gs + grad[:, j * 128 : (j + 1) * 128]
                if bias_to is not None:
                    cs = cs + c_h[:, j * 128 : (j + 1) * 128]
            r.sums[slope_to, rs] += gs
            if bias_to is not None:
                r.sums[bias_to, rs] += cs
            c_to[rs, at] = c_h.astype(bf16)
            t_to[rs, at] = (d * t_a).astype(bf16)

    def third_image():
        get_third.forward()
        get_third.finish()
        metas = [r.thirds[d, 9, 0:1, :] for d in range(n)]
        count_rows = [jnp.broadcast_to(meta[:, 0:1], (1, 128)) for meta in metas]
        masks = match(count_rows, me, 1.0, 3.0)
        helper, term = jnp.zeros((1, 128), f32), jnp.zeros((1, 128), f32) + terms[0, 1].astype(f32)
        for d in range(n):
            helper = helper + masks[d]
            term = jnp.where(masks[d] > 0.0, jnp.broadcast_to(metas[d][:, 1:2], (1, 128)), term)
        for at, ref in enumerate((r.images, r.probes, r.cots)):
            for c in range(3):
                picked = ref[3 + c]
                for d in range(n):
                    picked = jnp.where(masks[d] > 0.0, r.thirds[d, 3 * at + c], picked)
                r.picked[3 * at + c] = picked
        for at, place in ((0, SZ), (1, SP), (2, SC)):
            spread_field(r.picked, 3 * at, small, place, 1)
        r.live[...] = jnp.where(sub < 4, r.live[...], jnp.where(term > (sub % 4).astype(f32), 1.0, 0.0))

    def layer_one(b):
        @stage
        def _():
            pipeline([PARTS * b + k for k in range(PARTS)],
                     lambda k: (dot_tn(wa1[...], doubled(0, k)), dot_tn(wa1[...], doubled(2, k))),
                     functools.partial(forward, one, 0, None, r.a1, r.b1))
            for k in range(PARTS * b, PARTS * b + PARTS):
                r.ca[:, AT[k]] = dot_tn(wa3[...], doubled(4, k))
                r.c2[:, AT[k]] = dot_tn(wa3[...], doubled(6, k)).astype(bf16)

    layer_one(0)
    third_image()
    prepare_image(1)
    layer_one(1)
    get_mid.forward()
    get_mid.finish()
    q2, sigma2, right2 = prepare_mid(r.mids[...].reshape(C, C), lefts, mh, ml, r.left2)
    r.sums[...] = jnp.zeros_like(r.sums)

    @stage
    def layer_two():
        masks = tap_masks()

        def dots(k):
            a1 = r.a1[:, AT[k]]
            return dot_tn(mh[...], a1) + dot_tn(ml[...], a1), dot_tn(mh[...], r.b1[:, AT[k]])

        def after(k):
            to = slice((k % PARTS) * TILE, (k % PARTS + 1) * TILE)
            r.prod[0, :, to] = dot_nn(wp3[...], r.a2[:, AT[k]])
            r.prod[1, :, to] = dot_nn(wp3[...], r.b2[:, AT[k]])
            if k % PARTS == PARTS - 1:
                b = k // PARTS
                flow = small[SZ, b] + collapse(r.prod[0], False, masks) + bias_col
                fold_field(flow, r.firsts if b == 0 else r.results.at[me], 0)
                small[ST, b] = jnp.where(valid(), collapse(r.prod[1], False, masks), 0.0)

        pipeline(range(2 * PARTS), dots, functools.partial(forward, two, 2, 1, r.a2, r.b2), after)

    def pull(step):
        masks = tap_masks()
        for b in range(2):
            if step == 1:
                r.c2[:, IM[b]] = (r.c2[:, IM[b]].astype(f32) * r.d2[:, IM[b]]).astype(bf16)
            else:
                spread = expand(small[SV, b], True, 0.0, masks)
                wide_v = jnp.concatenate([spread, spread], 0)
                r.c2[:, IM[b]] = (dot_tn(wa3[...], wide_v) * r.d2[:, IM[b]]).astype(bf16)
        for b in range(2):
            r.t2[:, IM[b]] = (dot_nn(mh[...], r.c2[:, IM[b]]) * r.d1[:, IM[b]]).astype(bf16)
        sign = (-1.0) ** step
        for b in range(2):
            prod = dot_nn(wp1[...], r.t2[:, IM[b]])
            v = jnp.where(valid(), small[SD, b] * collapse(prod, True, masks), 0.0)
            small[SV, b] = v
            on = sign * alive(b, step)
            small[SN, b] = small[SN, b] - on * v
            small[SS, b] = small[SS, b] + (on / (step + 1.0)) * v

    for step in (1, 2, 3):
        stage(functools.partial(pull, step))

    @stage
    def back_two():
        masks = tap_masks()
        for b in range(2):
            r.field[6 + b] = expand(small[SN, b], True, 0.0, masks)
        pipeline(range(2 * PARTS), lambda k: (r.ca[:, AT[k]], dot_tn(wa3[...], doubled(6, k))),
                 functools.partial(backward, two, 2, 1, 0, r.c2, r.t2))

    raw = dot_nt(r.a1[...], r.c2[...]) + dot_nt(r.b1[...], r.t2[...])
    straight, across = correction(raw, r.mids[...].reshape(C, C), q2, sigma2)
    r.dmid[...] = (straight * raw + (across * right2) * r.left2[0:1, :]).reshape(n, w, C)
    sum_mid = Reduce(n, r.dmid, r.mid_pair, r.mid_chip, r.mid_chips, r.mid_sem)
    sum_mid.start()
    g3 = dot_nt(r.field[4], r.a2[:, 0:PX]) + dot_nt(r.field[6], r.b2[:, 0:PX])
    r.stage2[1] = g3 + dot_nt(r.field[5], r.a2[:, PX:]) + dot_nt(r.field[7], r.b2[:, PX:])
    sum_mid.forward()

    @stage
    def back_one():
        masks = tap_masks()

        def dots(k):
            c2 = r.c2[:, AT[k]]
            return dot_nn(mh[...], c2) + dot_nn(ml[...], c2), dot_nn(mh[...], r.t2[:, AT[k]])

        def after(k):
            to = slice((k % PARTS) * TILE, (k % PARTS + 1) * TILE)
            r.prod[0, :, to] = dot_nn(wp1[...], r.a2[:, AT[k]])
            r.prod[1, :, to] = dot_nn(wp1[...], r.b2[:, AT[k]])
            if k % PARTS == PARTS - 1:
                small[SA, k // PARTS] = collapse(r.prod[0], True, masks)
                small[SB, k // PARTS] = collapse(r.prod[1], True, masks)

        pipeline(range(2 * PARTS), dots, functools.partial(backward, one, 0, 2, None, r.a2, r.b2), after)

    g1 = dot_nt(r.field[0], r.a2[:, 0:PX]) + dot_nt(r.field[2], r.b2[:, 0:PX])
    g1 = g1 + dot_nt(r.field[1], r.a2[:, PX:]) + dot_nt(r.field[3], r.b2[:, PX:])
    ones = jnp.ones((8, 128), f32)
    row_of = lambda acc: lax.dot_general(
        ones, acc, (((1,), (1,)), ((), ())), precision=HIGH, preferred_element_type=f32)[0:1]
    dside = r.dside
    dside[27:28, :] = g1[38:39]
    dside[28:29, :] = row_of(r.sums[2]) * (sigmoid(side[28:29, :]))
    dside[29:30, :] = row_of(r.sums[0])
    dside[30:31, :] = row_of(r.sums[1]) * (sigmoid(side[30:31, :]))
    dside[58:64, :] = jnp.zeros((6, C), f32)
    row80 = lax.broadcasted_iota(jnp.int32, (80, C), 0)
    for at, (q, sigma, outer), grad, start in ((0, side1, g1, 0), (1, side3, r.stage2[1], 31)):
        joined = jnp.where((row80 % 8 < 3) & (row80 < 72), grad + pltpu.roll(grad, 77, 0), 0.0)
        straight, across = correction(joined, r.stage[at], q, sigma)
        r.stage2[at] = straight * joined + across * outer
        for color in range(3):
            for tap in range(9):
                to = start + 9 * color + tap
                dside[to : to + 1, :] = r.stage2[at, 8 * tap + color : 8 * tap + color + 1, :]
    for d in range(n):
        r.side_blocks[d] = pack(dside[:, d * w : (d + 1) * w], fold)
    sum_side = Reduce(n, r.side_blocks, r.side_pair, r.side_chip, r.side_chips, r.side_sem)
    sum_side.start()
    total_scale = tiny[0, 0, 2] + tiny[1, 0, 2] + tiny[2, 0, 2]
    tile = jnp.where(lane == 5, counts[0, 0].astype(f32), 0.0)
    for b in range(2):
        field, p, cot = small[SZ, b], small[SP, b], small[SC, b]
        c_a, t_a = small[SA, b], small[SB, b]
        x, t, e = pieces(field, slope0)
        q = 2.0 * e * (1.0 - x * t) * p * t_a
        c_z = jnp.where(valid(), cot + (1.0 + t + x * e) * c_a + slope0 * q, 0.0)
        slope_grad = jnp.where(valid(), field * (c_a * field * e + q), 0.0)
        fold_field(c_z * scale_col, r.firsts if b == 0 else r.results.at[me], 3)
        sums = [
            jnp.sum(cot, axis=1, keepdims=True),
            jnp.sum(c_z, axis=1, keepdims=True) * scale_col,
            jnp.sum(c_z * field, axis=1, keepdims=True) - 1024.0,
            jnp.sum(slope_grad, axis=1, keepdims=True) * (0.5 * sigmoid(slope_raw)),
        ]
        for k in range(4):
            tile = tile + jnp.where((lane == k) & (sub < 3), sums[k], 0.0)
        log_part = (1024.0 * total_scale + jnp.sum(small[SS, b] * small[ST, b])) / 3072.0
        tile = tile + jnp.where((lane == 4) & (sub == b), log_part, 0.0)
    r.results[me, 6] = tile
    share.start()
    sum_side.forward()
    share.forward()
    mid_grad = sum_mid.finish() / (2.0 * n)
    r.mid_g[...] = mid_grad
    diff = r.mid_o[...] - adam(r.mid_w[...], mid_grad, r.mid_f[...], r.mid_s[...], 0.01)[0]
    chunk = C // groups
    for k in range(groups):
        r.mid_diff[k] = diff[:, k * chunk : (k + 1) * chunk]
    ring1, ring2 = Across(groups, r.ring1_sem), Across(groups, r.ring2_sem)
    ring3, ring4 = Across(groups, r.ring3_sem), Across(groups, r.ring4_sem)
    for j, to in ring1.others():
        ring1.copy(r.mid_diff.at[to], r.mid_parts.at[j], j, to).start()
    side_grad = unpack(sum_side.finish(), fold)[0:58] / (2.0 * n)
    r.side_g[...] = side_grad
    new = adam(r.side_w[:, 0, :], side_grad, r.side_f[:, 0, :], r.side_s[:, 0, :], side_rate(w))[0]
    r.side_diff[grp] = pack(jnp.concatenate([r.side_o[...] - new, jnp.zeros((6, w), f32)], 0), fold)
    for j, to in ring3.others():
        ring3.copy(r.side_diff.at[grp], r.side_diff.at[grp], j, to).start()
    share.finish()
    tiny_sum = r.results[0, 6]
    for d in range(1, n):
        tiny_sum = tiny_sum + r.results[d, 6]
    r.out_small[0] = tiny_sum
    r.tiles[...] = jnp.zeros_like(r.tiles)
    for c in range(3):
        for k, ref in enumerate((r.tiny_w, r.tiny_f, r.tiny_s)):
            r.tiles[k, c : c + 1, 0:4] = ref[c, 0:1, :]
    r.tiles[3, 0:4, 0:3] = r.tiny_o[...]
    new = adam(r.tiles[0], tiny_sum / (2.0 * n), r.tiles[1], r.tiles[2], 0.05)[0]
    r.tiny_diff[grp] = r.tiles[3] - flip(jnp.where(lane < 4, new, 0.0))
    for j, to in ring4.others():
        ring4.copy(r.tiny_diff.at[grp], r.tiny_diff.at[grp], j, to).start()
    total = r.mid_diff[grp]
    for j, to in ring1.others():
        ring1.copy(r.mid_diff.at[to], r.mid_parts.at[j], j, to).wait_recv()
        total = total + r.mid_parts[j]
    r.mid_sum[grp] = total
    for j, to in ring2.others():
        ring2.copy(r.mid_sum.at[grp], r.mid_sum.at[grp], j, to).start()
    tiles = [r.results[d, 6] for d in range(n)]
    masks = match([jnp.broadcast_to(t[0:1, 5:6], (1, 128)) for t in tiles], me, 3.0, 1.0)
    log_third = jnp.zeros((1, 128), f32)
    for d in range(n):
        log_third = jnp.where(masks[d] > 0.0, jnp.broadcast_to(tiles[d][1:2, 4:5], (1, 128)), log_third)
    for k in range(6):
        out, c = (r.out_flow, k) if k < 3 else (r.out_back, k - 3)
        picked = jnp.zeros((8, 128), f32)
        for d in range(n):
            picked = jnp.where(masks[d] > 0.0, r.results[d, k], picked)
        out[c] = r.firsts[k]
        out[3 + c] = jnp.where(own_count > 1.5, r.results[me, k], 0.0)
        out[6 + c] = picked
    logs = [jnp.broadcast_to(tile[b : b + 1, 4:5], (1, 128)) for b in range(2)]
    logs[1] = jnp.where(own_count > 1.5, logs[1], 0.0)
    row_lane = lax.broadcasted_iota(jnp.int32, (1, 128), 1)
    r.out_small[1] = jnp.broadcast_to(
        jnp.where(row_lane == 0, logs[0], jnp.where(row_lane == 1, logs[1], log_third)), (8, 128))
    for j, to in ring3.others():
        ring3.copy(r.side_diff.at[grp], r.side_diff.at[grp], j, to).wait_recv()
    total = r.side_diff[0]
    for k in range(1, groups):
        total = total + r.side_diff[k]
    r.side_t[...] = unpack(total, fold)[0:58]
    for j, to in ring4.others():
        ring4.copy(r.tiny_diff.at[grp], r.tiny_diff.at[grp], j, to).wait_recv()
    total = r.tiny_diff[0]
    for k in range(1, groups):
        total = total + r.tiny_diff[k]
    r.out_small[2] = total
    for j, to in ring2.others():
        ring2.copy(r.mid_sum.at[grp], r.mid_sum.at[grp], j, to).wait_recv()
    for k in range(groups):
        r.mid_t[:, k * chunk : (k + 1) * chunk] = r.mid_sum[k]
    sum_mid.drain()
    sum_side.drain()
    for ring in (ring1, ring2):
        for j, to in ring.others():
            ring.copy(r.mid_sum.at[grp], r.mid_sum.at[grp], j, to).wait_send()
    for j, to in ring3.others():
        ring3.copy(r.side_diff.at[grp], r.side_diff.at[grp], j, to).wait_send()
    for j, to in ring4.others():
        ring4.copy(r.tiny_diff.at[grp], r.tiny_diff.at[grp], j, to).wait_send()


def last_kernel(n, groups, names, *refs):
    r = types.SimpleNamespace(**dict(zip(names, refs)))
    w = C // n
    lane = lax.broadcasted_iota(jnp.int32, (8, 128), 1)
    r.flow_o[...] = r.flow[...]
    r.back_o[...] = r.back[...]
    r.log_det[...] = r.small[1, 0:1, 0:3]
    tiny_sum = r.small[0]
    r.log_mean[...] = (tiny_sum[0:1, 4:5] + tiny_sum[1:2, 4:5]) / (2.0 * n)
    new, first, second = adam(r.mid_w[...], r.mid_g[...], r.mid_f[...], r.mid_s[...], 0.01)
    r.mid_f_new[...], r.mid_s_new[...], r.mid_new[...] = first, second, new
    new, first, second = adam(r.side_w[:, 0, :], r.side_g[...], r.side_f[:, 0, :], r.side_s[:, 0, :], side_rate(w))
    r.side_f_new[:, 0, :], r.side_s_new[:, 0, :], r.side_new[:, 0, :] = first, second, new
    r.tiles[...] = jnp.zeros_like(r.tiles)
    for c in range(3):
        for k, ref in enumerate((r.tiny_w, r.tiny_f, r.tiny_s)):
            r.tiles[k, c : c + 1, 0:4] = ref[c, 0:1, :]
    new, first, second = adam(r.tiles[0], tiny_sum / (2.0 * n), r.tiles[1], r.tiles[2], 0.05)
    for c in range(3):
        r.tiny_f_new[c, 0:1, :] = first[c : c + 1, 0:4]
        r.tiny_new[c, 0:1, :] = new[c : c + 1, 0:4]
    turned = flip(jnp.where(lane < 4, second, 0.0))
    for k in range(3):
        r.tiny_s_new[k, 0:1, :] = turned[k : k + 1, 0:3]
    r.slope_s_new[...] = turned[3:4, 0:3]

    def outer(diff, old, momentum, delta_out, momentum_out, out):
        delta = diff / groups
        mom = 0.9 * momentum[...] + delta
        delta_out[...], momentum_out[...] = delta, mom
        out[...] = old[...] - 0.7 * (delta + 0.9 * mom)

    outer(r.mid_t[...], r.mid_o, r.mid_m, r.mid_d, r.mid_m_new, r.mid_o_new)
    outer(r.side_t[...], r.side_o, r.side_m, r.side_d, r.side_m_new, r.side_o_new)
    outer(r.small[2, 0:4, 0:3], r.tiny_o, r.tiny_m, r.tiny_d, r.tiny_m_new, r.tiny_o_new)


def on_device(images, probes, out_cotangent, counts, terms, power_left, power_out, mid_weight, mid_first, mid_second,
              side_weight, side_first, side_second, tiny_weight, tiny_first, tiny_second,
              mid_outer, mid_momentum, side_outer, side_momentum, tiny_outer, tiny_momentum):
    n, groups = lax.axis_size("dp"), lax.axis_size("grp")
    w, fold, side_rows = scale_sizes(n)
    m = n // 2
    vm = pl.BlockSpec(memory_space=pltpu.VMEM)
    sm = pl.BlockSpec(memory_space=pltpu.SMEM)
    sd = lambda *shape: jax.ShapeDtypeStruct(shape, f32)
    dma = lambda *shape: pltpu.SemaphoreType.DMA(shape)
    vmem = lambda *shape: pltpu.VMEM(shape, f32)
    big = lambda dtype: pltpu.VMEM((C, 2 * PX), dtype)
    half = lambda *shape: pltpu.VMEM(shape, bf16)
    image = lambda x: x[0].reshape(9, 8, 128)
    turn = lambda x: jnp.swapaxes(x, -1, -2)
    row = lambda x: x[0][:, None, :]
    color = lambda x: jnp.transpose(x, (2, 0, 1))
    state = dict(
        mid_w=turn(mid_weight[0]), mid_f=turn(mid_first[0]), mid_s=turn(mid_second[0]), mid_o=turn(mid_outer),
        side_w=row(side_weight), side_f=row(side_first), side_s=row(side_second), side_o=side_outer,
        tiny_w=color(tiny_weight), tiny_f=color(tiny_first), tiny_s=color(tiny_second), tiny_o=tiny_outer,
    )
    vmem_in = dict(images=image(images), probes=image(probes), cots=image(out_cotangent), lefts=power_left[0], **state)
    smem_in = dict(counts=counts, terms=terms, out_left=power_out, tiny=color(tiny_weight))
    outs = dict(out_flow=sd(9, 8, 128), out_back=sd(9, 8, 128), out_small=sd(3, 8, 128), mid_g=sd(w, C), mid_t=sd(w, C),
                side_g=sd(58, w), side_t=sd(58, w))
    scratch = dict(
        stage=vmem(2, 80, C), stage2=vmem(2, 80, C), wa1=half(160, C), wp1=half(80, C), wa3=half(160, C), wp3=half(80, C),
        cols=vmem(3, C, 128), small=vmem(10, 2, 8, PX), sums=vmem(3, C, 128), field=half(8, 80, PX), prod=vmem(2, 80, PX),
        mh=half(C, C), ml=half(C, C), left2=vmem(8, C), live=vmem(8, 128), side=vmem(64, C),
        h1=big(f32), g1=big(f32), h2=big(f32), g2=big(f32),
        d1=big(f32), a1=big(bf16), b1=big(bf16), d2=big(f32), a2=big(bf16), b2=big(bf16), c2=big(bf16), t2=big(bf16),
        ca=big(f32), sides=vmem(n, side_rows, 128), thirds=vmem(n, 10, 8, 128), mids=vmem(n, w, C), results=vmem(n, 7, 8, 128),
        picked=vmem(9, 8, 128), firsts=vmem(6, 8, 128), dmid=vmem(n, w, C), dside=vmem(64, C),
        side_blocks=vmem(n, side_rows, 128),
        mid_pair=vmem(m, w, C), mid_chip=vmem(m, w, C), mid_chips=vmem(m, w, C),
        side_pair=vmem(m, side_rows, 128), side_chip=vmem(m, side_rows, 128), side_chips=vmem(m, side_rows, 128),
        mid_diff=vmem(groups, w, C // groups), mid_parts=vmem(groups, w, C // groups), mid_sum=vmem(groups, w, C // groups),
        side_diff=vmem(groups, side_rows, 128), tiny_diff=vmem(groups, 8, 128), tiles=vmem(4, 8, 128),
        sides_sem=dma(2, n), thirds_sem=dma(2, n), mids_sem=dma(2, n), results_sem=dma(2, n),
        mid_sem=dma(2, n), side_sem=dma(2, n),
        ring1_sem=dma(2, groups), ring2_sem=dma(2, groups), ring3_sem=dma(2, groups), ring4_sem=dma(2, groups),
    )
    ins = {**vmem_in, **smem_in}
    made = pl.pallas_call(
        functools.partial(main_kernel, n, groups, list(ins) + list(outs) + list(scratch)),
        in_specs=[vm] * len(vmem_in) + [sm] * len(smem_in),
        out_specs=[vm] * len(outs),
        out_shape=list(outs.values()),
        scratch_shapes=list(scratch.values()),
        compiler_params=pltpu.CompilerParams(vmem_limit_bytes=60 << 20, collective_id=0, has_side_effects=True),
    )(*ins.values())
    flow, back, small, mid_g, mid_t, side_g, side_t = made
    ins = dict(flow=flow, back=back, small=small, mid_g=mid_g, mid_t=mid_t, side_g=side_g, side_t=side_t, **state)
    ins.update(mid_m=turn(mid_momentum), side_m=side_momentum, tiny_m=tiny_momentum)
    scratch = dict(tiles=vmem(3, 8, 128))
    outs = dict(
        flow_o=sd(9, 8, 128), back_o=sd(9, 8, 128), log_det=sd(1, 3), log_mean=sd(1, 1),
        mid_f_new=sd(w, C), mid_s_new=sd(w, C), mid_new=sd(w, C),
        side_f_new=sd(58, 1, w), side_s_new=sd(58, 1, w), side_new=sd(58, 1, w),
        tiny_f_new=sd(3, 1, 4), tiny_s_new=sd(3, 1, 3), slope_s_new=sd(1, 3), tiny_new=sd(3, 1, 4),
        mid_d=sd(w, C), mid_m_new=sd(w, C), mid_o_new=sd(w, C),
        side_d=sd(58, w), side_m_new=sd(58, w), side_o_new=sd(58, w),
        tiny_d=sd(4, 3), tiny_m_new=sd(4, 3), tiny_o_new=sd(4, 3),
    )
    made = pl.pallas_call(
        functools.partial(last_kernel, n, groups, list(ins) + list(outs) + list(scratch)),
        in_specs=[vm] * len(ins),
        out_specs=[vm] * len(outs),
        out_shape=list(outs.values()),
        scratch_shapes=list(scratch.values()),
        compiler_params=pltpu.CompilerParams(vmem_limit_bytes=60 << 20),
    )(*ins.values())
    o = types.SimpleNamespace(**dict(zip(outs, made)))
    whole = lambda x: x.reshape(1, 3, 3, PX)
    back_turn = lambda x: turn(x)[None]
    return (
        whole(o.flow_o), whole(o.back_o), o.log_det, o.log_mean.reshape(1),
        back_turn(o.mid_f_new), back_turn(o.mid_s_new), back_turn(o.mid_new),
        o.side_f_new[:, 0][None], o.side_s_new[:, 0][None], o.side_new[:, 0][None],
        jnp.transpose(o.tiny_f_new, (1, 2, 0)), jnp.transpose(o.tiny_s_new, (1, 0, 2)), o.slope_s_new, jnp.transpose(o.tiny_new, (1, 2, 0)),
        turn(o.mid_d), turn(o.mid_m_new), turn(o.mid_o_new),
        o.side_d, o.side_m_new, o.side_o_new, o.tiny_d, o.tiny_m_new, o.tiny_o_new,
    )


def solution(mesh):
    split = P("grp", None, "dp")
    group = P("grp", None, None)
    image = P("grp", "dp", None, None)
    return jax.shard_map(
        on_device,
        mesh=mesh,
        in_specs=(image, image, image, P("grp", "dp"), P("grp", "dp"), group, P("grp", None),
                  split, split, split, split, split, split, group, group, group,
                  P(None, "dp"), P(None, "dp"), P(None, "dp"), P(None, "dp"), P(), P()),
        out_specs=(image, image, P("grp", "dp"), P("grp"), split, split, split, split, split, split,
                   group, group, P("grp", None), group) + (P(None, "dp"),) * 6 + (P(), P(), P()),
        check_vma=False,
    )
```

```python
import functools
import types

import jax, jax.numpy as jnp
from jax import lax
from jax.experimental import pallas as pl
from jax.experimental.pallas import tpu as pltpu
from jax.sharding import PartitionSpec as P

bf16, f32 = jnp.bfloat16, jnp.float32
HIGH = lax.Precision.HIGHEST
C, PX, TILE = 512, 1024, 512
CLIP = 0.98
LIP = 2.2


def dot_nn(a, b):
    return jnp.dot(a, b, preferred_element_type=f32)


def dot_tn(a, b):
    return lax.dot_general(a, b, (((0,), (0,)), ((), ())), preferred_element_type=f32)


def dot_nt(a, b):
    return lax.dot_general(a, b, (((1,), (1,)), ((), ())), preferred_element_type=f32)


def tap_masks():
    lane = lax.broadcasted_iota(jnp.int32, (8, PX), 1)
    row, col = lane // 32, lane % 32
    masks = []
    for tap in range(9):
        down, right = tap // 3 - 1, tap % 3 - 1
        ok = (row + down >= 0) & (row + down < 32) & (col + right >= 0) & (col + right < 32)
        masks.append(ok)
    return masks


def shift(field, tap, masks):
    if tap == 4:
        return field
    offset = (tap // 3 - 1) * 32 + tap % 3 - 1
    return jnp.where(masks[tap], pltpu.roll(field, (-offset) % PX, 1), 0.0)


def expand(field, flip, one, masks):
    high = field.astype(bf16).astype(f32)
    low = field - high
    row = lax.broadcasted_iota(jnp.int32, (8, PX), 0)
    base = jnp.where(row < 3, high, jnp.where(row < 6, pltpu.roll(low, 3, 0), one))
    parts = [shift(base, 8 - tap if flip else tap, masks) for tap in range(9)]
    return jnp.concatenate(parts + [jnp.zeros((8, PX), f32)], 0).astype(bf16)


def collapse(prod, flip, masks):
    total = prod[32:40]
    for tap in (0, 1, 2, 3, 5, 6, 7, 8):
        total = total + shift(prod[8 * tap : 8 * tap + 8], 8 - tap if flip else tap, masks)
    return total + pltpu.roll(total, 5, 0)


def pieces(h, slope_half):
    x = slope_half * h
    t = jnp.tanh(x)
    e = 1.0 - t * t
    return x, t, e


def softplus(raw):
    return jnp.maximum(raw, 0.0) + jnp.log1p(jnp.exp(-jnp.abs(raw)))


def sigmoid(raw):
    return 1.0 / (1.0 + jnp.exp(-raw))


def wide(ref, width):
    block = ref[...]
    return jnp.concatenate([block] * (width // 128), 1)


def to_column(row):
    return jnp.transpose(jnp.broadcast_to(row, (128, C)))


def prepare_side(side, lefts, out_left, stage, wa1, wp1, wa3, wp3, cols):
    rows = lax.broadcasted_iota(jnp.int32, (80, C), 0)
    stage[...] = jnp.zeros_like(stage)
    for color in range(3):
        for tap in range(9):
            stage[0, 8 * tap + color : 8 * tap + color + 1, :] = side[9 * color + tap : 9 * color + tap + 1, :]
            at = 31 + 9 * color + tap
            stage[1, 8 * tap + color : 8 * tap + color + 1, :] = side[at : at + 1, :]
    first = stage[0]
    u = lefts[0:1, :]
    right1 = jnp.sum(first * u, axis=1, keepdims=True)
    right1 = right1 / jnp.sqrt(jnp.sum(right1 * right1) + 1e-12)
    y1 = jnp.sum(first * right1, axis=0, keepdims=True)
    left1 = y1 / jnp.sqrt(jnp.sum(y1 * y1) + 1e-12)
    sigma1 = jnp.sum(left1 * y1)
    last = stage[1]
    inner = rows % 8
    weight = jnp.where(inner == 0, out_left[0], jnp.where(inner == 1, out_left[1], out_left[2]))
    mixed = jnp.where(inner < 3, last * weight, 0.0)
    right3 = mixed + pltpu.roll(mixed, 79, 0) + pltpu.roll(mixed, 78, 0)
    right3 = jnp.where(inner == 0, right3, 0.0)
    right3 = right3 / jnp.sqrt(jnp.sum(right3 * right3) + 1e-12)
    right3 = right3 + pltpu.roll(right3, 1, 0) + pltpu.roll(right3, 2, 0)
    prod = last * right3
    y3 = [jnp.sum(jnp.where(inner == k, prod, 0.0)) for k in range(3)]
    norm3 = jnp.sqrt(y3[0] * y3[0] + y3[1] * y3[1] + y3[2] * y3[2] + 1e-12)
    left3 = [value / norm3 for value in y3]
    sigma3 = left3[0] * y3[0] + left3[1] * y3[1] + left3[2] * y3[2]
    outer3 = jnp.where(inner == 0, left3[0], jnp.where(inner == 1, left3[1], left3[2])) * right3
    outer1 = right1 * left1
    q1, q3 = jnp.maximum(1.0, sigma1 / CLIP), jnp.maximum(1.0, sigma3 / CLIP)
    for at, q, wa, wp in ((0, q1, wa1, wp1), (1, q3, wa3, wp3)):
        scaled = stage[at] / (LIP * q)
        high = scaled.astype(bf16).astype(f32)
        low = scaled - high
        top = high + pltpu.roll(high, 3, 0)
        if at == 0:
            bias = side[27:28, :]
            bias_high = bias.astype(bf16).astype(f32)
            top = jnp.where(rows == 38, bias_high, jnp.where(rows == 39, bias - bias_high, top))
        wa[0:80, :] = top.astype(bf16)
        wa[80:160, :] = (low + pltpu.roll(low, 3, 0)).astype(bf16)
        wp[...] = (high + pltpu.roll(low, 3, 0)).astype(bf16)
    cols[0] = to_column(0.5 * softplus(side[28:29, :]))
    cols[1] = to_column(side[29:30, :])
    cols[2] = to_column(0.5 * softplus(side[30:31, :]))
    return (q1, sigma1, outer1), (q3, sigma3, outer3)


def prepare_mid(mid, lefts, m_high, m_low, outer):
    right = jnp.sum(mid * lefts[1:2, :], axis=1, keepdims=True)
    right = right / jnp.sqrt(jnp.sum(right * right) + 1e-12)
    y = jnp.sum(mid * right, axis=0, keepdims=True)
    left = y / jnp.sqrt(jnp.sum(y * y) + 1e-12)
    sigma = jnp.sum(left * y)
    q = jnp.maximum(1.0, sigma / CLIP)
    scaled = mid / (LIP * q)
    high = scaled.astype(bf16)
    m_high[...] = high
    m_low[...] = (scaled - high.astype(f32)).astype(bf16)
    outer[0:8, :] = jnp.broadcast_to(left, (8, C))
    return q, sigma, right


def correction(raw_grad, weight, q, sigma):
    ratio = sigma / CLIP
    active = jnp.where(ratio > 1.0, 1.0, jnp.where(ratio == 1.0, 0.5, 0.0))
    return 1.0 / (LIP * q), -active * jnp.sum(raw_grad * weight) / (LIP * q * q * CLIP)


def color_column(values):
    row = lax.broadcasted_iota(jnp.int32, (8, 1), 0)
    return jnp.where(row == 0, values[0], jnp.where(row == 1, values[1], values[2]))


PARTS = PX // TILE
RC = 32
AT = [slice(k * TILE, (k + 1) * TILE) for k in range(2 * PARTS)]
IM = (slice(0, PX), slice(PX, 2 * PX))
CHUNKS = [slice(k, k + RC) for k in range(0, C, RC)]


def pipeline(parts, dots, elem, after=None):
    held = dots(parts[0])
    for i, k in enumerate(parts):
        ahead = dots(parts[i + 1]) if i + 1 < len(parts) else None
        elem(k, *held)
        if after is not None and i >= 1:
            after(parts[i - 1])
        held = ahead
    if after is not None:
        after(parts[-1])


MESH = pl.DeviceIdType.MESH
SZ, SP, SC, SD, SV, SN, SS, ST, SA, SB = range(10)


def scale_sizes(n):
    w = C // n
    fold = 128 // w
    return w, fold, 64 // fold


def pack(block, fold):
    rows = block.shape[0] // fold
    return jnp.concatenate([block[i * rows : (i + 1) * rows] for i in range(fold)], 1)


def unpack(block, fold):
    w = 128 // fold
    return jnp.concatenate([block[:, i * w : (i + 1) * w] for i in range(fold)], 0)


class Gather:
    def __init__(self, n, buf, sems):
        self.n, self.m, self.buf, self.sems = n, n // 2, buf, sems
        self.me = lax.axis_index("dp")
        self.chip, self.core = self.me // 2, self.me % 2
        self.pair = self.me + 1 - 2 * self.core

    def copy(self, slot, sem, target):
        return pltpu.make_async_remote_copy(
            src_ref=self.buf.at[slot],
            dst_ref=self.buf.at[slot],
            send_sem=self.sems.at[0, sem],
            recv_sem=self.sems.at[1, sem],
            device_id={"dp": target},
            device_id_type=MESH,
        )

    def peer(self, j):
        return lax.rem(self.chip + j, self.m) * 2 + self.core

    def start(self):
        for j in range(1, self.m):
            self.copy(self.me, j, self.peer(j)).start()
        self.copy(self.me, self.m, self.pair).start()

    def forward(self):
        for j in range(1, self.m):
            source = self.peer(j)
            self.copy(source, self.m - j, source).wait_recv()
            self.copy(source, self.m + j, self.pair).start()

    def finish(self):
        for j in range(self.m):
            self.copy(self.me, self.m + j, self.pair).wait_recv()
        for j in range(1, 2 * self.m):
            self.copy(self.me, j, self.pair).wait_send()


class Reduce:
    def __init__(self, n, pieces, source, from_pair, chipsum, from_chips, sems):
        self.n, self.m, self.pieces = n, n // 2, pieces
        self.rows = source.shape[1] // pieces
        self.source, self.from_pair, self.chipsum, self.from_chips, self.sems = source, from_pair, chipsum, from_chips, sems
        self.me = lax.axis_index("dp")
        self.chip, self.core = self.me // 2, self.me % 2
        self.pair = self.me + 1 - 2 * self.core

    def piece(self, p):
        return pl.ds(p * self.rows, self.rows)

    def swap_copy(self, k, sem):
        return pltpu.make_async_remote_copy(
            src_ref=self.source.at[2 * k + 1 - self.core], dst_ref=self.from_pair.at[k],
            send_sem=self.sems.at[0, sem], recv_sem=self.sems.at[1, sem],
            device_id={"dp": self.pair}, device_id_type=MESH)

    def chip_copy(self, slot, j, p, target):
        sem = self.m + p * self.m + j
        return pltpu.make_async_remote_copy(
            src_ref=self.chipsum.at[slot, self.piece(p)], dst_ref=self.from_chips.at[j, self.piece(p)],
            send_sem=self.sems.at[0, sem], recv_sem=self.sems.at[1, sem],
            device_id={"dp": target}, device_id_type=MESH)

    def start(self):
        for j in range(1, self.m + 1):
            self.swap_copy(lax.rem(self.chip + j, self.m), j % self.m).start()

    def forward(self):
        for p in range(self.pieces):
            for j in range(1, self.m):
                to = lax.rem(self.chip + j, self.m)
                if p == 0:
                    self.swap_copy(to, j).wait_recv()
                    self.chipsum[to] = self.source[2 * to + self.core] + self.from_pair[to]
                self.chip_copy(to, j, p, to * 2 + self.core).start()
        self.swap_copy(self.chip, 0).wait_recv()
        self.chipsum[self.chip] = self.source[self.me] + self.from_pair[self.chip]

    def finish(self, p):
        total = self.chipsum[self.chip, self.piece(p)]
        for j in range(1, self.m):
            self.chip_copy(self.chip, j, p, self.pair).wait_recv()
            total = total + self.from_chips[j, self.piece(p)]
        return total

    def drain(self):
        for k in range(self.m):
            self.swap_copy(k, k).wait_send()
        for p in range(self.pieces):
            for j in range(1, self.m):
                self.chip_copy(self.chip, j, p, self.pair).wait_send()


class Across:
    def __init__(self, groups, sems):
        self.groups, self.sems, self.grp = groups, sems, lax.axis_index("grp")

    def copy(self, src, dst, j, target):
        return pltpu.make_async_remote_copy(
            src_ref=src, dst_ref=dst, send_sem=self.sems.at[0, j], recv_sem=self.sems.at[1, j],
            device_id={"grp": target}, device_id_type=MESH)

    def others(self):
        return [(j, lax.rem(self.grp + j, self.groups)) for j in range(1, self.groups)]


def barrier(n, groups):
    me, grp = lax.axis_index("dp"), lax.axis_index("grp")
    sem = pltpu.get_barrier_semaphore()
    m = n // 2
    chip, core = me // 2, me % 2
    for j in range(1, m):
        pl.semaphore_signal(sem, inc=1, device_id={"dp": lax.rem(chip + j, m) * 2 + core}, device_id_type=MESH)
    pl.semaphore_signal(sem, inc=1, device_id={"dp": me + 1 - 2 * core}, device_id_type=MESH)
    for j in range(1, groups):
        pl.semaphore_signal(sem, inc=1, device_id={"grp": lax.rem(grp + j, groups)}, device_id_type=MESH)
    pl.semaphore_wait(sem, m + groups - 1)


def match(counts, me, wanted_mine, wanted_theirs):
    zero = jnp.zeros((1, 128), f32)
    mine, my_rank = zero, zero
    for d in range(len(counts)):
        hit = jnp.where(counts[d] == wanted_mine, 1.0, 0.0)
        my_rank = my_rank + jnp.where(d < me, hit, zero)
        mine = mine + jnp.where(d == me, hit, zero)
    rank, masks = zero, []
    for d in range(len(counts)):
        hit = jnp.where(counts[d] == wanted_theirs, 1.0, 0.0)
        masks.append(jnp.where(rank == my_rank, hit * mine, zero))
        rank = rank + hit
    return masks


def adam(weight, gradient, first, second, rate):
    first = 0.9 * first + (1.0 - 0.9) * gradient
    second = 0.999 * second + (1.0 - 0.999) * gradient * gradient
    first_hat = first / (1.0 - 0.9**5.0)
    second_hat = second / (1.0 - 0.999**5.0)
    return weight - rate * (first_hat / (jnp.sqrt(second_hat) + 1e-8) + 0.01 * weight), first, second


def side_rate(w):
    return jnp.where(lax.broadcasted_iota(jnp.int32, (58, w), 0) >= 31, 0.004, 0.05)


def flip(tile):
    eye = lax.broadcasted_iota(jnp.int32, (8, 128), 0) == lax.broadcasted_iota(jnp.int32, (8, 128), 1)
    return lax.dot_general(tile, eye.astype(f32), (((0,), (0,)), ((), ())), precision=HIGH, preferred_element_type=f32)[0:8]


def spread_field(ref, base, small, at, b):
    for c in range(3):
        for k in range(8):
            small[at, b, c : c + 1, k * 128 : (k + 1) * 128] = ref[base + c, k : k + 1, :]


def fold_field(value, ref, base):
    for c in range(3):
        for k in range(8):
            ref[base + c, k : k + 1, :] = value[c : c + 1, k * 128 : (k + 1) * 128]


def main_kernel(n, groups, names, *refs):
    r = types.SimpleNamespace(**dict(zip(names, refs)))
    w, fold, side_rows = scale_sizes(n)
    m = n // 2
    me, grp = lax.axis_index("dp"), lax.axis_index("grp")
    counts, terms, tiny = r.counts, r.terms, r.tiny
    get_side = Gather(n, r.sides, r.sides_sem)
    get_third = Gather(n, r.thirds, r.thirds_sem)
    get_mid = Gather(n, r.mids, r.mids_sem)
    share = Gather(n, r.results, r.results_sem)
    share_flow = Gather(n, r.flows, r.flows_sem)
    r.sides[me] = pack(jnp.concatenate([r.side_w[:, 0, :], jnp.zeros((6, w), f32)], 0), fold)
    for at, ref in enumerate((r.images, r.probes, r.cots)):
        r.thirds[me, 3 * at : 3 * at + 3] = ref[6:9]
    lane = lax.broadcasted_iota(jnp.int32, (8, 128), 1)
    sub = lax.broadcasted_iota(jnp.int32, (8, 128), 0)
    own_count = jnp.broadcast_to(counts[0, 0].astype(f32), (1, 128))
    r.thirds[me, 9] = jnp.where(lane == 0, counts[0, 0].astype(f32), terms[0, 2].astype(f32))
    r.mids[me] = r.mid_w[...]
    barrier(n, groups)
    get_side.start()
    get_third.start()
    get_mid.start()
    small, side = r.small, r.side
    small[...] = jnp.zeros_like(small)
    for at, ref in ((SZ, r.images), (SP, r.probes), (SC, r.cots)):
        spread_field(ref, 0, small, at, 0)
    r.live[...] = jnp.where(terms[0, 0].astype(f32) > (sub % 4).astype(f32), 1.0, 0.0)
    bias_col = color_column([tiny[k, 0, 0] for k in range(3)])
    shift_col = color_column([tiny[k, 0, 1] for k in range(3)])
    scale_col = jnp.exp(color_column([tiny[k, 0, 2] for k in range(3)]))
    slope_raw = color_column([tiny[k, 0, 3] for k in range(3)])
    slope0 = 0.5 * softplus(slope_raw)

    def alive(b, step):
        return jnp.concatenate([r.live[b * 4 + step : b * 4 + step + 1, :]] * (PX // 128), 1)

    def prepare_image(b):
        masks = tap_masks()
        field = (small[SZ, b] + shift_col) * scale_col
        p = small[SP, b]
        small[SZ, b] = field
        x, t, e = pieces(field, slope0)
        d0 = 1.0 + t + x * e
        small[SD, b] = d0
        r.field[b] = expand(field + field * t, False, 1.0, masks)
        r.field[2 + b] = expand(d0 * p, False, 0.0, masks)
        r.field[4 + b] = expand(small[SC, b], True, 0.0, masks)
        r.field[6 + b] = expand(p, True, 0.0, masks)
        small[SV, b] = p
        small[SN, b] = -alive(b, 0) * p
        small[SS, b] = alive(b, 0) * p

    prepare_image(0)
    get_side.forward()
    get_side.finish()
    for i in range(fold):
        side[i * side_rows : (i + 1) * side_rows, :] = jnp.concatenate(
            [r.sides[d][:, i * w : (i + 1) * w] for d in range(n)], 1)
    lefts = r.lefts
    side1, side3 = prepare_side(side, lefts, [r.out_left[0, k] for k in range(3)], r.stage,
                                r.wa1, r.wp1, r.wa3, r.wp3, r.cols)
    wa1, wp1, wa3, wp3 = r.wa1, r.wp1, r.wa3, r.wp3
    mh, ml = r.mh, r.ml
    valid = lambda: lax.broadcasted_iota(jnp.int32, (8, PX), 0) < 3

    stages = []

    def stage(body):
        stages.append(body)
        pl.when(me + len(stages) > 0)(body)

    def doubled(index, k):
        block = r.field[index + k // PARTS, :, (k % PARTS) * TILE : (k % PARTS + 1) * TILE]
        return jnp.concatenate([block, block], 0)

    def column(which, rs):
        return jnp.concatenate([r.cols[which, rs]] * (TILE // 128), 1)

    one = (r.h1, r.g1, r.d1)
    two = (r.h2, r.g2, r.d2)

    def forward(kept, slope, bias, act, dact, k, h_all, dh_all):
        at = AT[k]
        hs, ys, ds = kept
        for rs in CHUNKS:
            h, dh = h_all[rs], dh_all[rs]
            if bias is not None:
                h = h + column(bias, rs)
            x = column(slope, rs) * h
            t = jnp.tanh(x)
            e = 1.0 - t * t
            d = 1.0 + t + x * e
            hs[rs, at] = h
            ds[rs, at] = d
            ys[rs, at] = e * (1.0 - x * t) * dh
            act[rs, at] = (h + h * t).astype(bf16)
            dact[rs, at] = (d * dh).astype(bf16)

    def backward(kept, slope, slope_to, bias_to, c_to, t_to, k, ca_all, ta_all):
        at = AT[k]
        hs, ys, ds = kept
        for rs in CHUNKS:
            h, d, c_a, t_a = hs[rs, at], ds[rs, at], ca_all[rs], ta_all[rs]
            sl = column(slope, rs)
            t = jnp.tanh(sl * h)
            he = h * (0.5 - 0.5 * (t * t))
            q = ys[rs, at] * t_a
            c_h = d * c_a + (sl + sl) * q
            grad = h * (c_a * he + q)
            gs, cs = grad[:, 0:128], c_h[:, 0:128]
            for j in range(1, TILE // 128):
                gs = gs + grad[:, j * 128 : (j + 1) * 128]
                if bias_to is not None:
                    cs = cs + c_h[:, j * 128 : (j + 1) * 128]
            r.sums[slope_to, rs] += gs
            if bias_to is not None:
                r.sums[bias_to, rs] += cs
            c_to[rs, at] = c_h.astype(bf16)
            t_to[rs, at] = (d * t_a).astype(bf16)

    def third_image():
        get_third.forward()
        get_third.finish()
        metas = [r.thirds[d, 9, 0:1, :] for d in range(n)]
        count_rows = [jnp.broadcast_to(meta[:, 0:1], (1, 128)) for meta in metas]
        masks = match(count_rows, me, 1.0, 3.0)
        helper, term = jnp.zeros((1, 128), f32), jnp.zeros((1, 128), f32) + terms[0, 1].astype(f32)
        for d in range(n):
            helper = helper + masks[d]
            term = jnp.where(masks[d] > 0.0, jnp.broadcast_to(metas[d][:, 1:2], (1, 128)), term)
        for at, ref in enumerate((r.images, r.probes, r.cots)):
            for c in range(3):
                picked = ref[3 + c]
                for d in range(n):
                    picked = jnp.where(masks[d] > 0.0, r.thirds[d, 3 * at + c], picked)
                r.picked[3 * at + c] = picked
        for at, place in ((0, SZ), (1, SP), (2, SC)):
            spread_field(r.picked, 3 * at, small, place, 1)
        r.live[...] = jnp.where(sub < 4, r.live[...], jnp.where(term > (sub % 4).astype(f32), 1.0, 0.0))

    def layer_one(b):
        @stage
        def _():
            pipeline([PARTS * b + k for k in range(PARTS)],
                     lambda k: (dot_tn(wa1[...], doubled(0, k)), dot_tn(wa1[...], doubled(2, k))),
                     functools.partial(forward, one, 0, None, r.a1, r.b1))
            for k in range(PARTS * b, PARTS * b + PARTS):
                r.ca[:, AT[k]] = dot_tn(wa3[...], doubled(4, k))
                r.c2[:, AT[k]] = dot_tn(wa3[...], doubled(6, k)).astype(bf16)

    layer_one(0)
    third_image()
    prepare_image(1)
    layer_one(1)
    get_mid.forward()
    get_mid.finish()
    q2, sigma2, right2 = prepare_mid(r.mids[...].reshape(C, C), lefts, mh, ml, r.left2)
    r.sums[...] = jnp.zeros_like(r.sums)

    @stage
    def layer_two():
        masks = tap_masks()

        def dots(k):
            a1 = r.a1[:, AT[k]]
            return dot_tn(mh[...], a1) + dot_tn(ml[...], a1), dot_tn(mh[...], r.b1[:, AT[k]])

        def after(k):
            to = slice((k % PARTS) * TILE, (k % PARTS + 1) * TILE)
            r.prod[0, :, to] = dot_nn(wp3[...], r.a2[:, AT[k]])
            r.prod[1, :, to] = dot_nn(wp3[...], r.b2[:, AT[k]])
            if k % PARTS == PARTS - 1:
                b = k // PARTS
                flow = small[SZ, b] + collapse(r.prod[0], False, masks) + bias_col
                fold_field(flow, r.firsts if b == 0 else r.flows.at[me], 0)
                small[ST, b] = jnp.where(valid(), collapse(r.prod[1], False, masks), 0.0)

        pipeline(range(2 * PARTS), dots, functools.partial(forward, two, 2, 1, r.a2, r.b2), after)

    def pull(step):
        masks = tap_masks()
        for b in range(2):
            if step == 1:
                r.c2[:, IM[b]] = (r.c2[:, IM[b]].astype(f32) * r.d2[:, IM[b]]).astype(bf16)
            else:
                spread = expand(small[SV, b], True, 0.0, masks)
                wide_v = jnp.concatenate([spread, spread], 0)
                r.c2[:, IM[b]] = (dot_tn(wa3[...], wide_v) * r.d2[:, IM[b]]).astype(bf16)
        for b in range(2):
            r.t2[:, IM[b]] = (dot_nn(mh[...], r.c2[:, IM[b]]) * r.d1[:, IM[b]]).astype(bf16)
        sign = (-1.0) ** step
        for b in range(2):
            prod = dot_nn(wp1[...], r.t2[:, IM[b]])
            v = jnp.where(valid(), small[SD, b] * collapse(prod, True, masks), 0.0)
            small[SV, b] = v
            on = sign * alive(b, step)
            small[SN, b] = small[SN, b] - on * v
            small[SS, b] = small[SS, b] + (on / (step + 1.0)) * v

    share_flow.start()
    for step in (1, 2, 3):
        stage(functools.partial(pull, step))
    share_flow.forward()

    @stage
    def back_two():
        masks = tap_masks()
        for b in range(2):
            r.field[6 + b] = expand(small[SN, b], True, 0.0, masks)
        pipeline(range(2 * PARTS), lambda k: (r.ca[:, AT[k]], dot_tn(wa3[...], doubled(6, k))),
                 functools.partial(backward, two, 2, 1, 0, r.c2, r.t2))

    raw = dot_nt(r.a1[...], r.c2[...]) + dot_nt(r.b1[...], r.t2[...])
    straight, across = correction(raw, r.mids[...].reshape(C, C), q2, sigma2)
    r.dmid[...] = (straight * raw + (across * right2) * r.left2[0:1, :]).reshape(n, w, C)
    sum_mid = Reduce(n, w // 16, r.dmid, r.mid_pair, r.mid_chip, r.mid_chips, r.mid_sem)
    sum_mid.start()
    g3 = dot_nt(r.field[4], r.a2[:, 0:PX]) + dot_nt(r.field[6], r.b2[:, 0:PX])
    g3 = g3 + dot_nt(r.field[5], r.a2[:, PX:]) + dot_nt(r.field[7], r.b2[:, PX:])
    ones = jnp.ones((8, 128), f32)
    row_of = lambda acc: lax.dot_general(
        ones, acc, (((1,), (1,)), ((), ())), precision=HIGH, preferred_element_type=f32)[0:1]
    dside = r.dside

    def put_taps(at, norm, grad, start):
        q, sigma, outer = norm
        row80 = lax.broadcasted_iota(jnp.int32, (80, C), 0)
        joined = jnp.where((row80 % 8 < 3) & (row80 < 72), grad + pltpu.roll(grad, 77, 0), 0.0)
        straight, across = correction(joined, r.stage[at], q, sigma)
        r.stage2[at] = straight * joined + across * outer
        for color in range(3):
            for tap in range(9):
                to = start + 9 * color + tap
                dside[to : to + 1, :] = r.stage2[at, 8 * tap + color : 8 * tap + color + 1, :]

    dside[29:30, :] = row_of(r.sums[0])
    dside[30:31, :] = row_of(r.sums[1]) * sigmoid(side[30:31, :])
    dside[58:64, :] = jnp.zeros((6, C), f32)
    put_taps(1, side3, g3, 31)
    sum_mid.forward()

    @stage
    def back_one():
        masks = tap_masks()

        def dots(k):
            c2 = r.c2[:, AT[k]]
            return dot_nn(mh[...], c2) + dot_nn(ml[...], c2), dot_nn(mh[...], r.t2[:, AT[k]])

        def after(k):
            to = slice((k % PARTS) * TILE, (k % PARTS + 1) * TILE)
            r.prod[0, :, to] = dot_nn(wp1[...], r.a2[:, AT[k]])
            r.prod[1, :, to] = dot_nn(wp1[...], r.b2[:, AT[k]])
            if k % PARTS == PARTS - 1:
                small[SA, k // PARTS] = collapse(r.prod[0], True, masks)
                small[SB, k // PARTS] = collapse(r.prod[1], True, masks)

        pipeline(range(2 * PARTS), dots, functools.partial(backward, one, 0, 2, None, r.a2, r.b2), after)

    g1 = dot_nt(r.field[0], r.a2[:, 0:PX]) + dot_nt(r.field[2], r.b2[:, 0:PX])
    g1 = g1 + dot_nt(r.field[1], r.a2[:, PX:]) + dot_nt(r.field[3], r.b2[:, PX:])
    dside[27:28, :] = g1[38:39]
    dside[28:29, :] = row_of(r.sums[2]) * sigmoid(side[28:29, :])
    put_taps(0, side1, g1, 0)
    for d in range(n):
        r.side_blocks[d] = pack(dside[:, d * w : (d + 1) * w], fold)
    sum_side = Reduce(n, 1, r.side_blocks, r.side_pair, r.side_chip, r.side_chips, r.side_sem)
    sum_side.start()
    total_scale = tiny[0, 0, 2] + tiny[1, 0, 2] + tiny[2, 0, 2]
    tile = jnp.where(lane == 5, counts[0, 0].astype(f32), 0.0)
    for b in range(2):
        field, p, cot = small[SZ, b], small[SP, b], small[SC, b]
        c_a, t_a = small[SA, b], small[SB, b]
        x, t, e = pieces(field, slope0)
        q = 2.0 * e * (1.0 - x * t) * p * t_a
        c_z = jnp.where(valid(), cot + (1.0 + t + x * e) * c_a + slope0 * q, 0.0)
        slope_grad = jnp.where(valid(), field * (c_a * field * e + q), 0.0)
        fold_field(c_z * scale_col, r.firsts if b == 0 else r.results.at[me], 3 if b == 0 else 0)
        sums = [
            jnp.sum(cot, axis=1, keepdims=True),
            jnp.sum(c_z, axis=1, keepdims=True) * scale_col,
            jnp.sum(c_z * field, axis=1, keepdims=True) - 1024.0,
            jnp.sum(slope_grad, axis=1, keepdims=True) * (0.5 * sigmoid(slope_raw)),
        ]
        for k in range(4):
            tile = tile + jnp.where((lane == k) & (sub < 3), sums[k], 0.0)
        log_part = (1024.0 * total_scale + jnp.sum(small[SS, b] * small[ST, b])) / 3072.0
        tile = tile + jnp.where((lane == 4) & (sub == b), log_part, 0.0)
    r.results[me, 3] = tile
    share.start()
    sum_side.forward()
    ring1 = Across(groups, r.ring1_sem)
    ring3, ring4 = Across(groups, r.ring3_sem), Across(groups, r.ring4_sem)
    cuts = w // 16

    def mid_copy(p, j, to):
        rows = pl.ds(16 * p, 16)
        return ring1.copy(r.mid_diff.at[grp, rows], r.mid_diff.at[grp, rows], p * groups + j, to)

    for p in range(cuts):
        rows = slice(16 * p, 16 * p + 16)
        mid_grad = sum_mid.finish(p) / (2.0 * n)
        r.mid_g[rows] = mid_grad
        r.mid_diff[grp, rows] = r.mid_o[rows] - adam(r.mid_w[rows], mid_grad, r.mid_f[rows], r.mid_s[rows], 0.01)[0]
        for j, to in ring1.others():
            mid_copy(p, j, to).start()
    share.forward()
    side_grad = unpack(sum_side.finish(0), fold)[0:58] / (2.0 * n)
    r.side_g[...] = side_grad
    new = adam(r.side_w[:, 0, :], side_grad, r.side_f[:, 0, :], r.side_s[:, 0, :], side_rate(w))[0]
    r.side_diff[grp] = pack(jnp.concatenate([r.side_o[...] - new, jnp.zeros((6, w), f32)], 0), fold)
    for j, to in ring3.others():
        ring3.copy(r.side_diff.at[grp], r.side_diff.at[grp], j, to).start()
    share.finish()
    tiny_sum = r.results[0, 3]
    for d in range(1, n):
        tiny_sum = tiny_sum + r.results[d, 3]
    r.out_small[0] = tiny_sum
    r.tiles[...] = jnp.zeros_like(r.tiles)
    for c in range(3):
        for k, ref in enumerate((r.tiny_w, r.tiny_f, r.tiny_s)):
            r.tiles[k, c : c + 1, 0:4] = ref[c, 0:1, :]
    r.tiles[3, 0:4, 0:3] = r.tiny_o[...]
    new = adam(r.tiles[0], tiny_sum / (2.0 * n), r.tiles[1], r.tiles[2], 0.05)[0]
    r.tiny_diff[grp] = r.tiles[3] - flip(jnp.where(lane < 4, new, 0.0))
    for j, to in ring4.others():
        ring4.copy(r.tiny_diff.at[grp], r.tiny_diff.at[grp], j, to).start()
    tiles = [r.results[d, 3] for d in range(n)]
    masks = match([jnp.broadcast_to(t[0:1, 5:6], (1, 128)) for t in tiles], me, 3.0, 1.0)
    log_third = jnp.zeros((1, 128), f32)
    for d in range(n):
        log_third = jnp.where(masks[d] > 0.0, jnp.broadcast_to(tiles[d][1:2, 4:5], (1, 128)), log_third)
    share_flow.finish()
    for out, ref, base in ((r.out_flow, r.flows, 0), (r.out_back, r.results, 3)):
        for c in range(3):
            picked = jnp.zeros((8, 128), f32)
            for d in range(n):
                picked = jnp.where(masks[d] > 0.0, ref[d, c], picked)
            out[c] = r.firsts[base + c]
            out[3 + c] = jnp.where(own_count > 1.5, ref[me, c], 0.0)
            out[6 + c] = picked
    logs = [jnp.broadcast_to(tile[b : b + 1, 4:5], (1, 128)) for b in range(2)]
    logs[1] = jnp.where(own_count > 1.5, logs[1], 0.0)
    row_lane = lax.broadcasted_iota(jnp.int32, (1, 128), 1)
    r.out_small[1] = jnp.broadcast_to(
        jnp.where(row_lane == 0, logs[0], jnp.where(row_lane == 1, logs[1], log_third)), (8, 128))
    for j, to in ring3.others():
        ring3.copy(r.side_diff.at[grp], r.side_diff.at[grp], j, to).wait_recv()
    total = r.side_diff[0]
    for k in range(1, groups):
        total = total + r.side_diff[k]
    r.side_t[...] = unpack(total, fold)[0:58]
    for j, to in ring4.others():
        ring4.copy(r.tiny_diff.at[grp], r.tiny_diff.at[grp], j, to).wait_recv()
    total = r.tiny_diff[0]
    for k in range(1, groups):
        total = total + r.tiny_diff[k]
    r.out_small[2] = total
    for p in range(cuts):
        rows = slice(16 * p, 16 * p + 16)
        for j, to in ring1.others():
            mid_copy(p, j, to).wait_recv()
        total = r.mid_diff[0, rows]
        for k in range(1, groups):
            total = total + r.mid_diff[k, rows]
        r.mid_t[rows] = total
    sum_mid.drain()
    sum_side.drain()
    for p in range(cuts):
        for j, to in ring1.others():
            mid_copy(p, j, to).wait_send()
    for j, to in ring3.others():
        ring3.copy(r.side_diff.at[grp], r.side_diff.at[grp], j, to).wait_send()
    for j, to in ring4.others():
        ring4.copy(r.tiny_diff.at[grp], r.tiny_diff.at[grp], j, to).wait_send()


def last_kernel(n, groups, names, *refs):
    r = types.SimpleNamespace(**dict(zip(names, refs)))
    w = C // n
    lane = lax.broadcasted_iota(jnp.int32, (8, 128), 1)
    r.flow_o[...] = r.flow[...]
    r.back_o[...] = r.back[...]
    r.log_det[...] = r.small[1, 0:1, 0:3]
    tiny_sum = r.small[0]
    r.log_mean[...] = (tiny_sum[0:1, 4:5] + tiny_sum[1:2, 4:5]) / (2.0 * n)
    new, first, second = adam(r.mid_w[...], r.mid_g[...], r.mid_f[...], r.mid_s[...], 0.01)
    r.mid_f_new[...], r.mid_s_new[...], r.mid_new[...] = first, second, new
    new, first, second = adam(r.side_w[:, 0, :], r.side_g[...], r.side_f[:, 0, :], r.side_s[:, 0, :], side_rate(w))
    r.side_f_new[:, 0, :], r.side_s_new[:, 0, :], r.side_new[:, 0, :] = first, second, new
    r.tiles[...] = jnp.zeros_like(r.tiles)
    for c in range(3):
        for k, ref in enumerate((r.tiny_w, r.tiny_f, r.tiny_s)):
            r.tiles[k, c : c + 1, 0:4] = ref[c, 0:1, :]
    new, first, second = adam(r.tiles[0], tiny_sum / (2.0 * n), r.tiles[1], r.tiles[2], 0.05)
    for c in range(3):
        r.tiny_f_new[c, 0:1, :] = first[c : c + 1, 0:4]
        r.tiny_new[c, 0:1, :] = new[c : c + 1, 0:4]
    turned = flip(jnp.where(lane < 4, second, 0.0))
    for k in range(3):
        r.tiny_s_new[k, 0:1, :] = turned[k : k + 1, 0:3]
    r.slope_s_new[...] = turned[3:4, 0:3]

    def outer(diff, old, momentum, delta_out, momentum_out, out):
        delta = diff / groups
        mom = 0.9 * momentum[...] + delta
        delta_out[...], momentum_out[...] = delta, mom
        out[...] = old[...] - 0.7 * (delta + 0.9 * mom)

    outer(r.mid_t[...], r.mid_o, r.mid_m, r.mid_d, r.mid_m_new, r.mid_o_new)
    outer(r.side_t[...], r.side_o, r.side_m, r.side_d, r.side_m_new, r.side_o_new)
    outer(r.small[2, 0:4, 0:3], r.tiny_o, r.tiny_m, r.tiny_d, r.tiny_m_new, r.tiny_o_new)


def on_device(images, probes, out_cotangent, counts, terms, power_left, power_out, mid_weight, mid_first, mid_second,
              side_weight, side_first, side_second, tiny_weight, tiny_first, tiny_second,
              mid_outer, mid_momentum, side_outer, side_momentum, tiny_outer, tiny_momentum):
    n, groups = lax.axis_size("dp"), lax.axis_size("grp")
    w, fold, side_rows = scale_sizes(n)
    m = n // 2
    vm = pl.BlockSpec(memory_space=pltpu.VMEM)
    sm = pl.BlockSpec(memory_space=pltpu.SMEM)
    sd = lambda *shape: jax.ShapeDtypeStruct(shape, f32)
    dma = lambda *shape: pltpu.SemaphoreType.DMA(shape)
    vmem = lambda *shape: pltpu.VMEM(shape, f32)
    big = lambda dtype: pltpu.VMEM((C, 2 * PX), dtype)
    half = lambda *shape: pltpu.VMEM(shape, bf16)
    image = lambda x: x[0].reshape(9, 8, 128)
    turn = lambda x: jnp.swapaxes(x, -1, -2)
    row = lambda x: x[0][:, None, :]
    color = lambda x: jnp.transpose(x, (2, 0, 1))
    state = dict(
        mid_w=turn(mid_weight[0]), mid_f=turn(mid_first[0]), mid_s=turn(mid_second[0]), mid_o=turn(mid_outer),
        side_w=row(side_weight), side_f=row(side_first), side_s=row(side_second), side_o=side_outer,
        tiny_w=color(tiny_weight), tiny_f=color(tiny_first), tiny_s=color(tiny_second), tiny_o=tiny_outer,
    )
    vmem_in = dict(images=image(images), probes=image(probes), cots=image(out_cotangent), lefts=power_left[0], **state)
    smem_in = dict(counts=counts, terms=terms, out_left=power_out, tiny=color(tiny_weight))
    outs = dict(out_flow=sd(9, 8, 128), out_back=sd(9, 8, 128), out_small=sd(3, 8, 128), mid_g=sd(w, C), mid_t=sd(w, C),
                side_g=sd(58, w), side_t=sd(58, w))
    scratch = dict(
        stage=vmem(2, 80, C), stage2=vmem(2, 80, C), wa1=half(160, C), wp1=half(80, C), wa3=half(160, C), wp3=half(80, C),
        cols=vmem(3, C, 128), small=vmem(10, 2, 8, PX), sums=vmem(3, C, 128), field=half(8, 80, PX), prod=vmem(2, 80, PX),
        mh=half(C, C), ml=half(C, C), left2=vmem(8, C), live=vmem(8, 128), side=vmem(64, C),
        h1=big(f32), g1=big(f32), h2=big(f32), g2=big(f32),
        d1=big(f32), a1=big(bf16), b1=big(bf16), d2=big(f32), a2=big(bf16), b2=big(bf16), c2=big(bf16), t2=big(bf16),
        ca=big(f32), sides=vmem(n, side_rows, 128), thirds=vmem(n, 10, 8, 128), mids=vmem(n, w, C), results=vmem(n, 4, 8, 128), flows=vmem(n, 3, 8, 128), flows_sem=dma(2, n),
        picked=vmem(9, 8, 128), firsts=vmem(6, 8, 128), dmid=vmem(n, w, C), dside=vmem(64, C),
        side_blocks=vmem(n, side_rows, 128),
        mid_pair=vmem(m, w, C), mid_chip=vmem(m, w, C), mid_chips=vmem(m, w, C),
        side_pair=vmem(m, side_rows, 128), side_chip=vmem(m, side_rows, 128), side_chips=vmem(m, side_rows, 128),
        mid_diff=vmem(groups, w, C),
        side_diff=vmem(groups, side_rows, 128), tiny_diff=vmem(groups, 8, 128), tiles=vmem(4, 8, 128),
        sides_sem=dma(2, n), thirds_sem=dma(2, n), mids_sem=dma(2, n), results_sem=dma(2, n),
        mid_sem=dma(2, m * (1 + w // 16)), side_sem=dma(2, n),
        ring1_sem=dma(2, groups * (w // 16)), ring3_sem=dma(2, groups), ring4_sem=dma(2, groups),
    )
    ins = {**vmem_in, **smem_in}
    made = pl.pallas_call(
        functools.partial(main_kernel, n, groups, list(ins) + list(outs) + list(scratch)),
        in_specs=[vm] * len(vmem_in) + [sm] * len(smem_in),
        out_specs=[vm] * len(outs),
        out_shape=list(outs.values()),
        scratch_shapes=list(scratch.values()),
        compiler_params=pltpu.CompilerParams(vmem_limit_bytes=60 << 20, collective_id=0, has_side_effects=True),
    )(*ins.values())
    flow, back, small, mid_g, mid_t, side_g, side_t = made
    ins = dict(flow=flow, back=back, small=small, mid_g=mid_g, mid_t=mid_t, side_g=side_g, side_t=side_t, **state)
    ins.update(mid_m=turn(mid_momentum), side_m=side_momentum, tiny_m=tiny_momentum)
    scratch = dict(tiles=vmem(3, 8, 128))
    outs = dict(
        flow_o=sd(9, 8, 128), back_o=sd(9, 8, 128), log_det=sd(1, 3), log_mean=sd(1, 1),
        mid_f_new=sd(w, C), mid_s_new=sd(w, C), mid_new=sd(w, C),
        side_f_new=sd(58, 1, w), side_s_new=sd(58, 1, w), side_new=sd(58, 1, w),
        tiny_f_new=sd(3, 1, 4), tiny_s_new=sd(3, 1, 3), slope_s_new=sd(1, 3), tiny_new=sd(3, 1, 4),
        mid_d=sd(w, C), mid_m_new=sd(w, C), mid_o_new=sd(w, C),
        side_d=sd(58, w), side_m_new=sd(58, w), side_o_new=sd(58, w),
        tiny_d=sd(4, 3), tiny_m_new=sd(4, 3), tiny_o_new=sd(4, 3),
    )
    made = pl.pallas_call(
        functools.partial(last_kernel, n, groups, list(ins) + list(outs) + list(scratch)),
        in_specs=[vm] * len(ins),
        out_specs=[vm] * len(outs),
        out_shape=list(outs.values()),
        scratch_shapes=list(scratch.values()),
        compiler_params=pltpu.CompilerParams(vmem_limit_bytes=60 << 20),
    )(*ins.values())
    o = types.SimpleNamespace(**dict(zip(outs, made)))
    whole = lambda x: x.reshape(1, 3, 3, PX)
    back_turn = lambda x: turn(x)[None]
    return (
        whole(o.flow_o), whole(o.back_o), o.log_det, o.log_mean.reshape(1),
        back_turn(o.mid_f_new), back_turn(o.mid_s_new), back_turn(o.mid_new),
        o.side_f_new[:, 0][None], o.side_s_new[:, 0][None], o.side_new[:, 0][None],
        jnp.transpose(o.tiny_f_new, (1, 2, 0)), jnp.transpose(o.tiny_s_new, (1, 0, 2)), o.slope_s_new, jnp.transpose(o.tiny_new, (1, 2, 0)),
        turn(o.mid_d), turn(o.mid_m_new), turn(o.mid_o_new),
        o.side_d, o.side_m_new, o.side_o_new, o.tiny_d, o.tiny_m_new, o.tiny_o_new,
    )


def solution(mesh):
    split = P("grp", None, "dp")
    group = P("grp", None, None)
    image = P("grp", "dp", None, None)
    return jax.shard_map(
        on_device,
        mesh=mesh,
        in_specs=(image, image, image, P("grp", "dp"), P("grp", "dp"), group, P("grp", None),
                  split, split, split, split, split, split, group, group, group,
                  P(None, "dp"), P(None, "dp"), P(None, "dp"), P(None, "dp"), P(), P()),
        out_specs=(image, image, P("grp", "dp"), P("grp"), split, split, split, split, split, split,
                   group, group, P("grp", None), group) + (P(None, "dp"),) * 6 + (P(), P(), P()),
        check_vma=False,
    )
```

```python
import functools
import types

import jax, jax.numpy as jnp
from jax import lax
from jax.experimental import pallas as pl
from jax.experimental.pallas import tpu as pltpu
from jax.sharding import PartitionSpec as P

bf16, f32 = jnp.bfloat16, jnp.float32
HIGH = lax.Precision.HIGHEST
C, PX, TILE = 512, 1024, 512
CLIP = 0.98
LIP = 2.2


def dot_nn(a, b):
    return jnp.dot(a, b, preferred_element_type=f32)


def dot_tn(a, b):
    return lax.dot_general(a, b, (((0,), (0,)), ((), ())), preferred_element_type=f32)


def dot_nt(a, b):
    return lax.dot_general(a, b, (((1,), (1,)), ((), ())), preferred_element_type=f32)


def tap_masks():
    lane = lax.broadcasted_iota(jnp.int32, (8, PX), 1)
    row, col = lane // 32, lane % 32
    masks = []
    for tap in range(9):
        down, right = tap // 3 - 1, tap % 3 - 1
        ok = (row + down >= 0) & (row + down < 32) & (col + right >= 0) & (col + right < 32)
        masks.append(ok)
    return masks


def shift(field, tap, masks):
    if tap == 4:
        return field
    offset = (tap // 3 - 1) * 32 + tap % 3 - 1
    return jnp.where(masks[tap], pltpu.roll(field, (-offset) % PX, 1), 0.0)


def expand(field, flip, one, masks):
    high = field.astype(bf16).astype(f32)
    low = field - high
    row = lax.broadcasted_iota(jnp.int32, (8, PX), 0)
    base = jnp.where(row < 3, high, jnp.where(row < 6, pltpu.roll(low, 3, 0), one))
    parts = [shift(base, 8 - tap if flip else tap, masks) for tap in range(9)]
    return jnp.concatenate(parts + [jnp.zeros((8, PX), f32)], 0).astype(bf16)


def collapse(prod, flip, masks):
    total = prod[32:40]
    for tap in (0, 1, 2, 3, 5, 6, 7, 8):
        total = total + shift(prod[8 * tap : 8 * tap + 8], 8 - tap if flip else tap, masks)
    return total + pltpu.roll(total, 5, 0)


def pieces(h, slope_half):
    x = slope_half * h
    t = jnp.tanh(x)
    e = 1.0 - t * t
    return x, t, e


def softplus(raw):
    return jnp.maximum(raw, 0.0) + jnp.log1p(jnp.exp(-jnp.abs(raw)))


def sigmoid(raw):
    return 1.0 / (1.0 + jnp.exp(-raw))


def wide(ref, width):
    block = ref[...]
    return jnp.concatenate([block] * (width // 128), 1)


def to_column(row):
    return jnp.transpose(jnp.broadcast_to(row, (128, C)))


def prepare_side(side, lefts, out_left, stage, wa1, wp1, wa3, wp3, cols):
    rows = lax.broadcasted_iota(jnp.int32, (80, C), 0)
    stage[...] = jnp.zeros_like(stage)
    for color in range(3):
        for tap in range(9):
            stage[0, 8 * tap + color : 8 * tap + color + 1, :] = side[9 * color + tap : 9 * color + tap + 1, :]
            at = 31 + 9 * color + tap
            stage[1, 8 * tap + color : 8 * tap + color + 1, :] = side[at : at + 1, :]
    first = stage[0]
    u = lefts[0:1, :]
    right1 = jnp.sum(first * u, axis=1, keepdims=True)
    right1 = right1 / jnp.sqrt(jnp.sum(right1 * right1) + 1e-12)
    y1 = jnp.sum(first * right1, axis=0, keepdims=True)
    left1 = y1 / jnp.sqrt(jnp.sum(y1 * y1) + 1e-12)
    sigma1 = jnp.sum(left1 * y1)
    last = stage[1]
    inner = rows % 8
    weight = jnp.where(inner == 0, out_left[0], jnp.where(inner == 1, out_left[1], out_left[2]))
    mixed = jnp.where(inner < 3, last * weight, 0.0)
    right3 = mixed + pltpu.roll(mixed, 79, 0) + pltpu.roll(mixed, 78, 0)
    right3 = jnp.where(inner == 0, right3, 0.0)
    right3 = right3 / jnp.sqrt(jnp.sum(right3 * right3) + 1e-12)
    right3 = right3 + pltpu.roll(right3, 1, 0) + pltpu.roll(right3, 2, 0)
    prod = last * right3
    y3 = [jnp.sum(jnp.where(inner == k, prod, 0.0)) for k in range(3)]
    norm3 = jnp.sqrt(y3[0] * y3[0] + y3[1] * y3[1] + y3[2] * y3[2] + 1e-12)
    left3 = [value / norm3 for value in y3]
    sigma3 = left3[0] * y3[0] + left3[1] * y3[1] + left3[2] * y3[2]
    outer3 = jnp.where(inner == 0, left3[0], jnp.where(inner == 1, left3[1], left3[2])) * right3
    outer1 = right1 * left1
    q1, q3 = jnp.maximum(1.0, sigma1 / CLIP), jnp.maximum(1.0, sigma3 / CLIP)
    for at, q, wa, wp in ((0, q1, wa1, wp1), (1, q3, wa3, wp3)):
        scaled = stage[at] / (LIP * q)
        high = scaled.astype(bf16).astype(f32)
        low = scaled - high
        top = high + pltpu.roll(high, 3, 0)
        if at == 0:
            bias = side[27:28, :]
            bias_high = bias.astype(bf16).astype(f32)
            top = jnp.where(rows == 38, bias_high, jnp.where(rows == 39, bias - bias_high, top))
        wa[0:80, :] = top.astype(bf16)
        wa[80:160, :] = (low + pltpu.roll(low, 3, 0)).astype(bf16)
        wp[...] = (high + pltpu.roll(low, 3, 0)).astype(bf16)
    cols[0] = to_column(0.5 * softplus(side[28:29, :]))
    cols[1] = to_column(side[29:30, :])
    cols[2] = to_column(0.5 * softplus(side[30:31, :]))
    return (q1, sigma1, outer1), (q3, sigma3, outer3)


def prepare_mid(mid, lefts, m_high, m_low, outer):
    right = jnp.sum(mid * lefts[1:2, :], axis=1, keepdims=True)
    right = right / jnp.sqrt(jnp.sum(right * right) + 1e-12)
    y = jnp.sum(mid * right, axis=0, keepdims=True)
    left = y / jnp.sqrt(jnp.sum(y * y) + 1e-12)
    sigma = jnp.sum(left * y)
    q = jnp.maximum(1.0, sigma / CLIP)
    scaled = mid / (LIP * q)
    high = scaled.astype(bf16)
    m_high[...] = high
    m_low[...] = (scaled - high.astype(f32)).astype(bf16)
    outer[0:8, :] = jnp.broadcast_to(left, (8, C))
    return q, sigma, right


def correction(raw_grad, weight, q, sigma):
    ratio = sigma / CLIP
    active = jnp.where(ratio > 1.0, 1.0, jnp.where(ratio == 1.0, 0.5, 0.0))
    return 1.0 / (LIP * q), -active * jnp.sum(raw_grad * weight) / (LIP * q * q * CLIP)


def color_column(values):
    row = lax.broadcasted_iota(jnp.int32, (8, 1), 0)
    return jnp.where(row == 0, values[0], jnp.where(row == 1, values[1], values[2]))


PARTS = PX // TILE
RC = 32
AT = [slice(k * TILE, (k + 1) * TILE) for k in range(2 * PARTS)]
IM = (slice(0, PX), slice(PX, 2 * PX))
CHUNKS = [slice(k, k + RC) for k in range(0, C, RC)]


def pipeline(parts, dots, elem, after=None):
    held = dots(parts[0])
    for i, k in enumerate(parts):
        ahead = dots(parts[i + 1]) if i + 1 < len(parts) else None
        elem(k, *held)
        if after is not None and i >= 1:
            after(parts[i - 1])
        held = ahead
    if after is not None:
        after(parts[-1])


MESH = pl.DeviceIdType.MESH
SZ, SP, SC, SD, SV, SN, SS, ST, SA, SB = range(10)


def scale_sizes(n):
    w = C // n
    fold = 128 // w
    return w, fold, 64 // fold


def pack(block, fold):
    rows = block.shape[0] // fold
    return jnp.concatenate([block[i * rows : (i + 1) * rows] for i in range(fold)], 1)


def unpack(block, fold):
    w = 128 // fold
    return jnp.concatenate([block[:, i * w : (i + 1) * w] for i in range(fold)], 0)


class Gather:
    def __init__(self, n, buf, sems):
        self.n, self.m, self.buf, self.sems = n, n // 2, buf, sems
        self.me = lax.axis_index("dp")
        self.chip, self.core = self.me // 2, self.me % 2
        self.pair = self.me + 1 - 2 * self.core

    def copy(self, slot, sem, target):
        return pltpu.make_async_remote_copy(
            src_ref=self.buf.at[slot],
            dst_ref=self.buf.at[slot],
            send_sem=self.sems.at[0, sem],
            recv_sem=self.sems.at[1, sem],
            device_id={"dp": target},
            device_id_type=MESH,
        )

    def peer(self, j):
        return lax.rem(self.chip + j, self.m) * 2 + self.core

    def start(self):
        for j in range(1, self.m):
            self.copy(self.me, j, self.peer(j)).start()
        self.copy(self.me, self.m, self.pair).start()

    def forward(self):
        for j in range(1, self.m):
            source = self.peer(j)
            self.copy(source, self.m - j, source).wait_recv()
            self.copy(source, self.m + j, self.pair).start()

    def finish(self):
        for j in range(self.m):
            self.copy(self.me, self.m + j, self.pair).wait_recv()
        for j in range(1, 2 * self.m):
            self.copy(self.me, j, self.pair).wait_send()


class Spread:
    def __init__(self, n, buf, sems):
        self.n, self.buf, self.sems, self.me = n, buf, sems, lax.axis_index("dp")

    def copy(self, j):
        return pltpu.make_async_remote_copy(
            src_ref=self.buf.at[self.me], dst_ref=self.buf.at[self.me],
            send_sem=self.sems.at[0, j], recv_sem=self.sems.at[1, j],
            device_id={"dp": lax.rem(self.me + j, self.n)}, device_id_type=MESH)

    def start(self):
        for j in range(1, self.n):
            self.copy(j).start()

    def finish(self):
        for j in range(1, self.n):
            self.copy(j).wait_recv()
        for j in range(1, self.n):
            self.copy(j).wait_send()


class Reduce:
    def __init__(self, n, pieces, source, from_pair, chipsum, from_chips, sems):
        self.n, self.m, self.pieces = n, n // 2, pieces
        self.rows = source.shape[1] // pieces
        self.source, self.from_pair, self.chipsum, self.from_chips, self.sems = source, from_pair, chipsum, from_chips, sems
        self.me = lax.axis_index("dp")
        self.chip, self.core = self.me // 2, self.me % 2
        self.pair = self.me + 1 - 2 * self.core

    def piece(self, p):
        return pl.ds(p * self.rows, self.rows)

    def swap_copy(self, k, sem):
        return pltpu.make_async_remote_copy(
            src_ref=self.source.at[2 * k + 1 - self.core], dst_ref=self.from_pair.at[k],
            send_sem=self.sems.at[0, sem], recv_sem=self.sems.at[1, sem],
            device_id={"dp": self.pair}, device_id_type=MESH)

    def chip_copy(self, slot, j, p, target):
        sem = self.m + p * self.m + j
        return pltpu.make_async_remote_copy(
            src_ref=self.chipsum.at[slot, self.piece(p)], dst_ref=self.from_chips.at[j, self.piece(p)],
            send_sem=self.sems.at[0, sem], recv_sem=self.sems.at[1, sem],
            device_id={"dp": target}, device_id_type=MESH)

    def start(self):
        for j in range(1, self.m + 1):
            self.swap_copy(lax.rem(self.chip + j, self.m), j % self.m).start()

    def forward(self):
        for p in range(self.pieces):
            for j in range(1, self.m):
                to = lax.rem(self.chip + j, self.m)
                if p == 0:
                    self.swap_copy(to, j).wait_recv()
                    self.chipsum[to] = self.source[2 * to + self.core] + self.from_pair[to]
                self.chip_copy(to, j, p, to * 2 + self.core).start()
        self.swap_copy(self.chip, 0).wait_recv()
        self.chipsum[self.chip] = self.source[self.me] + self.from_pair[self.chip]

    def finish(self, p):
        total = self.chipsum[self.chip, self.piece(p)]
        for j in range(1, self.m):
            self.chip_copy(self.chip, j, p, self.pair).wait_recv()
            total = total + self.from_chips[j, self.piece(p)]
        return total

    def drain(self):
        for k in range(self.m):
            self.swap_copy(k, k).wait_send()
        for p in range(self.pieces):
            for j in range(1, self.m):
                self.chip_copy(self.chip, j, p, self.pair).wait_send()


class Across:
    def __init__(self, groups, sems):
        self.groups, self.sems, self.grp = groups, sems, lax.axis_index("grp")

    def copy(self, src, dst, j, target):
        return pltpu.make_async_remote_copy(
            src_ref=src, dst_ref=dst, send_sem=self.sems.at[0, j], recv_sem=self.sems.at[1, j],
            device_id={"grp": target}, device_id_type=MESH)

    def others(self):
        return [(j, lax.rem(self.grp + j, self.groups)) for j in range(1, self.groups)]


def barrier(n, groups):
    me, grp = lax.axis_index("dp"), lax.axis_index("grp")
    sem = pltpu.get_barrier_semaphore()
    for j in range(1, n):
        pl.semaphore_signal(sem, inc=1, device_id={"dp": lax.rem(me + j, n)}, device_id_type=MESH)
    for j in range(1, groups):
        pl.semaphore_signal(sem, inc=1, device_id={"grp": lax.rem(grp + j, groups)}, device_id_type=MESH)
    pl.semaphore_wait(sem, n + groups - 2)


def match(counts, me, wanted_mine, wanted_theirs):
    zero = jnp.zeros((1, 128), f32)
    mine, my_rank = zero, zero
    for d in range(len(counts)):
        hit = jnp.where(counts[d] == wanted_mine, 1.0, 0.0)
        my_rank = my_rank + jnp.where(d < me, hit, zero)
        mine = mine + jnp.where(d == me, hit, zero)
    rank, masks = zero, []
    for d in range(len(counts)):
        hit = jnp.where(counts[d] == wanted_theirs, 1.0, 0.0)
        masks.append(jnp.where(rank == my_rank, hit * mine, zero))
        rank = rank + hit
    return masks


def adam(weight, gradient, first, second, rate):
    first = 0.9 * first + (1.0 - 0.9) * gradient
    second = 0.999 * second + (1.0 - 0.999) * gradient * gradient
    first_hat = first / (1.0 - 0.9**5.0)
    second_hat = second / (1.0 - 0.999**5.0)
    return weight - rate * (first_hat / (jnp.sqrt(second_hat) + 1e-8) + 0.01 * weight), first, second


def side_rate(w):
    return jnp.where(lax.broadcasted_iota(jnp.int32, (58, w), 0) >= 31, 0.004, 0.05)


def flip(tile):
    eye = lax.broadcasted_iota(jnp.int32, (8, 128), 0) == lax.broadcasted_iota(jnp.int32, (8, 128), 1)
    return lax.dot_general(tile, eye.astype(f32), (((0,), (0,)), ((), ())), precision=HIGH, preferred_element_type=f32)[0:8]


def spread_field(ref, base, small, at, b):
    for c in range(3):
        for k in range(8):
            small[at, b, c : c + 1, k * 128 : (k + 1) * 128] = ref[base + c, k : k + 1, :]


def fold_field(value, ref, base):
    for c in range(3):
        for k in range(8):
            ref[base + c, k : k + 1, :] = value[c : c + 1, k * 128 : (k + 1) * 128]


def main_kernel(n, groups, names, *refs):
    r = types.SimpleNamespace(**dict(zip(names, refs)))
    w, fold, side_rows = scale_sizes(n)
    m = n // 2
    me, grp = lax.axis_index("dp"), lax.axis_index("grp")
    counts, terms, tiny = r.counts, r.terms, r.tiny
    get_side = Gather(n, r.sides, r.sides_sem)
    get_third = Gather(n, r.thirds, r.thirds_sem)
    get_mid = Gather(n, r.mids, r.mids_sem)
    share = Gather(n, r.results, r.results_sem)
    share_flow = Gather(n, r.flows, r.flows_sem)
    r.sides[me] = pack(jnp.concatenate([r.side_w[:, 0, :], jnp.zeros((6, w), f32)], 0), fold)
    for at, ref in enumerate((r.images, r.probes, r.cots)):
        r.thirds[me, 3 * at : 3 * at + 3] = ref[6:9]
    lane = lax.broadcasted_iota(jnp.int32, (8, 128), 1)
    sub = lax.broadcasted_iota(jnp.int32, (8, 128), 0)
    own_count = jnp.broadcast_to(counts[0, 0].astype(f32), (1, 128))
    r.thirds[me, 9] = jnp.where(lane == 0, counts[0, 0].astype(f32), terms[0, 2].astype(f32))
    r.mids[me] = r.mid_w[...]
    barrier(n, groups)
    get_side.start()
    get_third.start()
    get_mid.start()
    small, side = r.small, r.side
    small[...] = jnp.zeros_like(small)
    for at, ref in ((SZ, r.images), (SP, r.probes), (SC, r.cots)):
        spread_field(ref, 0, small, at, 0)
    r.live[...] = jnp.where(terms[0, 0].astype(f32) > (sub % 4).astype(f32), 1.0, 0.0)
    bias_col = color_column([tiny[k, 0, 0] for k in range(3)])
    shift_col = color_column([tiny[k, 0, 1] for k in range(3)])
    scale_col = jnp.exp(color_column([tiny[k, 0, 2] for k in range(3)]))
    slope_raw = color_column([tiny[k, 0, 3] for k in range(3)])
    slope0 = 0.5 * softplus(slope_raw)

    def alive(b, step):
        return jnp.concatenate([r.live[b * 4 + step : b * 4 + step + 1, :]] * (PX // 128), 1)

    def prepare_image(b):
        masks = tap_masks()
        field = (small[SZ, b] + shift_col) * scale_col
        p = small[SP, b]
        small[SZ, b] = field
        x, t, e = pieces(field, slope0)
        d0 = 1.0 + t + x * e
        small[SD, b] = d0
        r.field[b] = expand(field + field * t, False, 1.0, masks)
        r.field[2 + b] = expand(d0 * p, False, 0.0, masks)
        r.field[4 + b] = expand(small[SC, b], True, 0.0, masks)
        r.field[6 + b] = expand(p, True, 0.0, masks)
        small[SV, b] = p
        small[SN, b] = -alive(b, 0) * p
        small[SS, b] = alive(b, 0) * p

    prepare_image(0)
    get_side.forward()
    get_side.finish()
    for i in range(fold):
        side[i * side_rows : (i + 1) * side_rows, :] = jnp.concatenate(
            [r.sides[d][:, i * w : (i + 1) * w] for d in range(n)], 1)
    lefts = r.lefts
    side1, side3 = prepare_side(side, lefts, [r.out_left[0, k] for k in range(3)], r.stage,
                                r.wa1, r.wp1, r.wa3, r.wp3, r.cols)
    wa1, wp1, wa3, wp3 = r.wa1, r.wp1, r.wa3, r.wp3
    mh, ml = r.mh, r.ml
    valid = lambda: lax.broadcasted_iota(jnp.int32, (8, PX), 0) < 3

    stages = []

    def stage(body):
        stages.append(body)
        pl.when(me + len(stages) > 0)(body)

    def doubled(index, k):
        block = r.field[index + k // PARTS, :, (k % PARTS) * TILE : (k % PARTS + 1) * TILE]
        return jnp.concatenate([block, block], 0)

    def column(which, rs):
        return jnp.concatenate([r.cols[which, rs]] * (TILE // 128), 1)

    one = (r.h1, r.g1, r.d1)
    two = (r.h2, r.g2, r.d2)

    def forward(kept, slope, bias, act, dact, k, h_all, dh_all):
        at = AT[k]
        hs, ys, ds = kept
        for rs in CHUNKS:
            h, dh = h_all[rs], dh_all[rs]
            if bias is not None:
                h = h + column(bias, rs)
            x = column(slope, rs) * h
            t = jnp.tanh(x)
            e = 1.0 - t * t
            d = 1.0 + t + x * e
            hs[rs, at] = h
            ds[rs, at] = d
            ys[rs, at] = e * (1.0 - x * t) * dh
            act[rs, at] = (h + h * t).astype(bf16)
            dact[rs, at] = (d * dh).astype(bf16)

    def backward(kept, slope, slope_to, bias_to, c_to, t_to, k, ca_all, ta_all):
        at = AT[k]
        hs, ys, ds = kept
        for rs in CHUNKS:
            h, d, c_a, t_a = hs[rs, at], ds[rs, at], ca_all[rs], ta_all[rs]
            sl = column(slope, rs)
            t = jnp.tanh(sl * h)
            he = h * (0.5 - 0.5 * (t * t))
            q = ys[rs, at] * t_a
            c_h = d * c_a + (sl + sl) * q
            grad = h * (c_a * he + q)
            gs, cs = grad[:, 0:128], c_h[:, 0:128]
            for j in range(1, TILE // 128):
                gs = gs + grad[:, j * 128 : (j + 1) * 128]
                if bias_to is not None:
                    cs = cs + c_h[:, j * 128 : (j + 1) * 128]
            r.sums[slope_to, rs] += gs
            if bias_to is not None:
                r.sums[bias_to, rs] += cs
            c_to[rs, at] = c_h.astype(bf16)
            t_to[rs, at] = (d * t_a).astype(bf16)

    def third_image():
        get_third.forward()
        get_third.finish()
        metas = [r.thirds[d, 9, 0:1, :] for d in range(n)]
        count_rows = [jnp.broadcast_to(meta[:, 0:1], (1, 128)) for meta in metas]
        masks = match(count_rows, me, 1.0, 3.0)
        helper, term = jnp.zeros((1, 128), f32), jnp.zeros((1, 128), f32) + terms[0, 1].astype(f32)
        for d in range(n):
            helper = helper + masks[d]
            term = jnp.where(masks[d] > 0.0, jnp.broadcast_to(metas[d][:, 1:2], (1, 128)), term)
        for at, ref in enumerate((r.images, r.probes, r.cots)):
            for c in range(3):
                picked = ref[3 + c]
                for d in range(n):
                    picked = jnp.where(masks[d] > 0.0, r.thirds[d, 3 * at + c], picked)
                r.picked[3 * at + c] = picked
        for at, place in ((0, SZ), (1, SP), (2, SC)):
            spread_field(r.picked, 3 * at, small, place, 1)
        r.live[...] = jnp.where(sub < 4, r.live[...], jnp.where(term > (sub % 4).astype(f32), 1.0, 0.0))

    def layer_one(b):
        @stage
        def _():
            pipeline([PARTS * b + k for k in range(PARTS)],
                     lambda k: (dot_tn(wa1[...], doubled(0, k)), dot_tn(wa1[...], doubled(2, k))),
                     functools.partial(forward, one, 0, None, r.a1, r.b1))
            for k in range(PARTS * b, PARTS * b + PARTS):
                r.ca[:, AT[k]] = dot_tn(wa3[...], doubled(4, k))
                r.c2[:, AT[k]] = dot_tn(wa3[...], doubled(6, k)).astype(bf16)

    layer_one(0)
    third_image()
    prepare_image(1)
    get_mid.forward()
    layer_one(1)
    get_mid.finish()
    q2, sigma2, right2 = prepare_mid(r.mids[...].reshape(C, C), lefts, mh, ml, r.left2)
    r.sums[...] = jnp.zeros_like(r.sums)

    @stage
    def layer_two():
        masks = tap_masks()

        def dots(k):
            a1 = r.a1[:, AT[k]]
            return dot_tn(mh[...], a1) + dot_tn(ml[...], a1), dot_tn(mh[...], r.b1[:, AT[k]])

        def after(k):
            to = slice((k % PARTS) * TILE, (k % PARTS + 1) * TILE)
            r.prod[0, :, to] = dot_nn(wp3[...], r.a2[:, AT[k]])
            r.prod[1, :, to] = dot_nn(wp3[...], r.b2[:, AT[k]])
            if k % PARTS == PARTS - 1:
                b = k // PARTS
                flow = small[SZ, b] + collapse(r.prod[0], False, masks) + bias_col
                fold_field(flow, r.firsts if b == 0 else r.flows.at[me], 0)
                small[ST, b] = jnp.where(valid(), collapse(r.prod[1], False, masks), 0.0)

        pipeline(range(2 * PARTS), dots, functools.partial(forward, two, 2, 1, r.a2, r.b2), after)

    share_flow.start()

    @stage
    def pulls():
        masks = tap_masks()
        v = [None, None]

        def first(b):
            if v[b] is None:
                r.c2[:, IM[b]] = (r.c2[:, IM[b]].astype(f32) * r.d2[:, IM[b]]).astype(bf16)
                return
            spread = expand(v[b], True, 0.0, masks)
            r.c2[:, IM[b]] = (dot_tn(wa3[...], jnp.concatenate([spread, spread], 0)) * r.d2[:, IM[b]]).astype(bf16)

        def second(b):
            r.t2[:, IM[b]] = (dot_nn(mh[...], r.c2[:, IM[b]]) * r.d1[:, IM[b]]).astype(bf16)

        def third(b, step):
            sign = (-1.0) ** step
            prod = dot_nn(wp1[...], r.t2[:, IM[b]])
            v[b] = jnp.where(valid(), small[SD, b] * collapse(prod, True, masks), 0.0)
            on = sign * alive(b, step)
            small[SN, b] = small[SN, b] - on * v[b]
            small[SS, b] = small[SS, b] + (on / (step + 1.0)) * v[b]

        first(0)
        second(0)
        first(1)
        third(0, 1)
        second(1)
        for step in (2, 3):
            first(0)
            third(1, step - 1)
            second(0)
            first(1)
            third(0, step)
            second(1)
        third(1, 3)

    share_flow.forward()

    @stage
    def back_two():
        masks = tap_masks()
        for b in range(2):
            r.field[6 + b] = expand(small[SN, b], True, 0.0, masks)
        pipeline(range(2 * PARTS), lambda k: (r.ca[:, AT[k]], dot_tn(wa3[...], doubled(6, k))),
                 functools.partial(backward, two, 2, 1, 0, r.c2, r.t2))

    raw = dot_nt(r.a1[...], r.c2[...]) + dot_nt(r.b1[...], r.t2[...])
    g3 = dot_nt(r.field[4], r.a2[:, 0:PX]) + dot_nt(r.field[6], r.b2[:, 0:PX])
    g3 = g3 + dot_nt(r.field[5], r.a2[:, PX:]) + dot_nt(r.field[7], r.b2[:, PX:])
    straight, across = correction(raw, r.mids[...].reshape(C, C), q2, sigma2)
    r.dmid[...] = (straight * raw + (across * right2) * r.left2[0:1, :]).reshape(n, w, C)
    sum_mid = Reduce(n, w // 16, r.dmid, r.mid_pair, r.mid_chip, r.mid_chips, r.mid_sem)
    sum_mid.start()
    ones = jnp.ones((8, 128), f32)
    row_of = lambda acc: lax.dot_general(
        ones, acc, (((1,), (1,)), ((), ())), precision=HIGH, preferred_element_type=f32)[0:1]
    dside = r.dside

    def put_taps(at, norm, grad, start):
        q, sigma, outer = norm
        row80 = lax.broadcasted_iota(jnp.int32, (80, C), 0)
        joined = jnp.where((row80 % 8 < 3) & (row80 < 72), grad + pltpu.roll(grad, 77, 0), 0.0)
        straight, across = correction(joined, r.stage[at], q, sigma)
        r.stage2[at] = straight * joined + across * outer
        for color in range(3):
            for tap in range(9):
                to = start + 9 * color + tap
                dside[to : to + 1, :] = r.stage2[at, 8 * tap + color : 8 * tap + color + 1, :]

    dside[29:30, :] = row_of(r.sums[0])
    dside[30:31, :] = row_of(r.sums[1]) * sigmoid(side[30:31, :])
    dside[58:64, :] = jnp.zeros((6, C), f32)
    put_taps(1, side3, g3, 31)
    sum_mid.forward()

    @stage
    def back_one():
        masks = tap_masks()

        def dots(k):
            c2 = r.c2[:, AT[k]]
            return dot_nn(mh[...], c2) + dot_nn(ml[...], c2), dot_nn(mh[...], r.t2[:, AT[k]])

        def after(k):
            to = slice((k % PARTS) * TILE, (k % PARTS + 1) * TILE)
            r.prod[0, :, to] = dot_nn(wp1[...], r.a2[:, AT[k]])
            r.prod[1, :, to] = dot_nn(wp1[...], r.b2[:, AT[k]])
            if k % PARTS == PARTS - 1:
                small[SA, k // PARTS] = collapse(r.prod[0], True, masks)
                small[SB, k // PARTS] = collapse(r.prod[1], True, masks)

        pipeline(range(2 * PARTS), dots, functools.partial(backward, one, 0, 2, None, r.a2, r.b2), after)

    g1 = dot_nt(r.field[0], r.a2[:, 0:PX]) + dot_nt(r.field[2], r.b2[:, 0:PX])
    g1 = g1 + dot_nt(r.field[1], r.a2[:, PX:]) + dot_nt(r.field[3], r.b2[:, PX:])
    dside[27:28, :] = g1[38:39]
    dside[28:29, :] = row_of(r.sums[2]) * sigmoid(side[28:29, :])
    put_taps(0, side1, g1, 0)
    for d in range(n):
        r.side_blocks[d] = pack(dside[:, d * w : (d + 1) * w], fold)
    sum_side = Reduce(n, 1, r.side_blocks, r.side_pair, r.side_chip, r.side_chips, r.side_sem)
    sum_side.start()
    total_scale = tiny[0, 0, 2] + tiny[1, 0, 2] + tiny[2, 0, 2]
    tile = jnp.where(lane == 5, counts[0, 0].astype(f32), 0.0)
    for b in range(2):
        field, p, cot = small[SZ, b], small[SP, b], small[SC, b]
        c_a, t_a = small[SA, b], small[SB, b]
        x, t, e = pieces(field, slope0)
        q = 2.0 * e * (1.0 - x * t) * p * t_a
        c_z = jnp.where(valid(), cot + (1.0 + t + x * e) * c_a + slope0 * q, 0.0)
        slope_grad = jnp.where(valid(), field * (c_a * field * e + q), 0.0)
        fold_field(c_z * scale_col, r.firsts if b == 0 else r.results.at[me], 3 if b == 0 else 0)
        sums = [
            jnp.sum(cot, axis=1, keepdims=True),
            jnp.sum(c_z, axis=1, keepdims=True) * scale_col,
            jnp.sum(c_z * field, axis=1, keepdims=True) - 1024.0,
            jnp.sum(slope_grad, axis=1, keepdims=True) * (0.5 * sigmoid(slope_raw)),
        ]
        for k in range(4):
            tile = tile + jnp.where((lane == k) & (sub < 3), sums[k], 0.0)
        log_part = (1024.0 * total_scale + jnp.sum(small[SS, b] * small[ST, b])) / 3072.0
        tile = tile + jnp.where((lane == 4) & (sub == b), log_part, 0.0)
    r.tiny_tiles[me] = tile
    spread = Spread(n, r.tiny_tiles, r.tiny_tiles_sem)
    sum_side.forward()
    spread.start()
    share.start()
    ring1 = Across(groups, r.ring1_sem)
    ring3, ring4 = Across(groups, r.ring3_sem), Across(groups, r.ring4_sem)
    cuts = w // 16

    def mid_copy(p, j, to):
        rows = pl.ds(16 * p, 16)
        return ring1.copy(r.mid_diff.at[grp, rows], r.mid_diff.at[grp, rows], p * groups + j, to)

    for p in range(cuts):
        rows = slice(16 * p, 16 * p + 16)
        mid_grad = sum_mid.finish(p) / (2.0 * n)
        r.mid_g[rows] = mid_grad
        r.mid_diff[grp, rows] = r.mid_o[rows] - adam(r.mid_w[rows], mid_grad, r.mid_f[rows], r.mid_s[rows], 0.01)[0]
        for j, to in ring1.others():
            mid_copy(p, j, to).start()
    side_grad = unpack(sum_side.finish(0), fold)[0:58] / (2.0 * n)
    r.side_g[...] = side_grad
    new = adam(r.side_w[:, 0, :], side_grad, r.side_f[:, 0, :], r.side_s[:, 0, :], side_rate(w))[0]
    r.side_diff[grp] = pack(jnp.concatenate([r.side_o[...] - new, jnp.zeros((6, w), f32)], 0), fold)
    for j, to in ring3.others():
        ring3.copy(r.side_diff.at[grp], r.side_diff.at[grp], j, to).start()
    spread.finish()
    tiny_sum = r.tiny_tiles[0]
    for d in range(1, n):
        tiny_sum = tiny_sum + r.tiny_tiles[d]
    r.out_small[0] = tiny_sum
    r.tiles[...] = jnp.zeros_like(r.tiles)
    for c in range(3):
        for k, ref in enumerate((r.tiny_w, r.tiny_f, r.tiny_s)):
            r.tiles[k, c : c + 1, 0:4] = ref[c, 0:1, :]
    r.tiles[3, 0:4, 0:3] = r.tiny_o[...]
    new = adam(r.tiles[0], tiny_sum / (2.0 * n), r.tiles[1], r.tiles[2], 0.05)[0]
    r.tiny_diff[grp] = r.tiles[3] - flip(jnp.where(lane < 4, new, 0.0))
    for j, to in ring4.others():
        ring4.copy(r.tiny_diff.at[grp], r.tiny_diff.at[grp], j, to).start()
    share.forward()
    tiles = [r.tiny_tiles[d] for d in range(n)]
    masks = match([jnp.broadcast_to(t[0:1, 5:6], (1, 128)) for t in tiles], me, 3.0, 1.0)
    log_third = jnp.zeros((1, 128), f32)
    for d in range(n):
        log_third = jnp.where(masks[d] > 0.0, jnp.broadcast_to(tiles[d][1:2, 4:5], (1, 128)), log_third)
    share_flow.finish()
    share.finish()
    for out, ref, base in ((r.out_flow, r.flows, 0), (r.out_back, r.results, 3)):
        for c in range(3):
            picked = jnp.zeros((8, 128), f32)
            for d in range(n):
                picked = jnp.where(masks[d] > 0.0, ref[d, c], picked)
            out[c] = r.firsts[base + c]
            out[3 + c] = jnp.where(own_count > 1.5, ref[me, c], 0.0)
            out[6 + c] = picked
    logs = [jnp.broadcast_to(tile[b : b + 1, 4:5], (1, 128)) for b in range(2)]
    logs[1] = jnp.where(own_count > 1.5, logs[1], 0.0)
    row_lane = lax.broadcasted_iota(jnp.int32, (1, 128), 1)
    r.out_small[1] = jnp.broadcast_to(
        jnp.where(row_lane == 0, logs[0], jnp.where(row_lane == 1, logs[1], log_third)), (8, 128))
    for j, to in ring3.others():
        ring3.copy(r.side_diff.at[grp], r.side_diff.at[grp], j, to).wait_recv()
    total = r.side_diff[0]
    for k in range(1, groups):
        total = total + r.side_diff[k]
    r.side_t[...] = unpack(total, fold)[0:58]
    for j, to in ring4.others():
        ring4.copy(r.tiny_diff.at[grp], r.tiny_diff.at[grp], j, to).wait_recv()
    total = r.tiny_diff[0]
    for k in range(1, groups):
        total = total + r.tiny_diff[k]
    r.out_small[2] = total
    for p in range(cuts):
        rows = slice(16 * p, 16 * p + 16)
        for j, to in ring1.others():
            mid_copy(p, j, to).wait_recv()
        total = r.mid_diff[0, rows]
        for k in range(1, groups):
            total = total + r.mid_diff[k, rows]
        r.mid_t[rows] = total
    sum_mid.drain()
    sum_side.drain()
    for p in range(cuts):
        for j, to in ring1.others():
            mid_copy(p, j, to).wait_send()
    for j, to in ring3.others():
        ring3.copy(r.side_diff.at[grp], r.side_diff.at[grp], j, to).wait_send()
    for j, to in ring4.others():
        ring4.copy(r.tiny_diff.at[grp], r.tiny_diff.at[grp], j, to).wait_send()


def last_kernel(n, groups, names, *refs):
    r = types.SimpleNamespace(**dict(zip(names, refs)))
    w = C // n
    lane = lax.broadcasted_iota(jnp.int32, (8, 128), 1)
    r.flow_o[...] = r.flow[...]
    r.back_o[...] = r.back[...]
    r.log_det[...] = r.small[1, 0:1, 0:3]
    tiny_sum = r.small[0]
    r.log_mean[...] = (tiny_sum[0:1, 4:5] + tiny_sum[1:2, 4:5]) / (2.0 * n)
    new, first, second = adam(r.mid_w[...], r.mid_g[...], r.mid_f[...], r.mid_s[...], 0.01)
    r.mid_f_new[...], r.mid_s_new[...], r.mid_new[...] = first, second, new
    new, first, second = adam(r.side_w[:, 0, :], r.side_g[...], r.side_f[:, 0, :], r.side_s[:, 0, :], side_rate(w))
    r.side_f_new[:, 0, :], r.side_s_new[:, 0, :], r.side_new[:, 0, :] = first, second, new
    r.tiles[...] = jnp.zeros_like(r.tiles)
    for c in range(3):
        for k, ref in enumerate((r.tiny_w, r.tiny_f, r.tiny_s)):
            r.tiles[k, c : c + 1, 0:4] = ref[c, 0:1, :]
    new, first, second = adam(r.tiles[0], tiny_sum / (2.0 * n), r.tiles[1], r.tiles[2], 0.05)
    for c in range(3):
        r.tiny_f_new[c, 0:1, :] = first[c : c + 1, 0:4]
        r.tiny_new[c, 0:1, :] = new[c : c + 1, 0:4]
    turned = flip(jnp.where(lane < 4, second, 0.0))
    for k in range(3):
        r.tiny_s_new[k, 0:1, :] = turned[k : k + 1, 0:3]
    r.slope_s_new[...] = turned[3:4, 0:3]

    def outer(diff, old, momentum, delta_out, momentum_out, out):
        delta = diff / groups
        mom = 0.9 * momentum[...] + delta
        delta_out[...], momentum_out[...] = delta, mom
        out[...] = old[...] - 0.7 * (delta + 0.9 * mom)

    outer(r.mid_t[...], r.mid_o, r.mid_m, r.mid_d, r.mid_m_new, r.mid_o_new)
    outer(r.side_t[...], r.side_o, r.side_m, r.side_d, r.side_m_new, r.side_o_new)
    outer(r.small[2, 0:4, 0:3], r.tiny_o, r.tiny_m, r.tiny_d, r.tiny_m_new, r.tiny_o_new)


def on_device(images, probes, out_cotangent, counts, terms, power_left, power_out, mid_weight, mid_first, mid_second,
              side_weight, side_first, side_second, tiny_weight, tiny_first, tiny_second,
              mid_outer, mid_momentum, side_outer, side_momentum, tiny_outer, tiny_momentum):
    n, groups = lax.axis_size("dp"), lax.axis_size("grp")
    w, fold, side_rows = scale_sizes(n)
    m = n // 2
    vm = pl.BlockSpec(memory_space=pltpu.VMEM)
    sm = pl.BlockSpec(memory_space=pltpu.SMEM)
    sd = lambda *shape: jax.ShapeDtypeStruct(shape, f32)
    dma = lambda *shape: pltpu.SemaphoreType.DMA(shape)
    vmem = lambda *shape: pltpu.VMEM(shape, f32)
    big = lambda dtype: pltpu.VMEM((C, 2 * PX), dtype)
    half = lambda *shape: pltpu.VMEM(shape, bf16)
    image = lambda x: x[0].reshape(9, 8, 128)
    turn = lambda x: jnp.swapaxes(x, -1, -2)
    row = lambda x: x[0][:, None, :]
    color = lambda x: jnp.transpose(x, (2, 0, 1))
    state = dict(
        mid_w=turn(mid_weight[0]), mid_f=turn(mid_first[0]), mid_s=turn(mid_second[0]), mid_o=turn(mid_outer),
        side_w=row(side_weight), side_f=row(side_first), side_s=row(side_second), side_o=side_outer,
        tiny_w=color(tiny_weight), tiny_f=color(tiny_first), tiny_s=color(tiny_second), tiny_o=tiny_outer,
    )
    vmem_in = dict(images=image(images), probes=image(probes), cots=image(out_cotangent), lefts=power_left[0], **state)
    smem_in = dict(counts=counts, terms=terms, out_left=power_out, tiny=color(tiny_weight))
    outs = dict(out_flow=sd(9, 8, 128), out_back=sd(9, 8, 128), out_small=sd(3, 8, 128), mid_g=sd(w, C), mid_t=sd(w, C),
                side_g=sd(58, w), side_t=sd(58, w))
    scratch = dict(
        stage=vmem(2, 80, C), stage2=vmem(2, 80, C), wa1=half(160, C), wp1=half(80, C), wa3=half(160, C), wp3=half(80, C),
        cols=vmem(3, C, 128), small=vmem(10, 2, 8, PX), sums=vmem(3, C, 128), field=half(8, 80, PX), prod=vmem(2, 80, PX),
        mh=half(C, C), ml=half(C, C), left2=vmem(8, C), live=vmem(8, 128), side=vmem(64, C),
        h1=big(f32), g1=big(f32), h2=big(f32), g2=big(f32),
        d1=big(f32), a1=big(bf16), b1=big(bf16), d2=big(f32), a2=big(bf16), b2=big(bf16), c2=big(bf16), t2=big(bf16),
        ca=big(f32), sides=vmem(n, side_rows, 128), thirds=vmem(n, 10, 8, 128), mids=vmem(n, w, C), results=vmem(n, 3, 8, 128), tiny_tiles=vmem(n, 8, 128), tiny_tiles_sem=dma(2, n), flows=vmem(n, 3, 8, 128), flows_sem=dma(2, n),
        picked=vmem(9, 8, 128), firsts=vmem(6, 8, 128), dmid=vmem(n, w, C), dside=vmem(64, C),
        side_blocks=vmem(n, side_rows, 128),
        mid_pair=vmem(m, w, C), mid_chip=vmem(m, w, C), mid_chips=vmem(m, w, C),
        side_pair=vmem(m, side_rows, 128), side_chip=vmem(m, side_rows, 128), side_chips=vmem(m, side_rows, 128),
        mid_diff=vmem(groups, w, C),
        side_diff=vmem(groups, side_rows, 128), tiny_diff=vmem(groups, 8, 128), tiles=vmem(4, 8, 128),
        sides_sem=dma(2, n), thirds_sem=dma(2, n), mids_sem=dma(2, n), results_sem=dma(2, n),
        mid_sem=dma(2, m * (1 + w // 16)), side_sem=dma(2, n),
        ring1_sem=dma(2, groups * (w // 16)), ring3_sem=dma(2, groups), ring4_sem=dma(2, groups),
    )
    ins = {**vmem_in, **smem_in}
    made = pl.pallas_call(
        functools.partial(main_kernel, n, groups, list(ins) + list(outs) + list(scratch)),
        in_specs=[vm] * len(vmem_in) + [sm] * len(smem_in),
        out_specs=[vm] * len(outs),
        out_shape=list(outs.values()),
        scratch_shapes=list(scratch.values()),
        compiler_params=pltpu.CompilerParams(vmem_limit_bytes=60 << 20, collective_id=0, has_side_effects=True),
    )(*ins.values())
    flow, back, small, mid_g, mid_t, side_g, side_t = made
    ins = dict(flow=flow, back=back, small=small, mid_g=mid_g, mid_t=mid_t, side_g=side_g, side_t=side_t, **state)
    ins.update(mid_m=turn(mid_momentum), side_m=side_momentum, tiny_m=tiny_momentum)
    scratch = dict(tiles=vmem(3, 8, 128))
    outs = dict(
        flow_o=sd(9, 8, 128), back_o=sd(9, 8, 128), log_det=sd(1, 3), log_mean=sd(1, 1),
        mid_f_new=sd(w, C), mid_s_new=sd(w, C), mid_new=sd(w, C),
        side_f_new=sd(58, 1, w), side_s_new=sd(58, 1, w), side_new=sd(58, 1, w),
        tiny_f_new=sd(3, 1, 4), tiny_s_new=sd(3, 1, 3), slope_s_new=sd(1, 3), tiny_new=sd(3, 1, 4),
        mid_d=sd(w, C), mid_m_new=sd(w, C), mid_o_new=sd(w, C),
        side_d=sd(58, w), side_m_new=sd(58, w), side_o_new=sd(58, w),
        tiny_d=sd(4, 3), tiny_m_new=sd(4, 3), tiny_o_new=sd(4, 3),
    )
    made = pl.pallas_call(
        functools.partial(last_kernel, n, groups, list(ins) + list(outs) + list(scratch)),
        in_specs=[vm] * len(ins),
        out_specs=[vm] * len(outs),
        out_shape=list(outs.values()),
        scratch_shapes=list(scratch.values()),
        compiler_params=pltpu.CompilerParams(vmem_limit_bytes=60 << 20),
    )(*ins.values())
    o = types.SimpleNamespace(**dict(zip(outs, made)))
    whole = lambda x: x.reshape(1, 3, 3, PX)
    back_turn = lambda x: turn(x)[None]
    return (
        whole(o.flow_o), whole(o.back_o), o.log_det, o.log_mean.reshape(1),
        back_turn(o.mid_f_new), back_turn(o.mid_s_new), back_turn(o.mid_new),
        o.side_f_new[:, 0][None], o.side_s_new[:, 0][None], o.side_new[:, 0][None],
        jnp.transpose(o.tiny_f_new, (1, 2, 0)), jnp.transpose(o.tiny_s_new, (1, 0, 2)), o.slope_s_new, jnp.transpose(o.tiny_new, (1, 2, 0)),
        turn(o.mid_d), turn(o.mid_m_new), turn(o.mid_o_new),
        o.side_d, o.side_m_new, o.side_o_new, o.tiny_d, o.tiny_m_new, o.tiny_o_new,
    )


def solution(mesh):
    split = P("grp", None, "dp")
    group = P("grp", None, None)
    image = P("grp", "dp", None, None)
    return jax.shard_map(
        on_device,
        mesh=mesh,
        in_specs=(image, image, image, P("grp", "dp"), P("grp", "dp"), group, P("grp", None),
                  split, split, split, split, split, split, group, group, group,
                  P(None, "dp"), P(None, "dp"), P(None, "dp"), P(None, "dp"), P(), P()),
        out_specs=(image, image, P("grp", "dp"), P("grp"), split, split, split, split, split, split,
                   group, group, P("grp", None), group) + (P(None, "dp"),) * 6 + (P(), P(), P()),
        check_vma=False,
    )
```

```python
import functools
import types

import jax, jax.numpy as jnp
from jax import lax
from jax.experimental import pallas as pl
from jax.experimental.pallas import tpu as pltpu
from jax.sharding import PartitionSpec as P

bf16, f32 = jnp.bfloat16, jnp.float32
HIGH = lax.Precision.HIGHEST
C, PX, TILE = 512, 1024, 512
CLIP = 0.98
LIP = 2.2


def dot_nn(a, b):
    return jnp.dot(a, b, preferred_element_type=f32)


def dot_tn(a, b):
    return lax.dot_general(a, b, (((0,), (0,)), ((), ())), preferred_element_type=f32)


def dot_nt(a, b):
    return lax.dot_general(a, b, (((1,), (1,)), ((), ())), preferred_element_type=f32)


def tap_masks():
    lane = lax.broadcasted_iota(jnp.int32, (8, PX), 1)
    row, col = lane // 32, lane % 32
    masks = []
    for tap in range(9):
        down, right = tap // 3 - 1, tap % 3 - 1
        ok = (row + down >= 0) & (row + down < 32) & (col + right >= 0) & (col + right < 32)
        masks.append(ok)
    return masks


def shift(field, tap, masks):
    if tap == 4:
        return field
    offset = (tap // 3 - 1) * 32 + tap % 3 - 1
    return jnp.where(masks[tap], pltpu.roll(field, (-offset) % PX, 1), 0.0)


def expand(field, flip, one, masks):
    high = field.astype(bf16).astype(f32)
    low = field - high
    row = lax.broadcasted_iota(jnp.int32, (8, PX), 0)
    base = jnp.where(row < 3, high, jnp.where(row < 6, pltpu.roll(low, 3, 0), one))
    parts = [shift(base, 8 - tap if flip else tap, masks) for tap in range(9)]
    return jnp.concatenate(parts + [jnp.zeros((8, PX), f32)], 0).astype(bf16)


def collapse(prod, flip, masks):
    total = prod[32:40]
    for tap in (0, 1, 2, 3, 5, 6, 7, 8):
        total = total + shift(prod[8 * tap : 8 * tap + 8], 8 - tap if flip else tap, masks)
    return total + pltpu.roll(total, 5, 0)


def pieces(h, slope_half):
    x = slope_half * h
    t = jnp.tanh(x)
    e = 1.0 - t * t
    return x, t, e


def softplus(raw):
    return jnp.maximum(raw, 0.0) + jnp.log1p(jnp.exp(-jnp.abs(raw)))


def sigmoid(raw):
    return 1.0 / (1.0 + jnp.exp(-raw))


def wide(ref, width):
    block = ref[...]
    return jnp.concatenate([block] * (width // 128), 1)


def to_column(row):
    return jnp.transpose(jnp.broadcast_to(row, (128, C)))


def prepare_side(side, lefts, out_left, stage, wa1, wp1, wa3, wp3, cols):
    rows = lax.broadcasted_iota(jnp.int32, (80, C), 0)
    stage[...] = jnp.zeros_like(stage)
    for color in range(3):
        for tap in range(9):
            stage[0, 8 * tap + color : 8 * tap + color + 1, :] = side[9 * color + tap : 9 * color + tap + 1, :]
            at = 31 + 9 * color + tap
            stage[1, 8 * tap + color : 8 * tap + color + 1, :] = side[at : at + 1, :]
    first = stage[0]
    u = lefts[0:1, :]
    right1 = jnp.sum(first * u, axis=1, keepdims=True)
    right1 = right1 / jnp.sqrt(jnp.sum(right1 * right1) + 1e-12)
    y1 = jnp.sum(first * right1, axis=0, keepdims=True)
    left1 = y1 / jnp.sqrt(jnp.sum(y1 * y1) + 1e-12)
    sigma1 = jnp.sum(left1 * y1)
    last = stage[1]
    inner = rows % 8
    weight = jnp.where(inner == 0, out_left[0], jnp.where(inner == 1, out_left[1], out_left[2]))
    mixed = jnp.where(inner < 3, last * weight, 0.0)
    right3 = mixed + pltpu.roll(mixed, 79, 0) + pltpu.roll(mixed, 78, 0)
    right3 = jnp.where(inner == 0, right3, 0.0)
    right3 = right3 / jnp.sqrt(jnp.sum(right3 * right3) + 1e-12)
    right3 = right3 + pltpu.roll(right3, 1, 0) + pltpu.roll(right3, 2, 0)
    prod = last * right3
    y3 = [jnp.sum(jnp.where(inner == k, prod, 0.0)) for k in range(3)]
    norm3 = jnp.sqrt(y3[0] * y3[0] + y3[1] * y3[1] + y3[2] * y3[2] + 1e-12)
    left3 = [value / norm3 for value in y3]
    sigma3 = left3[0] * y3[0] + left3[1] * y3[1] + left3[2] * y3[2]
    outer3 = jnp.where(inner == 0, left3[0], jnp.where(inner == 1, left3[1], left3[2])) * right3
    outer1 = right1 * left1
    q1, q3 = jnp.maximum(1.0, sigma1 / CLIP), jnp.maximum(1.0, sigma3 / CLIP)
    for at, q, wa, wp in ((0, q1, wa1, wp1), (1, q3, wa3, wp3)):
        scaled = stage[at] / (LIP * q)
        high = scaled.astype(bf16).astype(f32)
        low = scaled - high
        top = high + pltpu.roll(high, 3, 0)
        if at == 0:
            bias = side[27:28, :]
            bias_high = bias.astype(bf16).astype(f32)
            top = jnp.where(rows == 38, bias_high, jnp.where(rows == 39, bias - bias_high, top))
        wa[0:80, :] = top.astype(bf16)
        wa[80:160, :] = (low + pltpu.roll(low, 3, 0)).astype(bf16)
        wp[...] = (high + pltpu.roll(low, 3, 0)).astype(bf16)
    cols[0] = to_column(0.5 * softplus(side[28:29, :]))
    cols[1] = to_column(side[29:30, :])
    cols[2] = to_column(0.5 * softplus(side[30:31, :]))
    return (q1, sigma1, outer1), (q3, sigma3, outer3)


def prepare_mid(mid, lefts, m_high, m_low, outer):
    right = jnp.sum(mid * lefts[1:2, :], axis=1, keepdims=True)
    right = right / jnp.sqrt(jnp.sum(right * right) + 1e-12)
    y = jnp.sum(mid * right, axis=0, keepdims=True)
    left = y / jnp.sqrt(jnp.sum(y * y) + 1e-12)
    sigma = jnp.sum(left * y)
    q = jnp.maximum(1.0, sigma / CLIP)
    scaled = mid / (LIP * q)
    high = scaled.astype(bf16)
    m_high[...] = high
    m_low[...] = (scaled - high.astype(f32)).astype(bf16)
    outer[0:8, :] = jnp.broadcast_to(left, (8, C))
    return q, sigma, right


def correction(raw_grad, weight, q, sigma):
    ratio = sigma / CLIP
    active = jnp.where(ratio > 1.0, 1.0, jnp.where(ratio == 1.0, 0.5, 0.0))
    return 1.0 / (LIP * q), -active * jnp.sum(raw_grad * weight) / (LIP * q * q * CLIP)


def color_column(values):
    row = lax.broadcasted_iota(jnp.int32, (8, 1), 0)
    return jnp.where(row == 0, values[0], jnp.where(row == 1, values[1], values[2]))


PARTS = PX // TILE
RC = 32
AT = [slice(k * TILE, (k + 1) * TILE) for k in range(2 * PARTS)]
IM = (slice(0, PX), slice(PX, 2 * PX))
CHUNKS = [slice(k, k + RC) for k in range(0, C, RC)]


def pipeline(parts, dots, elem, after=None):
    held = dots(parts[0])
    for i, k in enumerate(parts):
        ahead = dots(parts[i + 1]) if i + 1 < len(parts) else None
        elem(k, *held)
        if after is not None and i >= 1:
            after(parts[i - 1])
        held = ahead
    if after is not None:
        after(parts[-1])


MESH = pl.DeviceIdType.MESH
SZ, SP, SC, SD, SV, SN, SS, ST, SA, SB = range(10)


def scale_sizes(n):
    w = C // n
    fold = 128 // w
    return w, fold, 64 // fold


def pack(block, fold):
    rows = block.shape[0] // fold
    return jnp.concatenate([block[i * rows : (i + 1) * rows] for i in range(fold)], 1)


def unpack(block, fold):
    w = 128 // fold
    return jnp.concatenate([block[:, i * w : (i + 1) * w] for i in range(fold)], 0)


class Gather:
    def __init__(self, n, buf, sems):
        self.n, self.m, self.buf, self.sems = n, n // 2, buf, sems
        self.me = lax.axis_index("dp")
        self.chip, self.core = self.me // 2, self.me % 2
        self.pair = self.me + 1 - 2 * self.core

    def copy(self, slot, sem, target):
        return pltpu.make_async_remote_copy(
            src_ref=self.buf.at[slot],
            dst_ref=self.buf.at[slot],
            send_sem=self.sems.at[0, sem],
            recv_sem=self.sems.at[1, sem],
            device_id={"dp": target},
            device_id_type=MESH,
        )

    def peer(self, j):
        return lax.rem(self.chip + j, self.m) * 2 + self.core

    def start(self):
        for j in range(1, self.m):
            self.copy(self.me, j, self.peer(j)).start()
        self.copy(self.me, self.m, self.pair).start()

    def forward(self):
        for j in range(1, self.m):
            source = self.peer(j)
            self.copy(source, self.m - j, source).wait_recv()
            self.copy(source, self.m + j, self.pair).start()

    def finish(self):
        for j in range(self.m):
            self.copy(self.me, self.m + j, self.pair).wait_recv()
        for j in range(1, 2 * self.m):
            self.copy(self.me, j, self.pair).wait_send()


class Spread:
    def __init__(self, n, buf, sems):
        self.n, self.buf, self.sems, self.me = n, buf, sems, lax.axis_index("dp")

    def copy(self, j):
        return pltpu.make_async_remote_copy(
            src_ref=self.buf.at[self.me], dst_ref=self.buf.at[self.me],
            send_sem=self.sems.at[0, j], recv_sem=self.sems.at[1, j],
            device_id={"dp": lax.rem(self.me + j, self.n)}, device_id_type=MESH)

    def start(self):
        for j in range(1, self.n):
            self.copy(j).start()

    def finish(self):
        for j in range(1, self.n):
            self.copy(j).wait_recv()
        for j in range(1, self.n):
            self.copy(j).wait_send()


class Reduce:
    def __init__(self, n, pieces, source, from_pair, chipsum, from_chips, sems):
        self.n, self.m, self.pieces = n, n // 2, pieces
        self.rows = source.shape[1] // pieces
        self.source, self.from_pair, self.chipsum, self.from_chips, self.sems = source, from_pair, chipsum, from_chips, sems
        self.me = lax.axis_index("dp")
        self.chip, self.core = self.me // 2, self.me % 2
        self.pair = self.me + 1 - 2 * self.core

    def piece(self, p):
        return pl.ds(p * self.rows, self.rows)

    def swap_copy(self, k, sem):
        return pltpu.make_async_remote_copy(
            src_ref=self.source.at[2 * k + 1 - self.core], dst_ref=self.from_pair.at[k],
            send_sem=self.sems.at[0, sem], recv_sem=self.sems.at[1, sem],
            device_id={"dp": self.pair}, device_id_type=MESH)

    def chip_copy(self, slot, j, p, target):
        sem = self.m + p * self.m + j
        return pltpu.make_async_remote_copy(
            src_ref=self.chipsum.at[slot, self.piece(p)], dst_ref=self.from_chips.at[j, self.piece(p)],
            send_sem=self.sems.at[0, sem], recv_sem=self.sems.at[1, sem],
            device_id={"dp": target}, device_id_type=MESH)

    def start(self):
        for j in range(1, self.m + 1):
            self.swap_copy(lax.rem(self.chip + j, self.m), j % self.m).start()

    def forward(self):
        for p in range(self.pieces):
            for j in range(1, self.m):
                to = lax.rem(self.chip + j, self.m)
                if p == 0:
                    self.swap_copy(to, j).wait_recv()
                    self.chipsum[to] = self.source[2 * to + self.core] + self.from_pair[to]
                self.chip_copy(to, j, p, to * 2 + self.core).start()
        self.swap_copy(self.chip, 0).wait_recv()
        self.chipsum[self.chip] = self.source[self.me] + self.from_pair[self.chip]

    def finish(self, p):
        total = self.chipsum[self.chip, self.piece(p)]
        for j in range(1, self.m):
            self.chip_copy(self.chip, j, p, self.pair).wait_recv()
            total = total + self.from_chips[j, self.piece(p)]
        return total

    def drain(self):
        for k in range(self.m):
            self.swap_copy(k, k).wait_send()
        for p in range(self.pieces):
            for j in range(1, self.m):
                self.chip_copy(self.chip, j, p, self.pair).wait_send()


class Across:
    def __init__(self, groups, sems):
        self.groups, self.sems, self.grp = groups, sems, lax.axis_index("grp")

    def copy(self, src, dst, j, target):
        return pltpu.make_async_remote_copy(
            src_ref=src, dst_ref=dst, send_sem=self.sems.at[0, j], recv_sem=self.sems.at[1, j],
            device_id={"grp": target}, device_id_type=MESH)

    def others(self):
        return [(j, lax.rem(self.grp + j, self.groups)) for j in range(1, self.groups)]


def greet(n, groups):
    me, grp = lax.axis_index("dp"), lax.axis_index("grp")
    sem = pltpu.get_barrier_semaphore()
    for j in range(1, n):
        pl.semaphore_signal(sem, inc=1, device_id={"dp": lax.rem(me + j, n)}, device_id_type=MESH)
    for j in range(1, groups):
        pl.semaphore_signal(sem, inc=1, device_id={"grp": lax.rem(grp + j, groups)}, device_id_type=MESH)


def match(counts, me, wanted_mine, wanted_theirs):
    zero = jnp.zeros((1, 128), f32)
    mine, my_rank = zero, zero
    for d in range(len(counts)):
        hit = jnp.where(counts[d] == wanted_mine, 1.0, 0.0)
        my_rank = my_rank + jnp.where(d < me, hit, zero)
        mine = mine + jnp.where(d == me, hit, zero)
    rank, masks = zero, []
    for d in range(len(counts)):
        hit = jnp.where(counts[d] == wanted_theirs, 1.0, 0.0)
        masks.append(jnp.where(rank == my_rank, hit * mine, zero))
        rank = rank + hit
    return masks


def adam(weight, gradient, first, second, rate):
    first = 0.9 * first + (1.0 - 0.9) * gradient
    second = 0.999 * second + (1.0 - 0.999) * gradient * gradient
    first_hat = first / (1.0 - 0.9**5.0)
    second_hat = second / (1.0 - 0.999**5.0)
    return weight - rate * (first_hat / (jnp.sqrt(second_hat) + 1e-8) + 0.01 * weight), first, second


def side_rate(w):
    return jnp.where(lax.broadcasted_iota(jnp.int32, (58, w), 0) >= 31, 0.004, 0.05)


def flip(tile):
    eye = lax.broadcasted_iota(jnp.int32, (8, 128), 0) == lax.broadcasted_iota(jnp.int32, (8, 128), 1)
    return lax.dot_general(tile, eye.astype(f32), (((0,), (0,)), ((), ())), precision=HIGH, preferred_element_type=f32)[0:8]


def spread_field(ref, base, small, at, b):
    for c in range(3):
        for k in range(8):
            small[at, b, c : c + 1, k * 128 : (k + 1) * 128] = ref[base + c, k : k + 1, :]


def fold_field(value, ref, base):
    for c in range(3):
        for k in range(8):
            ref[base + c, k : k + 1, :] = value[c : c + 1, k * 128 : (k + 1) * 128]


def main_kernel(n, groups, names, *refs):
    r = types.SimpleNamespace(**dict(zip(names, refs)))
    w, fold, side_rows = scale_sizes(n)
    m = n // 2
    me, grp = lax.axis_index("dp"), lax.axis_index("grp")
    counts, terms, tiny = r.counts, r.terms, r.tiny
    greet(n, groups)
    get_side = Gather(n, r.sides, r.sides_sem)
    get_third = Gather(n, r.thirds, r.thirds_sem)
    get_mid = Gather(n, r.mids, r.mids_sem)
    share = Gather(n, r.results, r.results_sem)
    share_flow = Gather(n, r.flows, r.flows_sem)
    r.sides[me] = pack(jnp.concatenate([r.side_w[:, 0, :], jnp.zeros((6, w), f32)], 0), fold)
    for at, ref in enumerate((r.images, r.probes, r.cots)):
        r.thirds[me, 3 * at : 3 * at + 3] = ref[6:9]
    lane = lax.broadcasted_iota(jnp.int32, (8, 128), 1)
    sub = lax.broadcasted_iota(jnp.int32, (8, 128), 0)
    own_count = jnp.broadcast_to(counts[0, 0].astype(f32), (1, 128))
    r.thirds[me, 9] = jnp.where(lane == 0, counts[0, 0].astype(f32), terms[0, 2].astype(f32))
    r.mids[me] = r.mid_w[...]
    pl.semaphore_wait(pltpu.get_barrier_semaphore(), n + groups - 2)
    get_side.start()
    get_third.start()
    get_mid.start()
    small, side = r.small, r.side
    small[...] = jnp.zeros_like(small)
    for at, ref in ((SZ, r.images), (SP, r.probes), (SC, r.cots)):
        spread_field(ref, 0, small, at, 0)
    r.live[...] = jnp.where(terms[0, 0].astype(f32) > (sub % 4).astype(f32), 1.0, 0.0)
    bias_col = color_column([tiny[k, 0, 0] for k in range(3)])
    shift_col = color_column([tiny[k, 0, 1] for k in range(3)])
    scale_col = jnp.exp(color_column([tiny[k, 0, 2] for k in range(3)]))
    slope_raw = color_column([tiny[k, 0, 3] for k in range(3)])
    slope0 = 0.5 * softplus(slope_raw)

    def alive(b, step):
        return jnp.concatenate([r.live[b * 4 + step : b * 4 + step + 1, :]] * (PX // 128), 1)

    def prepare_image(b):
        masks = tap_masks()
        field = (small[SZ, b] + shift_col) * scale_col
        p = small[SP, b]
        small[SZ, b] = field
        x, t, e = pieces(field, slope0)
        d0 = 1.0 + t + x * e
        small[SD, b] = d0
        r.field[b] = expand(field + field * t, False, 1.0, masks)
        r.field[2 + b] = expand(d0 * p, False, 0.0, masks)
        r.field[4 + b] = expand(small[SC, b], True, 0.0, masks)
        r.field[6 + b] = expand(p, True, 0.0, masks)
        small[SV, b] = p
        small[SN, b] = -alive(b, 0) * p
        small[SS, b] = alive(b, 0) * p

    prepare_image(0)
    get_side.forward()
    get_side.finish()
    for i in range(fold):
        side[i * side_rows : (i + 1) * side_rows, :] = jnp.concatenate(
            [r.sides[d][:, i * w : (i + 1) * w] for d in range(n)], 1)
    lefts = r.lefts
    side1, side3 = prepare_side(side, lefts, [r.out_left[0, k] for k in range(3)], r.stage,
                                r.wa1, r.wp1, r.wa3, r.wp3, r.cols)
    wa1, wp1, wa3, wp3 = r.wa1, r.wp1, r.wa3, r.wp3
    mh, ml = r.mh, r.ml
    valid = lambda: lax.broadcasted_iota(jnp.int32, (8, PX), 0) < 3

    stages = []

    def stage(body):
        stages.append(body)
        pl.when(me + len(stages) > 0)(body)

    def doubled(index, k):
        block = r.field[index + k // PARTS, :, (k % PARTS) * TILE : (k % PARTS + 1) * TILE]
        return jnp.concatenate([block, block], 0)

    def column(which, rs):
        return jnp.concatenate([r.cols[which, rs]] * (TILE // 128), 1)

    one = (r.h1, r.g1, r.d1)
    two = (r.h2, r.g2, r.d2)

    def forward(kept, slope, bias, act, dact, k, h_all, dh_all):
        at = AT[k]
        hs, ys, ds = kept
        for rs in CHUNKS:
            h, dh = h_all[rs], dh_all[rs]
            if bias is not None:
                h = h + column(bias, rs)
            x = column(slope, rs) * h
            t = jnp.tanh(x)
            e = 1.0 - t * t
            d = 1.0 + t + x * e
            hs[rs, at] = h
            ds[rs, at] = d
            ys[rs, at] = e * (1.0 - x * t) * dh
            act[rs, at] = (h + h * t).astype(bf16)
            dact[rs, at] = (d * dh).astype(bf16)

    def backward(kept, slope, slope_to, bias_to, c_to, t_to, k, ca_all, ta_all):
        at = AT[k]
        hs, ys, ds = kept
        for rs in CHUNKS:
            h, d, c_a, t_a = hs[rs, at], ds[rs, at], ca_all[rs], ta_all[rs]
            sl = column(slope, rs)
            t = jnp.tanh(sl * h)
            he = h * (0.5 - 0.5 * (t * t))
            q = ys[rs, at] * t_a
            c_h = d * c_a + (sl + sl) * q
            grad = h * (c_a * he + q)
            gs, cs = grad[:, 0:128], c_h[:, 0:128]
            for j in range(1, TILE // 128):
                gs = gs + grad[:, j * 128 : (j + 1) * 128]
                if bias_to is not None:
                    cs = cs + c_h[:, j * 128 : (j + 1) * 128]
            r.sums[slope_to, rs] += gs
            if bias_to is not None:
                r.sums[bias_to, rs] += cs
            c_to[rs, at] = c_h.astype(bf16)
            t_to[rs, at] = (d * t_a).astype(bf16)

    def third_image():
        get_third.forward()
        get_third.finish()
        metas = [r.thirds[d, 9, 0:1, :] for d in range(n)]
        count_rows = [jnp.broadcast_to(meta[:, 0:1], (1, 128)) for meta in metas]
        masks = match(count_rows, me, 1.0, 3.0)
        helper, term = jnp.zeros((1, 128), f32), jnp.zeros((1, 128), f32) + terms[0, 1].astype(f32)
        for d in range(n):
            helper = helper + masks[d]
            term = jnp.where(masks[d] > 0.0, jnp.broadcast_to(metas[d][:, 1:2], (1, 128)), term)
        for at, ref in enumerate((r.images, r.probes, r.cots)):
            for c in range(3):
                picked = ref[3 + c]
                for d in range(n):
                    picked = jnp.where(masks[d] > 0.0, r.thirds[d, 3 * at + c], picked)
                r.picked[3 * at + c] = picked
        for at, place in ((0, SZ), (1, SP), (2, SC)):
            spread_field(r.picked, 3 * at, small, place, 1)
        r.live[...] = jnp.where(sub < 4, r.live[...], jnp.where(term > (sub % 4).astype(f32), 1.0, 0.0))

    def layer_one(b):
        @stage
        def _():
            pipeline([PARTS * b + k for k in range(PARTS)],
                     lambda k: (dot_tn(wa1[...], doubled(0, k)), dot_tn(wa1[...], doubled(2, k))),
                     functools.partial(forward, one, 0, None, r.a1, r.b1))
            for k in range(PARTS * b, PARTS * b + PARTS):
                r.ca[:, AT[k]] = dot_tn(wa3[...], doubled(4, k))
                r.c2[:, AT[k]] = dot_tn(wa3[...], doubled(6, k)).astype(bf16)

    layer_one(0)
    third_image()
    prepare_image(1)
    get_mid.forward()
    layer_one(1)
    get_mid.finish()
    q2, sigma2, right2 = prepare_mid(r.mids[...].reshape(C, C), lefts, mh, ml, r.left2)
    r.sums[...] = jnp.zeros_like(r.sums)

    @stage
    def layer_two():
        masks = tap_masks()

        def dots(k):
            a1 = r.a1[:, AT[k]]
            return dot_tn(mh[...], a1) + dot_tn(ml[...], a1), dot_tn(mh[...], r.b1[:, AT[k]])

        def after(k):
            to = slice((k % PARTS) * TILE, (k % PARTS + 1) * TILE)
            r.prod[0, :, to] = dot_nn(wp3[...], r.a2[:, AT[k]])
            r.prod[1, :, to] = dot_nn(wp3[...], r.b2[:, AT[k]])
            if k % PARTS == PARTS - 1:
                b = k // PARTS
                flow = small[SZ, b] + collapse(r.prod[0], False, masks) + bias_col
                fold_field(flow, r.firsts if b == 0 else r.flows.at[me], 0)
                small[ST, b] = jnp.where(valid(), collapse(r.prod[1], False, masks), 0.0)

        pipeline(range(2 * PARTS), dots, functools.partial(forward, two, 2, 1, r.a2, r.b2), after)

    share_flow.start()

    @stage
    def pulls():
        masks = tap_masks()
        v = [None, None]

        def first(b):
            if v[b] is None:
                r.c2[:, IM[b]] = (r.c2[:, IM[b]].astype(f32) * r.d2[:, IM[b]]).astype(bf16)
                return
            spread = expand(v[b], True, 0.0, masks)
            r.c2[:, IM[b]] = (dot_tn(wa3[...], jnp.concatenate([spread, spread], 0)) * r.d2[:, IM[b]]).astype(bf16)

        def second(b):
            r.t2[:, IM[b]] = (dot_nn(mh[...], r.c2[:, IM[b]]) * r.d1[:, IM[b]]).astype(bf16)

        def third(b, step):
            sign = (-1.0) ** step
            prod = dot_nn(wp1[...], r.t2[:, IM[b]])
            v[b] = jnp.where(valid(), small[SD, b] * collapse(prod, True, masks), 0.0)
            on = sign * alive(b, step)
            small[SN, b] = small[SN, b] - on * v[b]
            small[SS, b] = small[SS, b] + (on / (step + 1.0)) * v[b]

        first(0)
        second(0)
        first(1)
        third(0, 1)
        second(1)
        for step in (2, 3):
            first(0)
            third(1, step - 1)
            second(0)
            first(1)
            third(0, step)
            second(1)
        third(1, 3)

    share_flow.forward()

    @stage
    def back_two():
        masks = tap_masks()
        for b in range(2):
            r.field[6 + b] = expand(small[SN, b], True, 0.0, masks)
        pipeline(range(2 * PARTS), lambda k: (r.ca[:, AT[k]], dot_tn(wa3[...], doubled(6, k))),
                 functools.partial(backward, two, 2, 1, 0, r.c2, r.t2))

    raw = dot_nt(r.a1[...], r.c2[...]) + dot_nt(r.b1[...], r.t2[...])
    g3 = dot_nt(r.field[4], r.a2[:, 0:PX]) + dot_nt(r.field[6], r.b2[:, 0:PX])
    g3 = g3 + dot_nt(r.field[5], r.a2[:, PX:]) + dot_nt(r.field[7], r.b2[:, PX:])
    straight, across = correction(raw, r.mids[...].reshape(C, C), q2, sigma2)
    r.dmid[...] = (straight * raw + (across * right2) * r.left2[0:1, :]).reshape(n, w, C)
    sum_mid = Reduce(n, w // 16, r.dmid, r.mid_pair, r.mid_chip, r.mid_chips, r.mid_sem)
    sum_mid.start()
    ones = jnp.ones((8, 128), f32)
    row_of = lambda acc: lax.dot_general(
        ones, acc, (((1,), (1,)), ((), ())), precision=HIGH, preferred_element_type=f32)[0:1]
    dside = r.dside

    def put_taps(at, norm, grad, start):
        q, sigma, outer = norm
        row80 = lax.broadcasted_iota(jnp.int32, (80, C), 0)
        joined = jnp.where((row80 % 8 < 3) & (row80 < 72), grad + pltpu.roll(grad, 77, 0), 0.0)
        straight, across = correction(joined, r.stage[at], q, sigma)
        r.stage2[at] = straight * joined + across * outer
        for color in range(3):
            for tap in range(9):
                to = start + 9 * color + tap
                dside[to : to + 1, :] = r.stage2[at, 8 * tap + color : 8 * tap + color + 1, :]

    dside[29:30, :] = row_of(r.sums[0])
    dside[30:31, :] = row_of(r.sums[1]) * sigmoid(side[30:31, :])
    dside[58:64, :] = jnp.zeros((6, C), f32)
    put_taps(1, side3, g3, 31)
    sum_mid.forward()

    @stage
    def back_one():
        masks = tap_masks()

        def dots(k):
            c2 = r.c2[:, AT[k]]
            return dot_nn(mh[...], c2) + dot_nn(ml[...], c2), dot_nn(mh[...], r.t2[:, AT[k]])

        def after(k):
            to = slice((k % PARTS) * TILE, (k % PARTS + 1) * TILE)
            r.prod[0, :, to] = dot_nn(wp1[...], r.a2[:, AT[k]])
            r.prod[1, :, to] = dot_nn(wp1[...], r.b2[:, AT[k]])
            if k % PARTS == PARTS - 1:
                small[SA, k // PARTS] = collapse(r.prod[0], True, masks)
                small[SB, k // PARTS] = collapse(r.prod[1], True, masks)

        pipeline(range(2 * PARTS), dots, functools.partial(backward, one, 0, 2, None, r.a2, r.b2), after)

    g1 = dot_nt(r.field[0], r.a2[:, 0:PX]) + dot_nt(r.field[2], r.b2[:, 0:PX])
    g1 = g1 + dot_nt(r.field[1], r.a2[:, PX:]) + dot_nt(r.field[3], r.b2[:, PX:])
    dside[27:28, :] = g1[38:39]
    dside[28:29, :] = row_of(r.sums[2]) * sigmoid(side[28:29, :])
    put_taps(0, side1, g1, 0)
    for d in range(n):
        r.side_blocks[d] = pack(dside[:, d * w : (d + 1) * w], fold)
    sum_side = Reduce(n, 1, r.side_blocks, r.side_pair, r.side_chip, r.side_chips, r.side_sem)
    sum_side.start()
    total_scale = tiny[0, 0, 2] + tiny[1, 0, 2] + tiny[2, 0, 2]
    tile = jnp.where(lane == 5, counts[0, 0].astype(f32), 0.0)
    for b in range(2):
        field, p, cot = small[SZ, b], small[SP, b], small[SC, b]
        c_a, t_a = small[SA, b], small[SB, b]
        x, t, e = pieces(field, slope0)
        q = 2.0 * e * (1.0 - x * t) * p * t_a
        c_z = jnp.where(valid(), cot + (1.0 + t + x * e) * c_a + slope0 * q, 0.0)
        slope_grad = jnp.where(valid(), field * (c_a * field * e + q), 0.0)
        fold_field(c_z * scale_col, r.firsts if b == 0 else r.results.at[me], 3 if b == 0 else 0)
        sums = [
            jnp.sum(cot, axis=1, keepdims=True),
            jnp.sum(c_z, axis=1, keepdims=True) * scale_col,
            jnp.sum(c_z * field, axis=1, keepdims=True) - 1024.0,
            jnp.sum(slope_grad, axis=1, keepdims=True) * (0.5 * sigmoid(slope_raw)),
        ]
        for k in range(4):
            tile = tile + jnp.where((lane == k) & (sub < 3), sums[k], 0.0)
        log_part = (1024.0 * total_scale + jnp.sum(small[SS, b] * small[ST, b])) / 3072.0
        tile = tile + jnp.where((lane == 4) & (sub == b), log_part, 0.0)
    r.tiny_tiles[me] = tile
    spread = Spread(n, r.tiny_tiles, r.tiny_tiles_sem)
    sum_side.forward()
    spread.start()
    share.start()
    ring1 = Across(groups, r.ring1_sem)
    ring3, ring4 = Across(groups, r.ring3_sem), Across(groups, r.ring4_sem)
    cuts = w // 16

    def mid_copy(p, j, to):
        rows = pl.ds(16 * p, 16)
        return ring1.copy(r.mid_diff.at[grp, rows], r.mid_diff.at[grp, rows], p * groups + j, to)

    for p in range(cuts):
        rows = slice(16 * p, 16 * p + 16)
        mid_grad = sum_mid.finish(p) / (2.0 * n)
        r.mid_g[rows] = mid_grad
        r.mid_diff[grp, rows] = r.mid_o[rows] - adam(r.mid_w[rows], mid_grad, r.mid_f[rows], r.mid_s[rows], 0.01)[0]
        for j, to in ring1.others():
            mid_copy(p, j, to).start()
    side_grad = unpack(sum_side.finish(0), fold)[0:58] / (2.0 * n)
    r.side_g[...] = side_grad
    new = adam(r.side_w[:, 0, :], side_grad, r.side_f[:, 0, :], r.side_s[:, 0, :], side_rate(w))[0]
    r.side_diff[grp] = pack(jnp.concatenate([r.side_o[...] - new, jnp.zeros((6, w), f32)], 0), fold)
    for j, to in ring3.others():
        ring3.copy(r.side_diff.at[grp], r.side_diff.at[grp], j, to).start()
    spread.finish()
    tiny_sum = r.tiny_tiles[0]
    for d in range(1, n):
        tiny_sum = tiny_sum + r.tiny_tiles[d]
    r.out_small[0] = tiny_sum
    r.tiles[...] = jnp.zeros_like(r.tiles)
    for c in range(3):
        for k, ref in enumerate((r.tiny_w, r.tiny_f, r.tiny_s)):
            r.tiles[k, c : c + 1, 0:4] = ref[c, 0:1, :]
    r.tiles[3, 0:4, 0:3] = r.tiny_o[...]
    new = adam(r.tiles[0], tiny_sum / (2.0 * n), r.tiles[1], r.tiles[2], 0.05)[0]
    r.tiny_diff[grp] = r.tiles[3] - flip(jnp.where(lane < 4, new, 0.0))
    for j, to in ring4.others():
        ring4.copy(r.tiny_diff.at[grp], r.tiny_diff.at[grp], j, to).start()
    share.forward()
    tiles = [r.tiny_tiles[d] for d in range(n)]
    masks = match([jnp.broadcast_to(t[0:1, 5:6], (1, 128)) for t in tiles], me, 3.0, 1.0)
    log_third = jnp.zeros((1, 128), f32)
    for d in range(n):
        log_third = jnp.where(masks[d] > 0.0, jnp.broadcast_to(tiles[d][1:2, 4:5], (1, 128)), log_third)
    share_flow.finish()
    share.finish()
    for out, ref, base in ((r.out_flow, r.flows, 0), (r.out_back, r.results, 3)):
        for c in range(3):
            picked = jnp.zeros((8, 128), f32)
            for d in range(n):
                picked = jnp.where(masks[d] > 0.0, ref[d, c], picked)
            out[c] = r.firsts[base + c]
            out[3 + c] = jnp.where(own_count > 1.5, ref[me, c], 0.0)
            out[6 + c] = picked
    logs = [jnp.broadcast_to(tile[b : b + 1, 4:5], (1, 128)) for b in range(2)]
    logs[1] = jnp.where(own_count > 1.5, logs[1], 0.0)
    row_lane = lax.broadcasted_iota(jnp.int32, (1, 128), 1)
    r.out_small[1] = jnp.broadcast_to(
        jnp.where(row_lane == 0, logs[0], jnp.where(row_lane == 1, logs[1], log_third)), (8, 128))
    for j, to in ring3.others():
        ring3.copy(r.side_diff.at[grp], r.side_diff.at[grp], j, to).wait_recv()
    total = r.side_diff[0]
    for k in range(1, groups):
        total = total + r.side_diff[k]
    r.side_t[...] = unpack(total, fold)[0:58]
    for j, to in ring4.others():
        ring4.copy(r.tiny_diff.at[grp], r.tiny_diff.at[grp], j, to).wait_recv()
    total = r.tiny_diff[0]
    for k in range(1, groups):
        total = total + r.tiny_diff[k]
    r.out_small[2] = total
    for p in range(cuts):
        rows = slice(16 * p, 16 * p + 16)
        for j, to in ring1.others():
            mid_copy(p, j, to).wait_recv()
        total = r.mid_diff[0, rows]
        for k in range(1, groups):
            total = total + r.mid_diff[k, rows]
        r.mid_t[rows] = total
    sum_mid.drain()
    sum_side.drain()
    for p in range(cuts):
        for j, to in ring1.others():
            mid_copy(p, j, to).wait_send()
    for j, to in ring3.others():
        ring3.copy(r.side_diff.at[grp], r.side_diff.at[grp], j, to).wait_send()
    for j, to in ring4.others():
        ring4.copy(r.tiny_diff.at[grp], r.tiny_diff.at[grp], j, to).wait_send()


def last_kernel(n, groups, names, *refs):
    r = types.SimpleNamespace(**dict(zip(names, refs)))
    w = C // n
    lane = lax.broadcasted_iota(jnp.int32, (8, 128), 1)
    r.flow_o[...] = r.flow[...]
    r.back_o[...] = r.back[...]
    r.log_det[...] = r.small[1, 0:1, 0:3]
    tiny_sum = r.small[0]
    r.log_mean[...] = (tiny_sum[0:1, 4:5] + tiny_sum[1:2, 4:5]) / (2.0 * n)
    new, first, second = adam(r.mid_w[...], r.mid_g[...], r.mid_f[...], r.mid_s[...], 0.01)
    r.mid_f_new[...], r.mid_s_new[...], r.mid_new[...] = first, second, new
    new, first, second = adam(r.side_w[:, 0, :], r.side_g[...], r.side_f[:, 0, :], r.side_s[:, 0, :], side_rate(w))
    r.side_f_new[:, 0, :], r.side_s_new[:, 0, :], r.side_new[:, 0, :] = first, second, new
    r.tiles[...] = jnp.zeros_like(r.tiles)
    for c in range(3):
        for k, ref in enumerate((r.tiny_w, r.tiny_f, r.tiny_s)):
            r.tiles[k, c : c + 1, 0:4] = ref[c, 0:1, :]
    new, first, second = adam(r.tiles[0], tiny_sum / (2.0 * n), r.tiles[1], r.tiles[2], 0.05)
    for c in range(3):
        r.tiny_f_new[c, 0:1, :] = first[c : c + 1, 0:4]
        r.tiny_new[c, 0:1, :] = new[c : c + 1, 0:4]
    turned = flip(jnp.where(lane < 4, second, 0.0))
    for k in range(3):
        r.tiny_s_new[k, 0:1, :] = turned[k : k + 1, 0:3]
    r.slope_s_new[...] = turned[3:4, 0:3]

    def outer(diff, old, momentum, delta_out, momentum_out, out):
        delta = diff / groups
        mom = 0.9 * momentum[...] + delta
        delta_out[...], momentum_out[...] = delta, mom
        out[...] = old[...] - 0.7 * (delta + 0.9 * mom)

    outer(r.mid_t[...], r.mid_o, r.mid_m, r.mid_d, r.mid_m_new, r.mid_o_new)
    outer(r.side_t[...], r.side_o, r.side_m, r.side_d, r.side_m_new, r.side_o_new)
    outer(r.small[2, 0:4, 0:3], r.tiny_o, r.tiny_m, r.tiny_d, r.tiny_m_new, r.tiny_o_new)


def on_device(images, probes, out_cotangent, counts, terms, power_left, power_out, mid_weight, mid_first, mid_second,
              side_weight, side_first, side_second, tiny_weight, tiny_first, tiny_second,
              mid_outer, mid_momentum, side_outer, side_momentum, tiny_outer, tiny_momentum):
    n, groups = lax.axis_size("dp"), lax.axis_size("grp")
    w, fold, side_rows = scale_sizes(n)
    m = n // 2
    vm = pl.BlockSpec(memory_space=pltpu.VMEM)
    sm = pl.BlockSpec(memory_space=pltpu.SMEM)
    sd = lambda *shape: jax.ShapeDtypeStruct(shape, f32)
    dma = lambda *shape: pltpu.SemaphoreType.DMA(shape)
    vmem = lambda *shape: pltpu.VMEM(shape, f32)
    big = lambda dtype: pltpu.VMEM((C, 2 * PX), dtype)
    half = lambda *shape: pltpu.VMEM(shape, bf16)
    image = lambda x: x[0].reshape(9, 8, 128)
    turn = lambda x: jnp.swapaxes(x, -1, -2)
    row = lambda x: x[0][:, None, :]
    color = lambda x: jnp.transpose(x, (2, 0, 1))
    state = dict(
        mid_w=turn(mid_weight[0]), mid_f=turn(mid_first[0]), mid_s=turn(mid_second[0]), mid_o=turn(mid_outer),
        side_w=row(side_weight), side_f=row(side_first), side_s=row(side_second), side_o=side_outer,
        tiny_w=color(tiny_weight), tiny_f=color(tiny_first), tiny_s=color(tiny_second), tiny_o=tiny_outer,
    )
    vmem_in = dict(images=image(images), probes=image(probes), cots=image(out_cotangent), lefts=power_left[0], **state)
    smem_in = dict(counts=counts, terms=terms, out_left=power_out, tiny=color(tiny_weight))
    outs = dict(out_flow=sd(9, 8, 128), out_back=sd(9, 8, 128), out_small=sd(3, 8, 128), mid_g=sd(w, C), mid_t=sd(w, C),
                side_g=sd(58, w), side_t=sd(58, w))
    scratch = dict(
        stage=vmem(2, 80, C), stage2=vmem(2, 80, C), wa1=half(160, C), wp1=half(80, C), wa3=half(160, C), wp3=half(80, C),
        cols=vmem(3, C, 128), small=vmem(10, 2, 8, PX), sums=vmem(3, C, 128), field=half(8, 80, PX), prod=vmem(2, 80, PX),
        mh=half(C, C), ml=half(C, C), left2=vmem(8, C), live=vmem(8, 128), side=vmem(64, C),
        h1=big(f32), g1=big(f32), h2=big(f32), g2=big(f32),
        d1=big(f32), a1=big(bf16), b1=big(bf16), d2=big(f32), a2=big(bf16), b2=big(bf16), c2=big(bf16), t2=big(bf16),
        ca=big(f32), sides=vmem(n, side_rows, 128), thirds=vmem(n, 10, 8, 128), mids=vmem(n, w, C), results=vmem(n, 3, 8, 128), tiny_tiles=vmem(n, 8, 128), tiny_tiles_sem=dma(2, n), flows=vmem(n, 3, 8, 128), flows_sem=dma(2, n),
        picked=vmem(9, 8, 128), firsts=vmem(6, 8, 128), dmid=vmem(n, w, C), dside=vmem(64, C),
        side_blocks=vmem(n, side_rows, 128),
        mid_pair=vmem(m, w, C), mid_chip=vmem(m, w, C), mid_chips=vmem(m, w, C),
        side_pair=vmem(m, side_rows, 128), side_chip=vmem(m, side_rows, 128), side_chips=vmem(m, side_rows, 128),
        mid_diff=vmem(groups, w, C),
        side_diff=vmem(groups, side_rows, 128), tiny_diff=vmem(groups, 8, 128), tiles=vmem(4, 8, 128),
        sides_sem=dma(2, n), thirds_sem=dma(2, n), mids_sem=dma(2, n), results_sem=dma(2, n),
        mid_sem=dma(2, m * (1 + w // 16)), side_sem=dma(2, n),
        ring1_sem=dma(2, groups * (w // 16)), ring3_sem=dma(2, groups), ring4_sem=dma(2, groups),
    )
    ins = {**vmem_in, **smem_in}
    made = pl.pallas_call(
        functools.partial(main_kernel, n, groups, list(ins) + list(outs) + list(scratch)),
        in_specs=[vm] * len(vmem_in) + [sm] * len(smem_in),
        out_specs=[vm] * len(outs),
        out_shape=list(outs.values()),
        scratch_shapes=list(scratch.values()),
        compiler_params=pltpu.CompilerParams(vmem_limit_bytes=60 << 20, collective_id=0, has_side_effects=True),
    )(*ins.values())
    flow, back, small, mid_g, mid_t, side_g, side_t = made
    ins = dict(flow=flow, back=back, small=small, mid_g=mid_g, mid_t=mid_t, side_g=side_g, side_t=side_t, **state)
    ins.update(mid_m=turn(mid_momentum), side_m=side_momentum, tiny_m=tiny_momentum)
    scratch = dict(tiles=vmem(3, 8, 128))
    outs = dict(
        flow_o=sd(9, 8, 128), back_o=sd(9, 8, 128), log_det=sd(1, 3), log_mean=sd(1, 1),
        mid_f_new=sd(w, C), mid_s_new=sd(w, C), mid_new=sd(w, C),
        side_f_new=sd(58, 1, w), side_s_new=sd(58, 1, w), side_new=sd(58, 1, w),
        tiny_f_new=sd(3, 1, 4), tiny_s_new=sd(3, 1, 3), slope_s_new=sd(1, 3), tiny_new=sd(3, 1, 4),
        mid_d=sd(w, C), mid_m_new=sd(w, C), mid_o_new=sd(w, C),
        side_d=sd(58, w), side_m_new=sd(58, w), side_o_new=sd(58, w),
        tiny_d=sd(4, 3), tiny_m_new=sd(4, 3), tiny_o_new=sd(4, 3),
    )
    made = pl.pallas_call(
        functools.partial(last_kernel, n, groups, list(ins) + list(outs) + list(scratch)),
        in_specs=[vm] * len(ins),
        out_specs=[vm] * len(outs),
        out_shape=list(outs.values()),
        scratch_shapes=list(scratch.values()),
        compiler_params=pltpu.CompilerParams(vmem_limit_bytes=60 << 20),
    )(*ins.values())
    o = types.SimpleNamespace(**dict(zip(outs, made)))
    whole = lambda x: x.reshape(1, 3, 3, PX)
    back_turn = lambda x: turn(x)[None]
    return (
        whole(o.flow_o), whole(o.back_o), o.log_det, o.log_mean.reshape(1),
        back_turn(o.mid_f_new), back_turn(o.mid_s_new), back_turn(o.mid_new),
        o.side_f_new[:, 0][None], o.side_s_new[:, 0][None], o.side_new[:, 0][None],
        jnp.transpose(o.tiny_f_new, (1, 2, 0)), jnp.transpose(o.tiny_s_new, (1, 0, 2)), o.slope_s_new, jnp.transpose(o.tiny_new, (1, 2, 0)),
        turn(o.mid_d), turn(o.mid_m_new), turn(o.mid_o_new),
        o.side_d, o.side_m_new, o.side_o_new, o.tiny_d, o.tiny_m_new, o.tiny_o_new,
    )


def solution(mesh):
    split = P("grp", None, "dp")
    group = P("grp", None, None)
    image = P("grp", "dp", None, None)
    return jax.shard_map(
        on_device,
        mesh=mesh,
        in_specs=(image, image, image, P("grp", "dp"), P("grp", "dp"), group, P("grp", None),
                  split, split, split, split, split, split, group, group, group,
                  P(None, "dp"), P(None, "dp"), P(None, "dp"), P(None, "dp"), P(), P()),
        out_specs=(image, image, P("grp", "dp"), P("grp"), split, split, split, split, split, split,
                   group, group, P("grp", None), group) + (P(None, "dp"),) * 6 + (P(), P(), P()),
        check_vma=False,
    )
```
